256 devices in a mesh: tm: 32 (over y_lo, z, core), rows: 8 (over y_hi, x).
Axes of the slice: x: 4, y: 4 (y_hi: 2, y_lo: 2; y = y_hi * 2 + y_lo), z: 8, core: 2. Of those that a mesh axis runs over, the one named last changes fastest.
Arguments:
- video: bfloat16 [64, 16, 96, 256], P('tm', 'rows'), may hold values from -6 to 6
- kernel_a: bfloat16 [6912, 256], replicated, may hold values from -0.078125 to 0.078125
- project: bfloat16 [256, 128], replicated, may hold values from -0.375 to 0.375
- kernel_b: bfloat16 [3456, 128], replicated, may hold values from -0.109375 to 0.109375
- cotangent: bfloat16 [64, 16, 96, 128], P('tm', 'rows'), may hold values from -6 to 6
Outputs:
- output: float32 [64, 16, 96, 128], P('tm', 'rows')
- grad_video: float32 [64, 16, 96, 256], P('tm', 'rows')
- grad_kernel_a: float32 [6912, 256], P('tm', 'rows')
- grad_kernel_b: float32 [3456, 128], P('tm', 'rows')
- grad_project: float32 [256, 128], P('tm', 'rows')
The draws below stay inside these ranges and needn't reach their ends.
All inputs are finite; a program needn't handle non-finite values.
Results may differ from the reference program's by a relative error of at most 0.0041.
Values may be sent and summed in bfloat16 or wider, within the bound.
A program may use at most 128 MiB of HBM per device.

```python
import jax
import jax.numpy as jnp
from jax import lax

CA = 256
CB = 128
WIDTH = 96
NF = 64
NR = 16


def levels(key, shape, pieces, low, high):
    factor_of, own = 1.0, jax.random.fold_in(key, 6)
    for dim, parts in pieces:
        steps = jnp.exp(jax.random.uniform(jax.random.fold_in(own, dim), (parts,), jnp.float32, low / len(pieces), high / len(pieces)))
        factor_of = factor_of * jnp.repeat(steps, shape[dim] // parts).reshape([-1 if axis == dim else 1 for axis in range(len(shape))])
    return factor_of


def centred(key, shape, scale, reach, pieces=(), held_as=jnp.bfloat16):
    array = scale * jax.random.normal(key, shape, jnp.float32)
    if pieces:
        array = array * levels(key, shape, pieces, -0.22, 0.18)
    return jnp.clip(array, -reach, reach).astype(held_as)


def setup_inputs(seed: int = 0) -> dict:
    seeds = jax.random.split(jax.random.key(seed), 6)
    return {
        "video": centred(seeds[0], (NF, NR, WIDTH, CA), 1.0, 6.0, ((0, 32), (1, 8))),
        "kernel_a": centred(seeds[1], (27 * CA, CA), (27 * CA) ** -0.5, 0.078125),
        "project": centred(seeds[2], (CA, CB), CA ** -0.5, 0.375),
        "kernel_b": centred(seeds[3], (27 * CB, CB), (27 * CB) ** -0.5, 0.109375),
        "cotangent": centred(seeds[4], (NF, NR, WIDTH, CB), 1.0, 6.0, ((0, 32), (1, 8))),
    }


def conv_taps(padded, weight, frames, rows, width, flip):
    cin = padded.shape[3]
    cout = weight.shape[1]
    total = jnp.zeros((frames * rows * width, weight.shape[0] // 27 if flip else cout), jnp.float32)
    for kt in range(3):
        for kr in range(3):
            for kc in range(3):
                tap = 9 * kt + 3 * kr + kc
                if flip:
                    piece = padded[2 - kt:2 - kt + frames, 2 - kr:2 - kr + rows, 2 - kc:2 - kc + width].reshape(-1, cin)
                    block = weight[tap * (weight.shape[0] // 27):(tap + 1) * (weight.shape[0] // 27)]
                    total = total + lax.dot_general(piece, block, (((1,), (1,)), ((), ())), preferred_element_type=jnp.float32)
                else:
                    piece = padded[kt:kt + frames, kr:kr + rows, kc:kc + width].reshape(-1, cin)
                    block = weight[tap * cin:(tap + 1) * cin]
                    total = total + jnp.dot(piece, block, preferred_element_type=jnp.float32)
    return total

def weight_grad(padded, grad, frames, rows, width):
    cin = padded.shape[3]
    flat = grad.reshape(-1, grad.shape[-1])
    blocks = []
    for kt in range(3):
        for kr in range(3):
            for kc in range(3):
                piece = padded[kt:kt + frames, kr:kr + rows, kc:kc + width].reshape(-1, cin)
                blocks.append(lax.dot_general(piece, flat, (((0,), (0,)), ((), ())), preferred_element_type=jnp.float32))
    return jnp.concatenate(blocks, 0)

def reference(video, kernel_a, project, kernel_b, cotangent):
    past = ((2, 0), (1, 1), (1, 1), (0, 0))
    future = ((0, 2), (1, 1), (1, 1), (0, 0))
    video_p = jnp.pad(video, past)
    pre = conv_taps(video_p, kernel_a, NF, NR, WIDTH, False)
    hidden = jax.nn.silu(pre).astype(jnp.bfloat16)
    mid = jnp.dot(hidden, project, preferred_element_type=jnp.float32)
    mid_b = mid.astype(jnp.bfloat16)
    mid_p = jnp.pad(mid_b.reshape(NF, NR, WIDTH, CB), past)
    out = conv_taps(mid_p, kernel_b, NF, NR, WIDTH, False) + mid
    cot_p = jnp.pad(cotangent, future)
    grad_mid = (cotangent.reshape(-1, CB).astype(jnp.float32) + conv_taps(cot_p, kernel_b, NF, NR, WIDTH, True)).astype(jnp.bfloat16)
    grad_h = lax.dot_general(grad_mid, project, (((1,), (1,)), ((), ())), preferred_element_type=jnp.float32)
    sig = jax.nn.sigmoid(pre)
    grad_pre = (grad_h * sig * (1.0 + pre * (1.0 - sig))).astype(jnp.bfloat16)
    grad_pre_p = jnp.pad(grad_pre.reshape(NF, NR, WIDTH, CA), future)
    grad_video = conv_taps(grad_pre_p, kernel_a, NF, NR, WIDTH, True)
    scale = 1.0 / jnp.sqrt(jnp.float32(NF * NR * WIDTH))
    grad_b = weight_grad(mid_p, cotangent, NF, NR, WIDTH) * scale
    grad_proj = lax.dot_general(hidden, grad_mid, (((0,), (0,)), ((), ())), preferred_element_type=jnp.float32) * scale
    grad_a = weight_grad(video_p, grad_pre, NF, NR, WIDTH) * scale
    return (out.reshape(NF, NR, WIDTH, CB), grad_video.reshape(NF, NR, WIDTH, CA), grad_a, grad_b, grad_proj)
```

```python
import jax
import jax.numpy as jnp
from jax import lax
from jax.experimental import pallas as pl
from jax.experimental.pallas import tpu as pltpu
from jax.sharding import PartitionSpec as P


def with_halo(x, sides, width):
    for axis, dim in sides:
        peers, length = (lax.axis_size(axis), x.shape[dim])
        up = [(i, (i + 1) % peers) for i in range(peers - 1)]
        down = [(j, i) for i, j in up]
        last = lax.slice_in_dim(x, length - width, length, axis=dim)
        leading = lax.slice_in_dim(x, 0, width, axis=dim)
        before = lax.ppermute(last, axis, up)
        after = lax.ppermute(leading, axis, down)
        x = jnp.concatenate([before, x, after], axis=dim)
    return x


def passed_along(block, axis, distance):
    devices = range(lax.axis_size(axis))
    route = [(i - distance, i) for i in devices if i - distance in devices]
    return lax.ppermute(block, axis, route)


def conv_taps(padded, weight, frames, rows, width, flip):
    cin = padded.shape[3]
    cout = weight.shape[1]
    total = jnp.zeros((frames * rows * width, weight.shape[0] // 27 if flip else cout), jnp.float32)
    for kt in range(3):
        for kr in range(3):
            for kc in range(3):
                tap = 9 * kt + 3 * kr + kc
                if flip:
                    piece = padded[
                        2 - kt : 2 - kt + frames, 2 - kr : 2 - kr + rows, 2 - kc : 2 - kc + width
                    ].reshape(-1, cin)
                    block = weight[
                        tap * (weight.shape[0] // 27) : (tap + 1) * (weight.shape[0] // 27)
                    ]
                    total = total + lax.dot_general(
                        piece, block, (((1,), (1,)), ((), ())), preferred_element_type=jnp.float32
                    )
                else:
                    piece = padded[kt : kt + frames, kr : kr + rows, kc : kc + width].reshape(
                        -1, cin
                    )
                    block = weight[tap * cin : (tap + 1) * cin]
                    total = total + jnp.dot(piece, block, preferred_element_type=jnp.float32)
    return total


def weight_grad(padded, grad, frames, rows, width):
    cin = padded.shape[3]
    flat = grad.reshape(-1, grad.shape[-1])
    blocks = []
    for kt in range(3):
        for kr in range(3):
            for kc in range(3):
                piece = padded[kt : kt + frames, kr : kr + rows, kc : kc + width].reshape(-1, cin)
                blocks.append(
                    lax.dot_general(
                        flat, piece, (((0,), (0,)), ((), ())), preferred_element_type=jnp.float32
                    )
                )
    return jnp.concatenate(blocks, 1)


LANES = 4480
LX = 2304
LY = LANES - LX


def arranged(grad_a, grad_b, grad_proj):
    part_a = grad_a.reshape(8, 2, 16, 2, 3456)
    halves = jnp.stack([grad_b[:, : 14 * 128], grad_b[:, 13 * 128 :]], 1)
    part_b = halves.reshape(8, 2, 8, 2, 2, 896).transpose(0, 1, 4, 2, 3, 5)
    part_b = part_b.reshape(8, 2, 16, 2, 896)
    part_p = grad_proj.reshape(8, 2, 8, 2, 128)
    part_p = jnp.pad(part_p, ((0, 0), (0, 0), (0, 8), (0, 0), (0, 0)))
    whole = jnp.concatenate([part_a, part_b, part_p], 4).astype(jnp.bfloat16)
    return whole.reshape(8, 2, 16, 2 * LANES)


def rs_kernel(
    p_ref, o_ref, recv0, s0x, s0y, r1x, r1y, s1x, s1y, r2y, r2x, t_ref, msg, r3,
    sem0, sem1x, sem1y, sem2y, sem2x, sem3,
):
    f32, bf16 = jnp.float32, jnp.bfloat16
    tm = lax.axis_index("tm")
    rows = lax.axis_index("rows")
    core = lax.rem(tm, 2)
    b = lax.rem(tm, 16)
    y_lo = tm // 16
    y_hi = rows // 4
    x = lax.rem(rows, 4)
    y = y_hi * 2 + y_lo

    def x_peer(d):
        return (tm, y_hi * 4 + lax.rem(x + d, 4))

    def y_peer(d):
        to = lax.rem(y + d, 4)
        return (lax.rem(to, 2) * 16 + b, (to // 2) * 4 + x)

    def z_peer(d):
        return (y_lo * 16 + lax.rem(b + d, 16), rows)

    partner = (tm + 1 - 2 * core, rows)

    def remote(src, dst, sem, slot, to):
        return pltpu.make_async_remote_copy(
            src_ref=src, dst_ref=dst, send_sem=sem.at[0, slot], recv_sem=sem.at[1, slot],
            device_id=to, device_id_type=pl.DeviceIdType.MESH,
        )

    barrier = pltpu.get_barrier_semaphore()
    for d in range(1, 4):
        pl.semaphore_signal(barrier, inc=1, device_id=x_peer(d), device_id_type=pl.DeviceIdType.MESH)
        pl.semaphore_signal(barrier, inc=1, device_id=y_peer(d), device_id_type=pl.DeviceIdType.MESH)
    for d in range(1, 16):
        pl.semaphore_signal(barrier, inc=1, device_id=z_peer(d), device_id_type=pl.DeviceIdType.MESH)
    pl.semaphore_wait(barrier, 21)

    order = [1, 2, 3, 0]
    core_copies = []
    for k, d in enumerate(order):
        for yh in range(2):
            j = yh * 4 + lax.rem(x + d, 4)
            cp = remote(p_ref.at[j, 1 - core], recv0.at[j], sem0, 2 * k + yh, partner)
            cp.start()
            core_copies.append(cp)

    x_copies, y_copies = [], []
    for k, d in enumerate(order):
        to = lax.rem(x + d, 4)
        for yh in range(2):
            j = yh * 4 + to
            core_copies[2 * k + yh].wait()
            for yl in range(2):
                at = yl * LANES
                s0x[to, yh * 2 + yl] = (
                    p_ref[j, core, :, at : at + LX].astype(f32)
                    + recv0[j, :, at : at + LX].astype(f32)
                ).astype(bf16)
                s0y[yh * 2 + yl, to] = (
                    p_ref[j, core, :, at + LX : at + LANES].astype(f32)
                    + recv0[j, :, at + LX : at + LANES].astype(f32)
                ).astype(bf16)
        if d:
            cp = remote(s0x.at[to], r1x.at[d - 1], sem1x, d - 1, x_peer(d))
            cp.start()
            x_copies.append(cp)
    for d in range(1, 4):
        cp = remote(s0y.at[lax.rem(y + d, 4)], r1y.at[d - 1], sem1y, d - 1, y_peer(d))
        cp.start()
        y_copies.append(cp)

    for cp in x_copies:
        cp.wait()
    second = []
    for d in order:
        to = lax.rem(y + d, 4)
        acc = s0x[x, to].astype(f32)
        for s in range(3):
            acc = acc + r1x[s, to].astype(f32)
        s1x[to] = acc.astype(bf16)
        if d:
            cp = remote(s1x.at[to], r2y.at[d - 1], sem2y, d - 1, y_peer(d))
            cp.start()
            second.append(cp)
    for cp in y_copies:
        cp.wait()
    for d in order:
        to = lax.rem(x + d, 4)
        acc = s0y[y, to].astype(f32)
        for s in range(3):
            acc = acc + r1y[s, to].astype(f32)
        s1y[to] = acc.astype(bf16)
        if d:
            cp = remote(s1y.at[to], r2x.at[d - 1], sem2x, d - 1, x_peer(d))
            cp.start()
            second.append(cp)
    for cp in second:
        cp.wait()
    acc = s1x[y].astype(f32)
    for s in range(3):
        acc = acc + r2y[s].astype(f32)
    t_ref[:, :LX] = acc
    acc = s1y[x].astype(f32)
    for s in range(3):
        acc = acc + r2x[s].astype(f32)
    t_ref[:, LX:] = acc

    part_b = jnp.concatenate([t_ref[0:8, 3456:4352], t_ref[8:16, 3456:4352]], 1)
    part_b = jnp.where(y_lo == 0, part_b[:, 0:1728], part_b[:, 64:1792])
    part_p = t_ref[0:8, 4352:4480]
    for k in range(16):
        msg[k] = jnp.zeros((16, 384), bf16)
        msg[k, :, 0:216] = t_ref[:, 216 * k : 216 * k + 216].astype(bf16)
        low = jnp.concatenate(
            [
                part_b[:, 108 * k : 108 * k + 108], jnp.zeros((8, 4), f32),
                part_p[:, 8 * k : 8 * k + 8], jnp.zeros((8, 8), f32),
            ], 1,
        )
        msg[k, :, 256:384] = jnp.concatenate([low, jnp.zeros((8, 128), f32)], 0).astype(bf16)
    last = []
    for d in range(1, 16):
        cp = remote(msg.at[lax.rem(b + d, 16)], r3.at[d - 1], sem3, d - 1, z_peer(d))
        cp.start()
        last.append(cp)
    for cp in last:
        cp.wait()
    same = msg[b].astype(f32)
    for d in range(2, 16, 2):
        same = same + r3[d - 1].astype(f32)
    other = r3[0].astype(f32)
    for d in range(3, 16, 2):
        other = other + r3[d - 1].astype(f32)
    o_ref[core] = same
    o_ref[1 - core] = other


def reduce_scattered(partial):
    bf16 = jnp.bfloat16
    dma = pltpu.SemaphoreType.DMA
    return pl.pallas_call(
        rs_kernel,
        out_shape=jax.ShapeDtypeStruct((2, 16, 384), jnp.float32),
        in_specs=[pl.BlockSpec(memory_space=pltpu.VMEM)],
        out_specs=pl.BlockSpec(memory_space=pltpu.VMEM),
        scratch_shapes=[
            pltpu.VMEM((8, 16, 2 * LANES), bf16),
            pltpu.VMEM((4, 4, 16, LX), bf16),
            pltpu.VMEM((4, 4, 16, LY), bf16),
            pltpu.VMEM((3, 4, 16, LX), bf16),
            pltpu.VMEM((3, 4, 16, LY), bf16),
            pltpu.VMEM((4, 16, LX), bf16),
            pltpu.VMEM((4, 16, LY), bf16),
            pltpu.VMEM((3, 16, LX), bf16),
            pltpu.VMEM((3, 16, LY), bf16),
            pltpu.VMEM((16, LANES), jnp.float32),
            pltpu.VMEM((16, 16, 384), bf16),
            pltpu.VMEM((15, 16, 384), bf16),
            dma((2, 8)), dma((2, 3)), dma((2, 3)), dma((2, 3)), dma((2, 3)), dma((2, 15)),
        ],
        compiler_params=pltpu.CompilerParams(
            collective_id=0, has_side_effects=True, vmem_limit_bytes=40 * 1024 * 1024
        ),
    )(partial)


def with_rims(block):
    return with_halo(block, (("rows", 1),), 1)


def pad_width(block):
    return jnp.pad(block, ((0, 0), (0, 0), (1, 1), (0, 0)))


def past_padded(block):
    banded = with_rims(block)
    earlier = passed_along(banded, "tm", 1)
    return pad_width(jnp.concatenate([earlier, banded], 0))


def future_padded(block):
    banded = with_rims(block)
    later = passed_along(banded, "tm", -1)
    return pad_width(jnp.concatenate([banded, later], 0))


def shards(video, kernel_a, project, kernel_b, cotangent):
    frames, rows, width, chan_a = video.shape
    chan_b = cotangent.shape[3]
    video_p = past_padded(video)
    pre = conv_taps(video_p, kernel_a, frames, rows, width, False)
    hidden = jax.nn.silu(pre).astype(jnp.bfloat16)
    mid = jnp.dot(hidden, project, preferred_element_type=jnp.float32)
    mid_b = mid.astype(jnp.bfloat16)
    mid_p = past_padded(mid_b.reshape(frames, rows, width, chan_b))
    result = conv_taps(mid_p, kernel_b, frames, rows, width, False) + mid
    cot_p = future_padded(cotangent)
    grad_mid = (
        cotangent.reshape(-1, chan_b).astype(jnp.float32)
        + conv_taps(cot_p, kernel_b, frames, rows, width, True)
    ).astype(jnp.bfloat16)
    total_cells = frames * lax.axis_size("tm") * rows * lax.axis_size("rows") * width
    scale = 1.0 / jnp.sqrt(jnp.float32(total_cells))
    grad_b = weight_grad(mid_p, cotangent, frames, rows, width)
    grad_proj = lax.dot_general(
        grad_mid, hidden, (((0,), (0,)), ((), ())), preferred_element_type=jnp.float32
    )
    grad_h = lax.dot_general(
        grad_mid, project, (((1,), (1,)), ((), ())), preferred_element_type=jnp.float32
    )
    sig = jax.nn.sigmoid(pre)
    grad_pre = (grad_h * sig * (1.0 + pre * (1.0 - sig))).astype(jnp.bfloat16)
    grad_pre_4 = grad_pre.reshape(frames, rows, width, chan_a)
    grad_pre_p = future_padded(grad_pre_4)
    grad_video = conv_taps(grad_pre_p, kernel_a, frames, rows, width, True)
    grad_a = weight_grad(video_p, grad_pre_4, frames, rows, width)
    partial = arranged(grad_a, grad_b, grad_proj)
    summed = reduce_scattered(partial) * scale
    return (
        result.reshape(frames, rows, width, chan_b),
        grad_video.reshape(frames, rows, width, chan_a),
        summed[:, :, 0:216].reshape(32, 216).T,
        summed[:, 0:8, 256:364].reshape(16, 108).T,
        summed[:, 0:8, 368:376].reshape(16, 8).T,
    )


def solution(mesh):
    in_specs = (P("tm", "rows", None, None), P(), P(), P(), P("tm", "rows", None, None))
    out_specs = (
        P("tm", "rows", None, None),
        P("tm", "rows", None, None),
        P("tm", "rows"),
        P("tm", "rows"),
        P("tm", "rows"),
    )
    return jax.shard_map(shards, mesh=mesh, in_specs=in_specs, out_specs=out_specs, check_vma=False)
```

```python
import jax
import jax.numpy as jnp
from jax import lax
from jax.experimental import pallas as pl
from jax.experimental.pallas import tpu as pltpu
from jax.sharding import PartitionSpec as P

F32, BF16 = jnp.float32, jnp.bfloat16
MESH = pl.DeviceIdType.MESH
CA, CB, W = 256, 128, 96
CELLS = 4 * W
HALF_A = 27 * CA // 2
XA, YA = 1792, HALF_A - 1792
XB, YB = 512, 512
PB = 896
ORDER = (1, 2, 3, 0)


def dot(a, b, ca=1, cb=0):
    return lax.dot_general(a, b, (((ca,), (cb,)), ((), ())), preferred_element_type=F32)


def kernel(
    video, cot, ka_hbm, project, kb_hbm,
    out, grad_video, grad_a, grad_b, grad_p,
    ka, kb, vbuf, cbuf, mbuf, gbuf, mown, gown, xs, us, ms, gs,
    gt, ct, qt, send_a, recv_a, send_b, recv_b, part,
    s0xa, s0ya, r1xa, r1ya, s1xa, s1ya, r2ya, r2xa,
    s0xb, s0yb, r1xb, r1yb, s1xb, s1yb, r2yb, r2xb,
    t_a, t_b, msg, r3, total,
    sem_w, sem_v, sem_c, sem_m, sem_g, sem_a, sem_b,
    sem1xa, sem1ya, sem2ya, sem2xa, sem1xb, sem1yb, sem2yb, sem2xb, sem3,
):
    tm = lax.axis_index("tm")
    rows = lax.axis_index("rows")
    core = lax.rem(tm, 2)
    b = lax.rem(tm, 16)
    y_lo = tm // 16
    x = lax.rem(rows, 4)
    y = (rows // 4) * 2 + y_lo

    def x_peer(d):
        return (tm, (rows // 4) * 4 + lax.rem(x + d, 4))

    def y_peer(d):
        to = lax.rem(y + d, 4)
        return (lax.rem(to, 2) * 16 + b, (to // 2) * 4 + x)

    def z_peer(d):
        return (y_lo * 16 + lax.rem(b + d, 16), rows)

    def near(dt, dr):
        return (lax.rem(tm + 32 + dt, 32), lax.rem(rows + 8 + dr, 8))

    partner = (tm + 1 - 2 * core, rows)

    def remote(src, dst, sem, slot, to):
        return pltpu.make_async_remote_copy(
            src_ref=src, dst_ref=dst, send_sem=sem.at[0, slot], recv_sem=sem.at[1, slot],
            device_id=to, device_id_type=MESH,
        )

    load_b = pltpu.make_async_copy(kb_hbm, kb, sem_w.at[0])
    load_a = pltpu.make_async_copy(ka_hbm, ka, sem_w.at[1])
    load_b.start()
    load_a.start()

    barrier = pltpu.get_barrier_semaphore()
    peers = [near(dt, dr) for dt in (-1, 0, 1) for dr in (-1, 0, 1) if dt or dr]
    peers += [x_peer(d) for d in range(1, 4)] + [y_peer(d) for d in range(1, 4)]
    peers += [z_peer(d) for d in range(1, 16)]
    for to in peers:
        pl.semaphore_signal(barrier, inc=1, device_id=to, device_id_type=MESH)
    pl.semaphore_wait(barrier, len(peers))

    def halo(src, buf, way, sem):
        own = 2 if way > 0 else 0
        other = 2 - own
        copies = [
            remote(src, buf.at[pl.ds(other, 2), pl.ds(1, 2)], sem, 0, near(way, 0)),
            remote(src.at[:, 1], buf.at[pl.ds(own, 2), 0], sem, 1, near(0, 1)),
            remote(src.at[:, 0], buf.at[pl.ds(own, 2), 3], sem, 2, near(0, -1)),
            remote(src.at[:, 1], buf.at[pl.ds(other, 2), 0], sem, 3, near(way, 1)),
            remote(src.at[:, 0], buf.at[pl.ds(other, 2), 3], sem, 4, near(way, -1)),
        ]
        for cp in copies:
            cp.start()
        return copies

    def shifted(src, buf, dst, way, chan):
        own = 2 if way > 0 else 0
        inside = (tm > 0) if way > 0 else (tm < 31)
        cell = lax.broadcasted_iota(jnp.int32, (W, chan), 0)
        for f in range(4):
            mine = own <= f < own + 2
            for r in range(4):
                if mine and 1 <= r <= 2:
                    v = src[f - own, r - 1].astype(F32)
                else:
                    keep = None if mine else inside
                    if r == 0:
                        keep = (rows > 0) if keep is None else keep & (rows > 0)
                    if r == 3:
                        keep = (rows < 7) if keep is None else keep & (rows < 7)
                    v = jnp.where(keep, buf[f, r].astype(F32), 0.0)
                dst[f, r, :, chan : 2 * chan] = v.astype(BF16)
                left = jnp.where(cell == 0, 0.0, pltpu.roll(v, 1, 0))
                right = jnp.where(cell == W - 1, 0.0, pltpu.roll(v, W - 1, 0))
                dst[f, r, :, 0:chan] = left.astype(BF16)
                dst[f, r, :, 2 * chan : 3 * chan] = right.astype(BF16)

    def conv(src, weight, chan):
        acc = None
        for kt in range(3):
            for kr in range(3):
                at = (3 * kt + kr) * 3 * chan
                piece = src[kt : kt + 2, kr : kr + 2].reshape(CELLS, 3 * chan)
                term = dot(piece, weight[at : at + 3 * chan])
                acc = term if acc is None else acc + term
        return acc

    def back(src, weight, chan):
        acc = None
        for kt in range(3):
            for kr in range(3):
                for kc in range(3):
                    at = (9 * kt + 3 * kr + kc) * chan
                    piece = src[2 - kt : 4 - kt, 2 - kr : 4 - kr, :, (2 - kc) * chan : (3 - kc) * chan]
                    term = dot(piece.reshape(CELLS, chan), weight[at : at + chan], 1, 1)
                    acc = term if acc is None else acc + term
        return acc

    halo_c = halo(cot, cbuf, -1, sem_c)
    halo_v = halo(video, vbuf, 1, sem_v)

    load_b.wait()
    for cp in halo_c:
        cp.wait()
    shifted(cot, cbuf, us, -1, CB)
    grad_mid = cot[...].reshape(CELLS, CB).astype(F32) + back(us, kb, CB)
    cot_t = cot[...].reshape(CELLS, CB).astype(F32).T
    mid_t = grad_mid.T
    for c in range(2):
        pick = [slice(16 * j + 8 * c, 16 * j + 8 * c + 8) for j in range(8)]
        ct[c] = jnp.concatenate([cot_t[s] for s in pick], 0).astype(BF16)
        qt[c] = jnp.concatenate([mid_t[s] for s in pick], 0).astype(BF16)
    grad_h = dot(grad_mid.astype(BF16), project[...], 1, 1)

    load_a.wait()
    for cp in halo_v:
        cp.wait()
    shifted(video, vbuf, xs, 1, CA)
    pre = conv(xs, ka, CA)
    sig = jax.nn.sigmoid(pre)
    hidden = (pre * sig).astype(BF16)
    mid = dot(hidden, project[...])
    mown[...] = mid.astype(BF16).reshape(2, 2, W, CB)
    halo_m = halo(mown, mbuf, 1, sem_m)
    grad_pre = grad_h * sig * (1.0 + pre * (1.0 - sig))
    gown[...] = grad_pre.astype(BF16).reshape(2, 2, W, CA)
    halo_g = halo(gown, gbuf, -1, sem_g)
    out[...] = mid.reshape(2, 2, W, CB)
    grad_t = grad_pre.T
    for c in range(2):
        for j in range(8):
            gt[c, j] = grad_t[32 * j + 16 * c : 32 * j + 16 * c + 16].astype(BF16)

    def grad_chunk(src, left, k, chan):
        kt, kr = k // 3, k % 3
        piece = src[kt : kt + 2, kr : kr + 2].reshape(CELLS, 3 * chan)
        return dot(left, piece)

    copies_a = []
    theirs = gt[1 - core].reshape(128, CELLS)
    for k in range(9):
        send_a[k] = grad_chunk(xs, theirs, k, CA).astype(BF16).reshape(8, 16, 768)
        cp = remote(send_a.at[k], recv_a.at[k], sem_a, k, partner)
        cp.start()
        copies_a.append(cp)
    proj_theirs = dot(qt[1 - core], hidden)
    proj_mine = dot(qt[core], hidden)

    mine = gt[core].reshape(128, CELLS)
    cuts = sorted({768 * k for k in range(10)} | {0, XA, HALF_A, HALF_A + XA, 2 * HALF_A})
    for k in range(9):
        value = grad_chunk(xs, mine, k, CA)
        copies_a[k].wait()
        value = (value + recv_a[k].reshape(128, 768).astype(F32)).astype(BF16)
        inside = [c for c in cuts if 768 * k <= c <= 768 * k + 768]
        for lo, hi in zip(inside[:-1], inside[1:]):
            yl, at = lo // HALF_A, lo % HALF_A
            for j in range(8):
                cut = value[16 * j : 16 * j + 16, lo - 768 * k : hi - 768 * k]
                if at < XA:
                    s0xa[j % 4, (j // 4) * 2 + yl, :, at : at + hi - lo] = cut
                else:
                    s0ya[(j // 4) * 2 + yl, j % 4, :, at - XA : at - XA + hi - lo] = cut

    def first(s0x, r1x, sem1x, s0y, r1y, sem1y):
        in_x, in_y = [], []
        for d in (2, 1, 3):
            cp = remote(s0x.at[lax.rem(x + d, 4)], r1x.at[d - 1], sem1x, d - 1, x_peer(d))
            cp.start()
            in_x.append(cp)
            cp = remote(s0y.at[lax.rem(y + d, 4)], r1y.at[d - 1], sem1y, d - 1, y_peer(d))
            cp.start()
            in_y.append(cp)
        return in_x, in_y

    def second(copies, s0x, r1x, s1x, r2y, sem2y, s0y, r1y, s1y, r2x, sem2x):
        started = []
        for cp in copies[0]:
            cp.wait()
        for d in ORDER:
            to = lax.rem(y + d, 4)
            acc = s0x[x, to].astype(F32)
            for s in range(3):
                acc = acc + r1x[s, to].astype(F32)
            s1x[to] = acc.astype(BF16)
            if d:
                cp = remote(s1x.at[to], r2y.at[d - 1], sem2y, d - 1, y_peer(d))
                cp.start()
                started.append(cp)
        for cp in copies[1]:
            cp.wait()
        for d in ORDER:
            to = lax.rem(x + d, 4)
            acc = s0y[y, to].astype(F32)
            for s in range(3):
                acc = acc + r1y[s, to].astype(F32)
            s1y[to] = acc.astype(BF16)
            if d:
                cp = remote(s1y.at[to], r2x.at[d - 1], sem2x, d - 1, x_peer(d))
                cp.start()
                started.append(cp)
        return started

    def summed(copies, s1x, r2y, s1y, r2x, t_ref, lx):
        for cp in copies:
            cp.wait()
        acc = s1x[y].astype(F32)
        for s in range(3):
            acc = acc + r2y[s].astype(F32)
        t_ref[:, :lx] = acc
        acc = s1y[x].astype(F32)
        for s in range(3):
            acc = acc + r2x[s].astype(F32)
        t_ref[:, lx:] = acc

    first_a = first(s0xa, r1xa, sem1xa, s0ya, r1ya, sem1ya)

    for cp in halo_m:
        cp.wait()
    shifted(mown, mbuf, ms, 1, CB)

    def packed(half, proj):
        left = ct[half]
        for k in range(9):
            part[:, 384 * k : 384 * k + 384] = grad_chunk(ms, left, k, CB)
        blocks = []
        for j in range(8):
            row = slice(8 * j, 8 * j + 8)
            for yl in range(2):
                at = 13 * 128 * yl
                body = jnp.concatenate([part[row, at : at + PB], part[row, at + PB : at + 2 * PB]], 0)
                tail = jnp.concatenate([proj[row, 128 * yl : 128 * yl + 128], jnp.zeros((8, 128), F32)], 0)
                blocks.append((j, yl, jnp.concatenate([body, tail], 1)))
        return blocks

    for j, yl, value in packed(1 - core, proj_theirs):
        send_b[j, yl] = value.astype(BF16)
    copy_b = remote(send_b, recv_b, sem_b, 0, partner)
    copy_b.start()
    out[...] = out[...] + conv(ms, kb, CB).reshape(2, 2, W, CB)
    blocks = packed(core, proj_mine)
    copy_b.wait()
    for j, yl, value in blocks:
        value = (value + recv_b[j, yl].astype(F32)).astype(BF16)
        s0xb[j % 4, (j // 4) * 2 + yl] = value[:, :XB]
        s0yb[(j // 4) * 2 + yl, j % 4] = value[:, XB:]
    first_b = first(s0xb, r1xb, sem1xb, s0yb, r1yb, sem1yb)

    for cp in halo_g:
        cp.wait()
    shifted(gown, gbuf, gs, -1, CA)
    grad_video[...] = back(gs, ka, CA).reshape(2, 2, W, CA)

    second_a = second(first_a, s0xa, r1xa, s1xa, r2ya, sem2ya, s0ya, r1ya, s1ya, r2xa, sem2xa)
    second_b = second(first_b, s0xb, r1xb, s1xb, r2yb, sem2yb, s0yb, r1yb, s1yb, r2xb, sem2xb)
    summed(second_a, s1xa, r2ya, s1ya, r2xa, t_a, XA)
    summed(second_b, s1xb, r2yb, s1yb, r2xb, t_b, XB)

    part_b = jnp.concatenate([t_b[0:8, 0:PB], t_b[8:16, 0:PB]], 1)
    part_b = jnp.where(y_lo == 0, part_b[:, 0:1728], part_b[:, 64:1792])
    part_p = t_b[0:8, PB : PB + 128]
    for k in range(16):
        high = jnp.concatenate([t_a[:, 216 * k : 216 * k + 216], jnp.zeros((16, 40), F32)], 1)
        low = jnp.concatenate(
            [
                part_b[:, 108 * k : 108 * k + 108], jnp.zeros((8, 4), F32),
                part_p[:, 8 * k : 8 * k + 8], jnp.zeros((8, 8), F32),
            ], 1,
        )
        low = jnp.concatenate([low, jnp.zeros((8, 128), F32)], 0)
        msg[k] = jnp.concatenate([high, low], 1).astype(BF16)
    last = []
    for d in range(1, 16):
        cp = remote(msg.at[lax.rem(b + d, 16)], r3.at[d - 1], sem3, d - 1, z_peer(d))
        cp.start()
        last.append(cp)
    for cp in last:
        cp.wait()
    same = msg[b].astype(F32)
    for d in range(2, 16, 2):
        same = same + r3[d - 1].astype(F32)
    other = r3[0].astype(F32)
    for d in range(3, 16, 2):
        other = other + r3[d - 1].astype(F32)
    scale = 1.0 / (64 * 16 * W) ** 0.5
    total[core] = same * scale
    total[1 - core] = other * scale
    grad_a[...] = total[:, :, 0:256].reshape(32, 256).T[0:216]
    low = jnp.concatenate([total[0, 0:8, 256:384], total[1, 0:8, 256:384]], 0).T
    grad_b[...] = low[0:108]
    grad_p[...] = low[112:120]


def shards(video, kernel_a, project, kernel_b, cotangent):
    dma = pltpu.SemaphoreType.DMA
    vmem = pl.BlockSpec(memory_space=pltpu.VMEM)
    hbm = pl.BlockSpec(memory_space=pl.ANY)

    def group(lx, ly):
        return [
            pltpu.VMEM((4, 4, 16, lx), BF16), pltpu.VMEM((4, 4, 16, ly), BF16),
            pltpu.VMEM((3, 4, 16, lx), BF16), pltpu.VMEM((3, 4, 16, ly), BF16),
            pltpu.VMEM((4, 16, lx), BF16), pltpu.VMEM((4, 16, ly), BF16),
            pltpu.VMEM((3, 16, lx), BF16), pltpu.VMEM((3, 16, ly), BF16),
        ]

    return pl.pallas_call(
        kernel,
        out_shape=[
            jax.ShapeDtypeStruct((2, 2, W, CB), F32),
            jax.ShapeDtypeStruct((2, 2, W, CA), F32),
            jax.ShapeDtypeStruct((216, 32), F32),
            jax.ShapeDtypeStruct((108, 16), F32),
            jax.ShapeDtypeStruct((8, 16), F32),
        ],
        in_specs=[vmem, vmem, hbm, vmem, hbm],
        out_specs=[vmem] * 5,
        scratch_shapes=[
            pltpu.VMEM((27 * CA, CA), BF16), pltpu.VMEM((27 * CB, CB), BF16),
            pltpu.VMEM((4, 4, W, CA), BF16), pltpu.VMEM((4, 4, W, CB), BF16),
            pltpu.VMEM((4, 4, W, CB), BF16), pltpu.VMEM((4, 4, W, CA), BF16),
            pltpu.VMEM((2, 2, W, CB), BF16), pltpu.VMEM((2, 2, W, CA), BF16),
            pltpu.VMEM((4, 4, W, 3 * CA), BF16), pltpu.VMEM((4, 4, W, 3 * CB), BF16),
            pltpu.VMEM((4, 4, W, 3 * CB), BF16), pltpu.VMEM((4, 4, W, 3 * CA), BF16),
            pltpu.VMEM((2, 8, 16, CELLS), BF16), pltpu.VMEM((2, 64, CELLS), BF16),
            pltpu.VMEM((2, 64, CELLS), BF16),
            pltpu.VMEM((9, 8, 16, 768), BF16), pltpu.VMEM((9, 8, 16, 768), BF16),
            pltpu.VMEM((8, 2, 16, XB + YB), BF16), pltpu.VMEM((8, 2, 16, XB + YB), BF16),
            pltpu.VMEM((64, 27 * CB), F32),
            *group(XA, YA),
            *group(XB, YB),
            pltpu.VMEM((16, HALF_A), F32), pltpu.VMEM((16, XB + YB), F32),
            pltpu.VMEM((16, 16, 384), BF16), pltpu.VMEM((15, 16, 384), BF16),
            pltpu.VMEM((2, 16, 384), F32),
            dma((2,)), dma((2, 5)), dma((2, 5)), dma((2, 5)), dma((2, 5)), dma((2, 9)), dma((2, 1)),
            *[dma((2, 3)) for _ in range(8)],
            dma((2, 15)),
        ],
        compiler_params=pltpu.CompilerParams(
            collective_id=0, has_side_effects=True, vmem_limit_bytes=56 * 1024 * 1024
        ),
    )(video, cotangent, kernel_a, project, kernel_b)


def solution(mesh):
    cells = P("tm", "rows", None, None)
    return jax.shard_map(
        shards,
        mesh=mesh,
        in_specs=(cells, P(), P(), P(), cells),
        out_specs=(cells, cells, P("tm", "rows"), P("tm", "rows"), P("tm", "rows")),
        check_vma=False,
    )
```

```python
import jax
import jax.numpy as jnp
from jax import lax
from jax.experimental import pallas as pl
from jax.experimental.pallas import tpu as pltpu
from jax.sharding import PartitionSpec as P

F32, BF16 = jnp.float32, jnp.bfloat16
MESH = pl.DeviceIdType.MESH
CA, CB, W = 256, 128, 96
CELLS = 4 * W
HALF_A = 27 * CA // 2
XA, YA = 1792, HALF_A - 1792
XB, YB = 512, 512
PB = 896
ORDER = (1, 2, 3, 0)


def dot(a, b, ca=1, cb=0):
    return lax.dot_general(a, b, (((ca,), (cb,)), ((), ())), preferred_element_type=F32)


def kernel(
    video_hbm, cot_hbm, ka_hbm, project_hbm, kb_hbm,
    out, grad_video, grad_a, grad_b, grad_p,
    video, cot, project, ka, kb, vbuf, cbuf, mbuf, gbuf, mown, gown, xs, us, ms, gs,
    gt, qt, send_a, recv_a, send_b, recv_b, part,
    s0xa, s0ya, r1xa, r1ya, s1xa, s1ya, r2ya, r2xa,
    s0xb, s0yb, r1xb, r1yb, s1xb, s1yb, r2yb, r2xb,
    t_a, t_b, msg, r3, total,
    sem_w, sem_v, sem_c, sem_m, sem_g, sem_a, sem_b,
    sem1xa, sem1ya, sem2ya, sem2xa, sem1xb, sem1yb, sem2yb, sem2xb, sem3,
):
    tm = lax.axis_index("tm")
    rows = lax.axis_index("rows")
    core = lax.rem(tm, 2)
    b = lax.rem(tm, 16)
    y_lo = tm // 16
    x = lax.rem(rows, 4)
    y = (rows // 4) * 2 + y_lo
    upper, lower = rows > 0, rows < 7

    def x_peer(d):
        return (tm, (rows // 4) * 4 + lax.rem(x + d, 4))

    def y_peer(d):
        to = lax.rem(y + d, 4)
        return (lax.rem(to, 2) * 16 + b, (to // 2) * 4 + x)

    def z_peer(d):
        return (y_lo * 16 + lax.rem(b + d, 16), rows)

    def near(dt, dr):
        return (lax.rem(tm + 32 + dt, 32), lax.rem(rows + 8 + dr, 8))

    partner = (tm + 1 - 2 * core, rows)

    def remote(src, dst, sem, slot, to):
        return pltpu.make_async_remote_copy(
            src_ref=src, dst_ref=dst, send_sem=sem.at[0, slot], recv_sem=sem.at[1, slot],
            device_id=to, device_id_type=MESH,
        )

    barrier = pltpu.get_barrier_semaphore()
    peers = [near(dt, dr) for dt, dr in ((0, 1), (0, -1), (1, 0), (-1, 0))]
    peers += [x_peer(d) for d in range(1, 4)] + [y_peer(d) for d in range(1, 4)]
    peers += [z_peer(d) for d in range(1, 16)]
    for to in peers:
        pl.semaphore_signal(barrier, inc=1, device_id=to, device_id_type=MESH)

    loads = [
        pltpu.make_async_copy(src, dst, sem_w.at[i])
        for i, (src, dst) in enumerate(
            ((cot_hbm, cot), (video_hbm, video), (kb_hbm, kb), (project_hbm, project), (ka_hbm, ka))
        )
    ]
    for cp in loads:
        cp.start()

    for buf, chan in ((vbuf, CA), (cbuf, CB), (mbuf, CB), (gbuf, CA)):

        @pl.when(rows == 0)
        def _():
            buf[:, 0] = jnp.zeros((4, W, chan), BF16)

        @pl.when(rows == 7)
        def _():
            buf[:, 3] = jnp.zeros((4, W, chan), BF16)

    class Halo:
        def __init__(self, src, buf, way, sem):
            own = 2 if way > 0 else 0
            mine, theirs = pl.ds(own, 2), pl.ds(2 - own, 2)
            beside = near(way, 0)
            self.full = remote(src, buf.at[theirs, pl.ds(1, 2)], sem, 0, beside)
            self.down = remote(src.at[:, 1], buf.at[mine, 0], sem, 1, near(0, 1))
            self.up = remote(src.at[:, 0], buf.at[mine, 3], sem, 2, near(0, -1))
            self.on_top = remote(buf.at[mine, 0], buf.at[theirs, 0], sem, 3, beside)
            self.on_low = remote(buf.at[mine, 3], buf.at[theirs, 3], sem, 4, beside)

        def rims(self):
            pl.when(lower)(self.down.start)
            pl.when(upper)(self.up.start)

        def forward(self):
            @pl.when(upper)
            def _():
                self.down.wait_recv()
                self.on_top.start()

            @pl.when(lower)
            def _():
                self.up.wait_recv()
                self.on_low.start()

        def corners(self):
            @pl.when(upper)
            def _():
                self.on_top.wait()
                self.up.wait_send()

            @pl.when(lower)
            def _():
                self.on_low.wait()
                self.down.wait_send()

    class Shifts:
        def __init__(self, src, buf, dst, way, chan):
            self.own = 2 if way > 0 else 0
            self.inside = (tm > 0) if way > 0 else (tm < 31)
            self.src, self.buf, self.dst, self.chan = src, buf, dst, chan

        def make(self, frames, rows_of):
            chan, dst = self.chan, self.dst
            cell = lax.broadcasted_iota(jnp.int32, (W, chan), 0)
            first = self.own if frames == "own" else 2 - self.own
            for f in (first, first + 1):
                for r in rows_of:
                    if frames == "own" and 1 <= r <= 2:
                        v = self.src[f - self.own, r - 1]
                    else:
                        v = self.buf[f, r]
                    v = v.astype(F32)
                    if frames != "own":
                        v = jnp.where(self.inside, v, 0.0)
                    dst[f, r, :, chan : 2 * chan] = v.astype(BF16)
                    left = jnp.where(cell == 0, 0.0, pltpu.roll(v, 1, 0))
                    right = jnp.where(cell == W - 1, 0.0, pltpu.roll(v, W - 1, 0))
                    dst[f, r, :, 0:chan] = left.astype(BF16)
                    dst[f, r, :, 2 * chan : 3 * chan] = right.astype(BF16)

    CENTRE, EDGE, PAST, CORNERS = (
        [(2, 1)], [(2, 0), (2, 2)], [(0, 1), (1, 1)], [(0, 0), (0, 2), (1, 0), (1, 2)],
    )

    def conv(acc, src, weight, chan, taps):
        for kt, kr in taps:
            at = (3 * kt + kr) * 3 * chan
            piece = src[kt : kt + 2, kr : kr + 2].reshape(CELLS, 3 * chan)
            term = dot(piece, weight[at : at + 3 * chan])
            acc = term if acc is None else acc + term
        return acc

    def back(acc, src, weight, chan, taps):
        for kt, kr in taps:
            for kc in range(3):
                at = (9 * kt + 3 * kr + kc) * chan
                piece = src[2 - kt : 4 - kt, 2 - kr : 4 - kr, :, (2 - kc) * chan : (3 - kc) * chan]
                term = dot(piece.reshape(CELLS, chan), weight[at : at + chan], 1, 1)
                acc = term if acc is None else acc + term
        return acc

    halo_c = Halo(cot, cbuf, -1, sem_c)
    halo_v = Halo(video, vbuf, 1, sem_v)
    shift_c = Shifts(cot, cbuf, us, -1, CB)
    shift_v = Shifts(video, vbuf, xs, 1, CA)

    loads[0].wait()
    loads[1].wait()
    shift_c.make("own", (1, 2))
    shift_v.make("own", (1, 2))
    loads[2].wait()
    loads[3].wait()
    back_b = back(None, us, kb, CB, CENTRE)
    loads[4].wait()
    pre = conv(None, xs, ka, CA, CENTRE)

    pl.semaphore_wait(barrier, len(peers))
    halo_c.rims()
    halo_v.rims()
    halo_c.full.start()
    halo_v.full.start()
    halo_c.forward()
    halo_v.forward()
    shift_c.make("own", (0, 3))
    shift_v.make("own", (0, 3))
    back_b = back(back_b, us, kb, CB, EDGE)
    pre = conv(pre, xs, ka, CA, EDGE)
    halo_c.full.wait()
    shift_c.make("other", (1, 2))
    back_b = back(back_b, us, kb, CB, PAST)
    halo_v.full.wait()
    shift_v.make("other", (1, 2))
    pre = conv(pre, xs, ka, CA, PAST)
    halo_c.corners()
    shift_c.make("other", (0, 3))
    back_b = back(back_b, us, kb, CB, CORNERS)
    grad_mid = cot[...].reshape(CELLS, CB).astype(F32) + back_b
    mid_t = grad_mid.T
    for c in range(2):
        pick = [mid_t[16 * j + 8 * c : 16 * j + 8 * c + 8] for j in range(8)]
        qt[c] = jnp.concatenate(pick, 0).astype(BF16)
    grad_h = dot(grad_mid.astype(BF16), project[...], 1, 1)

    halo_v.corners()
    shift_v.make("other", (0, 3))
    pre = conv(pre, xs, ka, CA, CORNERS)
    sig = jax.nn.sigmoid(pre)
    hidden = (pre * sig).astype(BF16)
    mid = dot(hidden, project[...])
    mown[...] = mid.astype(BF16).reshape(2, 2, W, CB)
    halo_m = Halo(mown, mbuf, 1, sem_m)
    halo_m.rims()
    halo_m.full.start()
    grad_pre = grad_h * sig * (1.0 + pre * (1.0 - sig))
    gown[...] = grad_pre.astype(BF16).reshape(2, 2, W, CA)
    halo_g = Halo(gown, gbuf, -1, sem_g)
    halo_g.rims()
    halo_g.full.start()
    out[...] = mid.reshape(2, 2, W, CB)
    grad_t = grad_pre.T
    for c in range(2):
        for j in range(8):
            gt[c, j] = grad_t[32 * j + 16 * c : 32 * j + 16 * c + 16].astype(BF16)

    def chunk_a(left, k):
        kt, kr = k // 3, k % 3
        return dot(left, xs[kt : kt + 2, kr : kr + 2].reshape(CELLS, 3 * CA))

    copies_a = []
    theirs = gt[1 - core].reshape(128, CELLS)
    for k in range(9):
        send_a[k] = chunk_a(theirs, k).astype(BF16).reshape(8, 16, 768)
        cp = remote(send_a.at[k], recv_a.at[k], sem_a, k, partner)
        cp.start()
        copies_a.append(cp)

    class Group:
        def __init__(self, s0x, r1x, s1x, r2y, sem1x, sem2y, s0y, r1y, s1y, r2x, sem1y, sem2x):
            self.s0x, self.r1x, self.s1x, self.r2y, self.sem1x, self.sem2y = s0x, r1x, s1x, r2y, sem1x, sem2y
            self.s0y, self.r1y, self.s1y, self.r2x, self.sem1y, self.sem2x = s0y, r1y, s1y, r2x, sem1y, sem2x

        def x1(self, d, yl):
            src = self.s0x.at[lax.rem(x + d, 4), yl]
            return remote(src, self.r1x.at[d - 1, yl], self.sem1x, 2 * (d - 1) + yl, x_peer(d))

        def y1(self, d):
            return remote(self.s0y.at[lax.rem(y + d, 4)], self.r1y.at[d - 1], self.sem1y, d - 1, y_peer(d))

        def y2(self, d):
            return remote(self.s1x.at[lax.rem(y + d, 4)], self.r2y.at[d - 1], self.sem2y, d - 1, y_peer(d))

        def x2(self, d):
            return remote(self.s1y.at[lax.rem(x + d, 4)], self.r2x.at[d - 1], self.sem2x, d - 1, x_peer(d))

        def send_x(self, yl):
            for d in (2, 1, 3):
                self.x1(d, yl).start()

        def send_y(self, yl):
            for yh in range(2):
                d = lax.rem(2 * yh + yl - y + 4, 4)

                @pl.when(d > 0)
                def _():
                    self.y1(d).start()

        def add_x(self, yl):
            for d in (1, 2, 3):
                self.x1(d, yl).wait()
            for yh in range(2):
                to = 2 * yh + yl
                acc = self.s0x[x, yl, yh].astype(F32)
                for s in range(3):
                    acc = acc + self.r1x[s, yl, yh].astype(F32)
                self.s1x[to] = acc.astype(BF16)
                d = lax.rem(to - y + 4, 4)

                @pl.when(d > 0)
                def _():
                    self.y2(d).start()

        def add_y(self):
            for d in (1, 2, 3):
                self.y1(d).wait()
            for d in ORDER:
                to = lax.rem(x + d, 4)
                acc = self.s0y[y, to].astype(F32)
                for s in range(3):
                    acc = acc + self.r1y[s, to].astype(F32)
                self.s1y[to] = acc.astype(BF16)
                if d:
                    self.x2(d).start()

        def finish(self, t_ref, lx):
            for d in (1, 2, 3):
                self.y2(d).wait()
            acc = self.s1x[y].astype(F32)
            for s in range(3):
                acc = acc + self.r2y[s].astype(F32)
            t_ref[:, :lx] = acc
            for d in (1, 2, 3):
                self.x2(d).wait()
            acc = self.s1y[x].astype(F32)
            for s in range(3):
                acc = acc + self.r2x[s].astype(F32)
            t_ref[:, lx:] = acc

    group_a = Group(s0xa, r1xa, s1xa, r2ya, sem1xa, sem2ya, s0ya, r1ya, s1ya, r2xa, sem1ya, sem2xa)
    group_b = Group(s0xb, r1xb, s1xb, r2yb, sem1xb, sem2yb, s0yb, r1yb, s1yb, r2xb, sem1yb, sem2xb)

    mine = gt[core].reshape(128, CELLS)
    cuts = sorted({768 * k for k in range(10)} | {0, XA, HALF_A, HALF_A + XA, 2 * HALF_A})
    for k in range(9):
        value = chunk_a(mine, k)
        copies_a[k].wait()
        value = (value + recv_a[k].reshape(128, 768).astype(F32)).astype(BF16)
        inside = [c for c in cuts if 768 * k <= c <= 768 * k + 768]
        for lo, hi in zip(inside[:-1], inside[1:]):
            yl, at = lo // HALF_A, lo % HALF_A
            for j in range(8):
                cut = value[16 * j : 16 * j + 16, lo - 768 * k : hi - 768 * k]
                if at < XA:
                    s0xa[j % 4, yl, j // 4, :, at : at + hi - lo] = cut
                else:
                    s0ya[(j // 4) * 2 + yl, j % 4, :, at - XA : at - XA + hi - lo] = cut
            if hi % HALF_A == XA:
                group_a.send_x(yl)
            if hi % HALF_A == 0:
                group_a.send_y(yl)

    mid_own = mid.T.astype(BF16)
    for k in range(9):
        kt, kr = k // 3, k % 3
        value = dot(mid_own, us[2 - kt : 4 - kt, 2 - kr : 4 - kr].reshape(CELLS, 3 * CB))
        for kc in range(3):
            tap = value[:, (2 - kc) * CB : (3 - kc) * CB].T
            at = (3 * k + kc) * CB
            for c in range(2):
                for j in range(8):
                    part[c, j, :, at : at + CB] = tap[16 * j + 8 * c : 16 * j + 8 * c + 8]

    def packed(half):
        proj = dot(qt[half], hidden)
        for j in range(8):
            for yl in range(2):
                at = 13 * CB * yl
                upper_half = part[half, j, :, at : at + PB]
                lower_half = part[half, j, :, at + PB : at + 2 * PB]
                body = jnp.concatenate([upper_half, lower_half], 0)
                tail = proj[8 * j : 8 * j + 8, 128 * yl : 128 * yl + 128]
                tail = jnp.concatenate([tail, jnp.zeros((8, 128), F32)], 0)
                yield j, yl, jnp.concatenate([body, tail], 1)

    for j, yl, value in packed(1 - core):
        send_b[j, yl] = value.astype(BF16)
    copy_b = remote(send_b, recv_b, sem_b, 0, partner)
    copy_b.start()
    halo_m.forward()
    halo_g.forward()
    copy_b.wait()
    for j, yl, value in packed(core):
        value = (value + recv_b[j, yl].astype(F32)).astype(BF16)
        s0xb[j % 4, yl, j // 4] = value[:, :XB]
        s0yb[(j // 4) * 2 + yl, j % 4] = value[:, XB:]
    for yl in range(2):
        group_b.send_x(yl)
        group_b.send_y(yl)

    every = CENTRE + EDGE + PAST + CORNERS
    shift_m = Shifts(mown, mbuf, ms, 1, CB)
    shift_m.make("own", (0, 1, 2, 3))
    halo_m.full.wait()
    halo_m.corners()
    shift_m.make("other", (0, 1, 2, 3))
    out[...] = out[...] + conv(None, ms, kb, CB, every).reshape(2, 2, W, CB)
    shift_g = Shifts(gown, gbuf, gs, -1, CA)
    shift_g.make("own", (0, 1, 2, 3))
    halo_g.full.wait()
    halo_g.corners()
    shift_g.make("other", (0, 1, 2, 3))
    grad_video[...] = back(None, gs, ka, CA, every).reshape(2, 2, W, CA)

    group_a.add_x(0)
    group_a.add_x(1)
    group_a.add_y()
    group_b.add_x(0)
    group_b.add_x(1)
    group_b.add_y()
    group_a.finish(t_a, XA)
    group_b.finish(t_b, XB)

    part_b = jnp.concatenate([t_b[0:8, 0:PB], t_b[8:16, 0:PB]], 1)
    part_b = jnp.where(y_lo == 0, part_b[:, 0:1728], part_b[:, 64:1792])
    part_p = t_b[0:8, PB : PB + 128]
    for k in range(16):
        high = jnp.concatenate([t_a[:, 216 * k : 216 * k + 216], jnp.zeros((16, 40), F32)], 1)
        low = jnp.concatenate(
            [
                part_b[:, 108 * k : 108 * k + 108], jnp.zeros((8, 4), F32),
                part_p[:, 8 * k : 8 * k + 8], jnp.zeros((8, 8), F32),
            ], 1,
        )
        low = jnp.concatenate([low, jnp.zeros((8, 128), F32)], 0)
        msg[k] = jnp.concatenate([high, low], 1).astype(BF16)
    last = []
    for d in range(1, 16):
        cp = remote(msg.at[lax.rem(b + d, 16)], r3.at[d - 1], sem3, d - 1, z_peer(d))
        cp.start()
        last.append(cp)
    for cp in last:
        cp.wait()
    same = msg[b].astype(F32)
    for d in range(2, 16, 2):
        same = same + r3[d - 1].astype(F32)
    other = r3[0].astype(F32)
    for d in range(3, 16, 2):
        other = other + r3[d - 1].astype(F32)
    scale = 1.0 / (64 * 16 * W) ** 0.5
    total[core] = same * scale
    total[1 - core] = other * scale
    grad_a[...] = total[:, :, 0:216].reshape(32, 216)
    low = jnp.concatenate([total[0, 0:8, 256:384], total[1, 0:8, 256:384]], 0)
    grad_b[...] = low[:, 0:108]
    grad_p[...] = low.T[112:120]


def written(*refs):
    for i in range(5):
        refs[5 + i][...] = refs[i][...]


def shards(video, kernel_a, project, kernel_b, cotangent):
    dma = pltpu.SemaphoreType.DMA
    vmem = pl.BlockSpec(memory_space=pltpu.VMEM)
    hbm = pl.BlockSpec(memory_space=pl.ANY)

    def group(lx, ly):
        return [
            pltpu.VMEM((4, 2, 2, 16, lx), BF16), pltpu.VMEM((4, 4, 16, ly), BF16),
            pltpu.VMEM((3, 2, 2, 16, lx), BF16), pltpu.VMEM((3, 4, 16, ly), BF16),
            pltpu.VMEM((4, 16, lx), BF16), pltpu.VMEM((4, 16, ly), BF16),
            pltpu.VMEM((3, 16, lx), BF16), pltpu.VMEM((3, 16, ly), BF16),
        ]

    results = pl.pallas_call(
        kernel,
        out_shape=[
            jax.ShapeDtypeStruct((2, 2, W, CB), F32),
            jax.ShapeDtypeStruct((2, 2, W, CA), F32),
            jax.ShapeDtypeStruct((32, 216), F32),
            jax.ShapeDtypeStruct((16, 108), F32),
            jax.ShapeDtypeStruct((8, 16), F32),
        ],
        in_specs=[hbm] * 5,
        out_specs=[vmem] * 5,
        scratch_shapes=[
            pltpu.VMEM((2, 2, W, CA), BF16), pltpu.VMEM((2, 2, W, CB), BF16), pltpu.VMEM((CA, CB), BF16),
            pltpu.VMEM((27 * CA, CA), BF16), pltpu.VMEM((27 * CB, CB), BF16),
            pltpu.VMEM((4, 4, W, CA), BF16), pltpu.VMEM((4, 4, W, CB), BF16),
            pltpu.VMEM((4, 4, W, CB), BF16), pltpu.VMEM((4, 4, W, CA), BF16),
            pltpu.VMEM((2, 2, W, CB), BF16), pltpu.VMEM((2, 2, W, CA), BF16),
            pltpu.VMEM((4, 4, W, 3 * CA), BF16), pltpu.VMEM((4, 4, W, 3 * CB), BF16),
            pltpu.VMEM((4, 4, W, 3 * CB), BF16), pltpu.VMEM((4, 4, W, 3 * CA), BF16),
            pltpu.VMEM((2, 8, 16, CELLS), BF16), pltpu.VMEM((2, 64, CELLS), BF16),
            pltpu.VMEM((9, 8, 16, 768), BF16), pltpu.VMEM((9, 8, 16, 768), BF16),
            pltpu.VMEM((8, 2, 16, XB + YB), BF16), pltpu.VMEM((8, 2, 16, XB + YB), BF16),
            pltpu.VMEM((2, 8, 8, 27 * CB), F32),
            *group(XA, YA),
            *group(XB, YB),
            pltpu.VMEM((16, HALF_A), F32), pltpu.VMEM((16, XB + YB), F32),
            pltpu.VMEM((16, 16, 384), BF16), pltpu.VMEM((15, 16, 384), BF16),
            pltpu.VMEM((2, 16, 384), F32),
            dma((5,)), dma((2, 5)), dma((2, 5)), dma((2, 5)), dma((2, 5)), dma((2, 9)), dma((2, 1)),
            *[dma((2, n)) for n in (6, 3, 3, 3) * 2],
            dma((2, 15)),
        ],
        compiler_params=pltpu.CompilerParams(
            collective_id=0, has_side_effects=True, vmem_limit_bytes=56 * 1024 * 1024
        ),
    )(video, cotangent, kernel_a, project, kernel_b)
    results = pl.pallas_call(
        written,
        out_shape=[jax.ShapeDtypeStruct(r.shape, F32) for r in results],
        in_specs=[vmem] * 5,
        out_specs=[vmem] * 5,
    )(*results)
    return results[0], results[1], results[2].T, results[3].T, results[4]


def solution(mesh):
    cells = P("tm", "rows", None, None)
    return jax.shard_map(
        shards,
        mesh=mesh,
        in_specs=(cells, P(), P(), P(), cells),
        out_specs=(cells, cells, P("tm", "rows"), P("tm", "rows"), P("tm", "rows")),
        check_vma=False,
    )
```

```python
import jax
import jax.numpy as jnp
from jax import lax
from jax.experimental import pallas as pl
from jax.experimental.pallas import tpu as pltpu
from jax.sharding import PartitionSpec as P

F32, BF16 = jnp.float32, jnp.bfloat16
MESH = pl.DeviceIdType.MESH
CA, CB, W = 256, 128, 96
CELLS = 4 * W
HALF_A = 27 * CA // 2
XA, YA = 1792, HALF_A - 1792
ORDER = (1, 2, 3, 0)


def dot(a, b, ca=1, cb=0):
    return lax.dot_general(a, b, (((ca,), (cb,)), ((), ())), preferred_element_type=F32)


def kernel(
    video_hbm, cot_hbm, ka_hbm, project_hbm, kb_hbm,
    out_hbm, grad_video_hbm, grad_a, grad_b, grad_p,
    out, grad_video, video, cot, project, ka, kb, vbuf, cbuf, mbuf, gbuf, mown, gown, xs, us, ms, gs,
    gt, qt, send_a, recv_a, send_b, recv_b, part,
    s0xa, s0ya, r1xa, r1ya, s1xa, s1ya, r2ya, r2xa,
    s0b, r1b, s1b, r2b, tb, gb,
    t_a, msg, r3, total,
    sem_w, sem_v, sem_c, sem_m, sem_g, sem_a, sem_b,
    sem1xa, sem1ya, sem2ya, sem2xa, sem3, sem1b, sem2b, sem3b, sem_o,
):
    tm = lax.axis_index("tm")
    rows = lax.axis_index("rows")
    core = lax.rem(tm, 2)
    b = lax.rem(tm, 16)
    y_lo = tm // 16
    x = lax.rem(rows, 4)
    y = (rows // 4) * 2 + y_lo
    upper, lower = rows > 0, rows < 7
    since, until = tm > 0, tm < 31

    def x_peer(d):
        return (tm, (rows // 4) * 4 + lax.rem(x + d, 4))

    def y_peer(d):
        to = lax.rem(y + d, 4)
        return (lax.rem(to, 2) * 16 + b, (to // 2) * 4 + x)

    def z_peer(d):
        return (y_lo * 16 + lax.rem(b + d, 16), rows)

    def same_core(d):
        return (y_lo * 16 + lax.rem(b + 2 * d, 16), rows)

    def plane(dx, dy):
        to = lax.rem(y + dy, 4)
        return (lax.rem(to, 2) * 16 + b, (to // 2) * 4 + lax.rem(x + dx, 4))

    def near(dt, dr):
        return (lax.rem(tm + 32 + dt, 32), lax.rem(rows + 8 + dr, 8))

    partner = (tm + 1 - 2 * core, rows)

    def remote(src, dst, sem, slot, to):
        return pltpu.make_async_remote_copy(
            src_ref=src, dst_ref=dst, send_sem=sem.at[0, slot], recv_sem=sem.at[1, slot],
            device_id=to, device_id_type=MESH,
        )

    barrier = pltpu.get_barrier_semaphore()
    peers = [near(dt, dr) for dt in (-1, 0, 1) for dr in (-1, 0, 1) if dt or dr]
    peers += [plane(dx, dy) for dx in range(4) for dy in range(4) if dx or dy]
    peers += [z_peer(d) for d in range(1, 16)]
    for to in peers:
        pl.semaphore_signal(barrier, inc=1, device_id=to, device_id_type=MESH)

    loads = [
        pltpu.make_async_copy(src, dst, sem_w.at[i])
        for i, (src, dst) in enumerate(
            ((cot_hbm, cot), (video_hbm, video), (kb_hbm, kb), (project_hbm, project), (ka_hbm, ka))
        )
    ]
    for cp in loads:
        cp.start()

    for buf, chan in ((vbuf, CA), (cbuf, CB), (mbuf, CB), (gbuf, CA)):

        @pl.when(rows == 0)
        def _():
            buf[:, 0] = jnp.zeros((4, W, chan), BF16)

        @pl.when(rows == 7)
        def _():
            buf[:, 3] = jnp.zeros((4, W, chan), BF16)

    @pl.when(tm == 0)
    def _():
        vbuf[0:2] = jnp.zeros((2, 4, W, CA), BF16)
        mbuf[0:2] = jnp.zeros((2, 4, W, CB), BF16)

    @pl.when(tm == 31)
    def _():
        cbuf[2:4] = jnp.zeros((2, 4, W, CB), BF16)
        gbuf[2:4] = jnp.zeros((2, 4, W, CA), BF16)

    class Halo:
        def __init__(self, src, buf, way, sem, direct):
            own = 2 if way > 0 else 0
            mine, theirs = pl.ds(own, 2), pl.ds(2 - own, 2)
            self.gives, self.takes = (until, since) if way > 0 else (since, until)
            self.full = remote(src, buf.at[theirs, pl.ds(1, 2)], sem, 0, near(way, 0))
            self.down = remote(src.at[:, 1], buf.at[mine, 0], sem, 1, near(0, 1))
            self.up = remote(src.at[:, 0], buf.at[mine, 3], sem, 2, near(0, -1))
            if direct:
                self.top = remote(src.at[:, 1], buf.at[theirs, 0], sem, 3, near(way, 1))
                self.low = remote(src.at[:, 0], buf.at[theirs, 3], sem, 4, near(way, -1))
                self.gives_top, self.gives_low = self.gives & lower, self.gives & upper
            else:
                self.top = remote(buf.at[mine, 0], buf.at[theirs, 0], sem, 3, near(way, 0))
                self.low = remote(buf.at[mine, 3], buf.at[theirs, 3], sem, 4, near(way, 0))
                self.gives_top, self.gives_low = self.gives & upper, self.gives & lower

        def rims(self):
            pl.when(lower)(self.down.start)
            pl.when(upper)(self.up.start)

        def ahead(self):
            pl.when(self.gives)(self.full.start)

        def corners(self):
            pl.when(self.gives_top)(self.top.start)
            pl.when(self.gives_low)(self.low.start)

        def wait_rims(self):
            pl.when(upper)(self.down.wait_recv)
            pl.when(lower)(self.up.wait_recv)

        def wait_ahead(self):
            pl.when(self.takes)(self.full.wait_recv)

        def wait_corners(self):
            pl.when(self.takes & upper)(self.top.wait_recv)
            pl.when(self.takes & lower)(self.low.wait_recv)

        def sent(self):
            pl.when(lower)(self.down.wait_send)
            pl.when(upper)(self.up.wait_send)
            pl.when(self.gives)(self.full.wait_send)
            pl.when(self.gives_top)(self.top.wait_send)
            pl.when(self.gives_low)(self.low.wait_send)

    class Shifts:
        def __init__(self, src, buf, dst, way, chan):
            self.own = 2 if way > 0 else 0
            self.src, self.buf, self.dst, self.chan = src, buf, dst, chan

        def make(self, frames, rows_of):
            chan, dst = self.chan, self.dst
            cell = lax.broadcasted_iota(jnp.int32, (W, chan), 0)
            first = self.own if frames == "own" else 2 - self.own
            for f in (first, first + 1):
                for r in rows_of:
                    if frames == "own" and 1 <= r <= 2:
                        v = self.src[f - self.own, r - 1]
                    else:
                        v = self.buf[f, r]
                    v = v.astype(F32)
                    dst[f, r, :, chan : 2 * chan] = v.astype(BF16)
                    left = jnp.where(cell == 0, 0.0, pltpu.roll(v, 1, 0))
                    right = jnp.where(cell == W - 1, 0.0, pltpu.roll(v, W - 1, 0))
                    dst[f, r, :, 0:chan] = left.astype(BF16)
                    dst[f, r, :, 2 * chan : 3 * chan] = right.astype(BF16)

    CENTRE, EDGE, PAST, CORNERS = (
        [(2, 1)], [(2, 0), (2, 2)], [(0, 1), (1, 1)], [(0, 0), (0, 2), (1, 0), (1, 2)],
    )

    def conv(acc, src, weight, chan, taps):
        for kt, kr in taps:
            at = (3 * kt + kr) * 3 * chan
            piece = src[kt : kt + 2, kr : kr + 2].reshape(CELLS, 3 * chan)
            term = dot(piece, weight[at : at + 3 * chan])
            acc = term if acc is None else acc + term
        return acc

    def back(acc, src, weight, chan, taps):
        for kt, kr in taps:
            for kc in range(3):
                at = (9 * kt + 3 * kr + kc) * chan
                piece = src[2 - kt : 4 - kt, 2 - kr : 4 - kr, :, (2 - kc) * chan : (3 - kc) * chan]
                term = dot(piece.reshape(CELLS, chan), weight[at : at + chan], 1, 1)
                acc = term if acc is None else acc + term
        return acc

    halo_c = Halo(cot, cbuf, -1, sem_c, True)
    halo_v = Halo(video, vbuf, 1, sem_v, True)
    shift_c = Shifts(cot, cbuf, us, -1, CB)
    shift_v = Shifts(video, vbuf, xs, 1, CA)

    loads[0].wait()
    loads[1].wait()
    shift_c.make("own", (1, 2))
    shift_v.make("own", (1, 2))
    loads[2].wait()
    loads[3].wait()
    back_b = back(None, us, kb, CB, CENTRE)
    loads[4].wait()
    pre = conv(None, xs, ka, CA, CENTRE)

    pl.semaphore_wait(barrier, len(peers))
    halo_c.rims()
    halo_v.rims()
    halo_c.corners()
    halo_v.corners()
    halo_c.ahead()
    halo_v.ahead()
    halo_c.wait_rims()
    shift_c.make("own", (0, 3))
    back_b = back(back_b, us, kb, CB, EDGE)
    halo_v.wait_rims()
    shift_v.make("own", (0, 3))
    pre = conv(pre, xs, ka, CA, EDGE)
    halo_c.wait_ahead()
    shift_c.make("other", (1, 2))
    back_b = back(back_b, us, kb, CB, PAST)
    halo_v.wait_ahead()
    shift_v.make("other", (1, 2))
    pre = conv(pre, xs, ka, CA, PAST)
    halo_c.wait_corners()
    shift_c.make("other", (0, 3))
    back_b = back(back_b, us, kb, CB, CORNERS)
    grad_mid = cot[...].reshape(CELLS, CB).astype(F32) + back_b
    mid_t = grad_mid.T
    for c in range(2):
        pick = [mid_t[16 * j + 8 * c : 16 * j + 8 * c + 8] for j in range(8)]
        qt[c] = jnp.concatenate(pick, 0).astype(BF16)
    grad_h = dot(grad_mid.astype(BF16), project[...], 1, 1)

    halo_v.wait_corners()
    shift_v.make("other", (0, 3))
    pre = conv(pre, xs, ka, CA, CORNERS)
    sig = jax.nn.sigmoid(pre)
    hidden = (pre * sig).astype(BF16)
    mid = dot(hidden, project[...])
    mown[...] = mid.astype(BF16).reshape(2, 2, W, CB)
    halo_m = Halo(mown, mbuf, 1, sem_m, False)
    halo_m.rims()
    halo_m.ahead()
    grad_pre = grad_h * sig * (1.0 + pre * (1.0 - sig))
    gown[...] = grad_pre.astype(BF16).reshape(2, 2, W, CA)
    halo_g = Halo(gown, gbuf, -1, sem_g, False)
    halo_g.rims()
    halo_g.ahead()
    out[...] = mid.reshape(2, 2, W, CB)
    grad_t = grad_pre.T
    for c in range(2):
        for j in range(8):
            gt[c, j] = grad_t[32 * j + 16 * c : 32 * j + 16 * c + 16].astype(BF16)

    def chunk_a(left, k):
        kt, kr = k // 3, k % 3
        return dot(left, xs[kt : kt + 2, kr : kr + 2].reshape(CELLS, 3 * CA))

    copies_a = []
    theirs = gt[1 - core].reshape(128, CELLS)
    for k in range(9):
        send_a[k] = chunk_a(theirs, k).astype(BF16).reshape(8, 16, 768)
        cp = remote(send_a.at[k], recv_a.at[k], sem_a, k, partner)
        cp.start()
        copies_a.append(cp)

    class Group:
        def __init__(self, s0x, r1x, s1x, r2y, sem1x, sem2y, s0y, r1y, s1y, r2x, sem1y, sem2x):
            self.s0x, self.r1x, self.s1x, self.r2y, self.sem1x, self.sem2y = s0x, r1x, s1x, r2y, sem1x, sem2y
            self.s0y, self.r1y, self.s1y, self.r2x, self.sem1y, self.sem2x = s0y, r1y, s1y, r2x, sem1y, sem2x

        def x1(self, d, yl):
            src = self.s0x.at[lax.rem(x + d, 4), yl]
            return remote(src, self.r1x.at[d - 1, yl], self.sem1x, 2 * (d - 1) + yl, x_peer(d))

        def y1(self, d):
            return remote(self.s0y.at[lax.rem(y + d, 4)], self.r1y.at[d - 1], self.sem1y, d - 1, y_peer(d))

        def y2(self, d):
            return remote(self.s1x.at[lax.rem(y + d, 4)], self.r2y.at[d - 1], self.sem2y, d - 1, y_peer(d))

        def x2(self, d):
            return remote(self.s1y.at[lax.rem(x + d, 4)], self.r2x.at[d - 1], self.sem2x, d - 1, x_peer(d))

        def send_x(self, yl):
            for d in (2, 1, 3):
                self.x1(d, yl).start()

        def send_y(self, yl):
            for yh in range(2):
                d = lax.rem(2 * yh + yl - y + 4, 4)

                @pl.when(d > 0)
                def _():
                    self.y1(d).start()

        def add_x(self, yl):
            for d in (1, 2, 3):
                self.x1(d, yl).wait()
            for yh in range(2):
                to = 2 * yh + yl
                acc = self.s0x[x, yl, yh].astype(F32)
                for s in range(3):
                    acc = acc + self.r1x[s, yl, yh].astype(F32)
                self.s1x[to] = acc.astype(BF16)
                d = lax.rem(to - y + 4, 4)

                @pl.when(d > 0)
                def _():
                    self.y2(d).start()

        def add_y(self):
            for d in (1, 2, 3):
                self.y1(d).wait()
            for d in ORDER:
                to = lax.rem(x + d, 4)
                acc = self.s0y[y, to].astype(F32)
                for s in range(3):
                    acc = acc + self.r1y[s, to].astype(F32)
                self.s1y[to] = acc.astype(BF16)
                if d:
                    self.x2(d).start()

        def finish(self, t_ref, lx):
            for d in (1, 2, 3):
                self.y2(d).wait()
            acc = self.s1x[y].astype(F32)
            for s in range(3):
                acc = acc + self.r2y[s].astype(F32)
            t_ref[:, :lx] = acc
            for d in (1, 2, 3):
                self.x2(d).wait()
            acc = self.s1y[x].astype(F32)
            for s in range(3):
                acc = acc + self.r2x[s].astype(F32)
            t_ref[:, lx:] = acc

    group_a = Group(s0xa, r1xa, s1xa, r2ya, sem1xa, sem2ya, s0ya, r1ya, s1ya, r2xa, sem1ya, sem2xa)

    mine = gt[core].reshape(128, CELLS)
    cuts = sorted({768 * k for k in range(10)} | {0, XA, HALF_A, HALF_A + XA, 2 * HALF_A})
    for k in range(9):
        value = chunk_a(mine, k)
        copies_a[k].wait()
        value = (value + recv_a[k].reshape(128, 768).astype(F32)).astype(BF16)
        inside = [c for c in cuts if 768 * k <= c <= 768 * k + 768]
        for lo, hi in zip(inside[:-1], inside[1:]):
            yl, at = lo // HALF_A, lo % HALF_A
            for j in range(8):
                cut = value[16 * j : 16 * j + 16, lo - 768 * k : hi - 768 * k]
                if at < XA:
                    s0xa[j % 4, yl, j // 4, :, at : at + hi - lo] = cut
                else:
                    s0ya[(j // 4) * 2 + yl, j % 4, :, at - XA : at - XA + hi - lo] = cut
            if hi % HALF_A == XA:
                group_a.send_x(yl)
            if hi % HALF_A == 0:
                group_a.send_y(yl)

    mid_own = mid.T.astype(BF16)
    for k in range(9):
        kt, kr = k // 3, k % 3
        value = dot(mid_own, us[2 - kt : 4 - kt, 2 - kr : 4 - kr].reshape(CELLS, 3 * CB))
        for kc in range(3):
            tap = value[:, (2 - kc) * CB : (3 - kc) * CB].T
            at = (3 * k + kc) * CB
            for c in range(2):
                for j in range(8):
                    part[c, j, :, at : at + CB] = tap[16 * j + 8 * c : 16 * j + 8 * c + 8]

    def packed(half):
        proj = dot(qt[half], hidden)
        for j in range(8):
            for yl in range(2):
                for z in range(8):
                    both = []
                    for c in range(2):
                        at, to = 1728 * yl + 216 * z + 108 * c, 128 * yl + 16 * z + 8 * c
                        tail = proj[8 * j : 8 * j + 8, to : to + 8]
                        both.append(jnp.concatenate([part[half, j, :, at : at + 108], tail, jnp.zeros((8, 12), F32)], 1))
                    yield z, j, yl, jnp.concatenate(both, 0)

    for z, j, yl, value in packed(1 - core):
        send_b[z, j, yl] = value.astype(BF16)
    copy_b = remote(send_b, recv_b, sem_b, 0, partner)
    copy_b.start()
    halo_m.wait_rims()
    halo_m.corners()
    halo_g.wait_rims()
    halo_g.corners()
    copy_b.wait()
    for z, j, yl, value in packed(core):
        s0b[z, j, yl] = (value + recv_b[z, j, yl].astype(F32)).astype(BF16)
    me_z = b // 2
    first_b = [
        remote(s0b.at[lax.rem(me_z + d, 8)], r1b.at[d - 1], sem1b, d - 1, same_core(d)) for d in range(1, 8)
    ]
    for d in (4, 3, 5, 2, 6, 1, 7):
        first_b[d - 1].start()

    every = CENTRE + EDGE + PAST + CORNERS
    shift_m = Shifts(mown, mbuf, ms, 1, CB)
    shift_m.make("own", (0, 1, 2, 3))
    halo_m.wait_ahead()
    halo_m.wait_corners()
    shift_m.make("other", (0, 1, 2, 3))
    out[...] = out[...] + conv(None, ms, kb, CB, every).reshape(2, 2, W, CB)
    done = [pltpu.make_async_copy(out, out_hbm, sem_o.at[0]), pltpu.make_async_copy(grad_video, grad_video_hbm, sem_o.at[1])]
    done[0].start()
    shift_g = Shifts(gown, gbuf, gs, -1, CA)
    shift_g.make("own", (0, 1, 2, 3))
    halo_g.wait_ahead()
    halo_g.wait_corners()
    shift_g.make("other", (0, 1, 2, 3))
    grad_video[...] = back(None, gs, ka, CA, every).reshape(2, 2, W, CA)

    done[1].start()

    group_a.add_x(0)
    group_a.add_x(1)
    group_a.add_y()
    for cp in first_b:
        cp.wait()
    for j in range(8):
        acc = s0b[me_z, j].astype(F32)
        for s in range(7):
            acc = acc + r1b[s, j].astype(F32)
        s1b[j // 4, j % 4] = acc.astype(BF16)
    second_b = []
    for dx in range(4):
        for dy in range(4):
            if dx or dy:
                to = lax.rem(y + dy, 4)
                src = s1b.at[to // 2, lax.rem(x + dx, 4), lax.rem(to, 2)]
                slot = 4 * dx + dy - 1
                cp = remote(src, r2b.at[slot], sem2b, slot, plane(dx, dy))
                cp.start()
                second_b.append(cp)
    group_a.finish(t_a, XA)
    for k in range(16):
        high = jnp.concatenate([t_a[:, 216 * k : 216 * k + 216], jnp.zeros((16, 40), F32)], 1)
        msg[k] = high.astype(BF16)
    last = []
    for d in range(1, 16):
        cp = remote(msg.at[lax.rem(b + d, 16)], r3.at[d - 1], sem3, d - 1, z_peer(d))
        cp.start()
        last.append(cp)
    for cp in second_b:
        cp.wait()
    acc = s1b[y // 2, x, lax.rem(y, 2)].astype(F32)
    for s in range(15):
        acc = acc + r2b[s].astype(F32)
    scale = 1.0 / (64 * 16 * W) ** 0.5
    tb[...] = (acc * scale).reshape(2, 8, 128)
    swap = remote(tb.at[1 - core], gb.at[core], sem3b, 0, partner)
    swap.start()
    for cp in last:
        cp.wait()
    same = msg[b].astype(F32)
    for d in range(2, 16, 2):
        same = same + r3[d - 1].astype(F32)
    other = r3[0].astype(F32)
    for d in range(3, 16, 2):
        other = other + r3[d - 1].astype(F32)
    total[core] = same * scale
    total[1 - core] = other * scale
    grad_a[...] = total[:, :, 0:216].reshape(32, 216)
    swap.wait()
    gb[core] = tb[core]
    low = gb[...].reshape(16, 128)
    grad_b[...] = low[:, 0:108]
    grad_p[...] = low.T[108:116]
    for halo in (halo_c, halo_v, halo_m, halo_g):
        halo.sent()
    for cp in done:
        cp.wait()


def written(*refs):
    took, gives, held, sem = refs[:5], refs[5:10], refs[10:15], refs[15]
    reads = [pltpu.make_async_copy(took[i], held[i], sem.at[0, i]) for i in range(5)]
    writes = [pltpu.make_async_copy(held[i], gives[i], sem.at[1, i]) for i in range(5)]
    for cp in reads:
        cp.start()
    for i in range(5):
        reads[i].wait()
        writes[i].start()
    for cp in writes:
        cp.wait()


def shards(video, kernel_a, project, kernel_b, cotangent):
    dma = pltpu.SemaphoreType.DMA
    vmem = pl.BlockSpec(memory_space=pltpu.VMEM)
    hbm = pl.BlockSpec(memory_space=pl.ANY)

    def group(lx, ly):
        return [
            pltpu.VMEM((4, 2, 2, 16, lx), BF16), pltpu.VMEM((4, 4, 16, ly), BF16),
            pltpu.VMEM((3, 2, 2, 16, lx), BF16), pltpu.VMEM((3, 4, 16, ly), BF16),
            pltpu.VMEM((4, 16, lx), BF16), pltpu.VMEM((4, 16, ly), BF16),
            pltpu.VMEM((3, 16, lx), BF16), pltpu.VMEM((3, 16, ly), BF16),
        ]

    results = pl.pallas_call(
        kernel,
        out_shape=[
            jax.ShapeDtypeStruct((2, 2, W, CB), F32),
            jax.ShapeDtypeStruct((2, 2, W, CA), F32),
            jax.ShapeDtypeStruct((32, 216), F32),
            jax.ShapeDtypeStruct((16, 108), F32),
            jax.ShapeDtypeStruct((8, 16), F32),
        ],
        in_specs=[hbm] * 5,
        out_specs=[hbm, hbm, vmem, vmem, vmem],
        scratch_shapes=[
            pltpu.VMEM((2, 2, W, CB), F32), pltpu.VMEM((2, 2, W, CA), F32),
            pltpu.VMEM((2, 2, W, CA), BF16), pltpu.VMEM((2, 2, W, CB), BF16), pltpu.VMEM((CA, CB), BF16),
            pltpu.VMEM((27 * CA, CA), BF16), pltpu.VMEM((27 * CB, CB), BF16),
            pltpu.VMEM((4, 4, W, CA), BF16), pltpu.VMEM((4, 4, W, CB), BF16),
            pltpu.VMEM((4, 4, W, CB), BF16), pltpu.VMEM((4, 4, W, CA), BF16),
            pltpu.VMEM((2, 2, W, CB), BF16), pltpu.VMEM((2, 2, W, CA), BF16),
            pltpu.VMEM((4, 4, W, 3 * CA), BF16), pltpu.VMEM((4, 4, W, 3 * CB), BF16),
            pltpu.VMEM((4, 4, W, 3 * CB), BF16), pltpu.VMEM((4, 4, W, 3 * CA), BF16),
            pltpu.VMEM((2, 8, 16, CELLS), BF16), pltpu.VMEM((2, 64, CELLS), BF16),
            pltpu.VMEM((9, 8, 16, 768), BF16), pltpu.VMEM((9, 8, 16, 768), BF16),
            pltpu.VMEM((8, 8, 2, 16, 128), BF16), pltpu.VMEM((8, 8, 2, 16, 128), BF16),
            pltpu.VMEM((2, 8, 8, 27 * CB), F32),
            *group(XA, YA),
            pltpu.VMEM((8, 8, 2, 16, 128), BF16), pltpu.VMEM((7, 8, 2, 16, 128), BF16),
            pltpu.VMEM((2, 4, 2, 16, 128), BF16), pltpu.VMEM((15, 16, 128), BF16),
            pltpu.VMEM((2, 8, 128), F32), pltpu.VMEM((2, 8, 128), F32),
            pltpu.VMEM((16, HALF_A), F32),
            pltpu.VMEM((16, 16, 256), BF16), pltpu.VMEM((15, 16, 256), BF16),
            pltpu.VMEM((2, 16, 256), F32),
            dma((5,)), dma((2, 5)), dma((2, 5)), dma((2, 5)), dma((2, 5)), dma((2, 9)), dma((2, 1)),
            *[dma((2, n)) for n in (6, 3, 3, 3, 15, 7, 15, 1)],
            dma((2,)),
        ],
        compiler_params=pltpu.CompilerParams(
            collective_id=0, has_side_effects=True, vmem_limit_bytes=56 * 1024 * 1024
        ),
    )(video, cotangent, kernel_a, project, kernel_b)
    results = pl.pallas_call(
        written,
        out_shape=[jax.ShapeDtypeStruct(r.shape, F32) for r in results],
        in_specs=[hbm] * 5,
        out_specs=[hbm] * 5,
        scratch_shapes=[*[pltpu.VMEM(r.shape, F32) for r in results], dma((2, 5))],
    )(*results)
    return results[0], results[1], results[2].T, results[3].T, results[4]


def solution(mesh):
    cells = P("tm", "rows", None, None)
    return jax.shard_map(
        shards,
        mesh=mesh,
        in_specs=(cells, P(), P(), P(), cells),
        out_specs=(cells, cells, P("tm", "rows"), P("tm", "rows"), P("tm", "rows")),
        check_vma=False,
    )
```

```python
import jax
import jax.numpy as jnp
from jax import lax
from jax.experimental import pallas as pl
from jax.experimental.pallas import tpu as pltpu
from jax.sharding import PartitionSpec as P

F32, BF16 = jnp.float32, jnp.bfloat16
MESH = pl.DeviceIdType.MESH
CA, CB, W = 256, 128, 96
CELLS = 4 * W
HALF_A = 27 * CA // 2
XA, YA = 1664, HALF_A - 1664
XB, YB = 512, 512
PB = 896
LAG = 3
ORDER = (1, 2, 3, 0)


def dot(a, b, ca=1, cb=0):
    return lax.dot_general(a, b, (((ca,), (cb,)), ((), ())), preferred_element_type=F32)


def kernel(
    video_hbm, cot_hbm, ka_hbm, project_hbm, kb_hbm,
    out_hbm, grad_video_hbm, grad_a, grad_b, grad_p,
    out, grad_video, video, cot, project, ka, kb, vbuf, cbuf, mbuf, gbuf, mown, gown, xs, us, ms, gs,
    gt, qt, send_a, recv_a, own_a, send_b, recv_b, part,
    s0xa, s0ya, q1xa, q1ya, r1xa, r1ya, s1xa, s1ya, r2ya, r2xa,
    s0xb, s0yb, q1xb, q1yb, r1xb, r1yb, s1xb, s1yb, r2yb, r2xb,
    t_a, t_b, msg, r3, total,
    sem_w, sem_v, sem_c, sem_m, sem_g, sem_a, sem_b,
    sem1xa, sem1ya, sem2ya, sem2xa, sem1xb, sem1yb, sem2yb, sem2xb, sem3, sem_o,
):
    tm = lax.axis_index("tm")
    rows = lax.axis_index("rows")
    core = lax.rem(tm, 2)
    b = lax.rem(tm, 16)
    y_lo = tm // 16
    x = lax.rem(rows, 4)
    y = (rows // 4) * 2 + y_lo
    upper, lower = rows > 0, rows < 7
    since, until = tm > 0, tm < 31

    def x_peer(d):
        return (tm, (rows // 4) * 4 + lax.rem(x + d, 4))

    def y_peer(d):
        to = lax.rem(y + d, 4)
        return (lax.rem(to, 2) * 16 + b, (to // 2) * 4 + x)

    def z_peer(d):
        return (y_lo * 16 + lax.rem(b + d, 16), rows)

    def near(dt, dr):
        return (lax.rem(tm + 32 + dt, 32), lax.rem(rows + 8 + dr, 8))

    partner = (tm + 1 - 2 * core, rows)

    def remote(src, dst, sem, slot, to):
        return pltpu.make_async_remote_copy(
            src_ref=src, dst_ref=dst, send_sem=sem.at[0, slot], recv_sem=sem.at[1, slot],
            device_id=to, device_id_type=MESH,
        )

    barrier = pltpu.get_barrier_semaphore()
    peers = [near(dt, dr) for dt, dr in ((0, 1), (0, -1), (1, 0), (-1, 0))]
    peers += [x_peer(d) for d in range(1, 4)] + [y_peer(d) for d in range(1, 4)]
    peers += [z_peer(d) for d in range(1, 16)]
    for to in peers:
        pl.semaphore_signal(barrier, inc=1, device_id=to, device_id_type=MESH)

    loads = [
        pltpu.make_async_copy(src, dst, sem_w.at[i])
        for i, (src, dst) in enumerate(
            ((cot_hbm, cot), (video_hbm, video), (kb_hbm, kb), (project_hbm, project), (ka_hbm, ka))
        )
    ]
    for cp in loads:
        cp.start()

    for buf, chan in ((vbuf, CA), (cbuf, CB), (mbuf, CB), (gbuf, CA)):

        @pl.when(rows == 0)
        def _():
            buf[:, 0] = jnp.zeros((4, W, chan), BF16)

        @pl.when(rows == 7)
        def _():
            buf[:, 3] = jnp.zeros((4, W, chan), BF16)

    @pl.when(tm == 0)
    def _():
        vbuf[0:2] = jnp.zeros((2, 4, W, CA), BF16)
        mbuf[0:2] = jnp.zeros((2, 4, W, CB), BF16)

    @pl.when(tm == 31)
    def _():
        cbuf[2:4] = jnp.zeros((2, 4, W, CB), BF16)
        gbuf[2:4] = jnp.zeros((2, 4, W, CA), BF16)

    class Halo:
        def __init__(self, src, buf, way, sem):
            own = 2 if way > 0 else 0
            mine, theirs = pl.ds(own, 2), pl.ds(2 - own, 2)
            self.gives, self.takes = (until, since) if way > 0 else (since, until)
            self.full = remote(src, buf.at[theirs, pl.ds(1, 2)], sem, 0, near(way, 0))
            self.down = remote(src.at[:, 1], buf.at[mine, 0], sem, 1, near(0, 1))
            self.up = remote(src.at[:, 0], buf.at[mine, 3], sem, 2, near(0, -1))
            self.top = remote(buf.at[mine, 0], buf.at[theirs, 0], sem, 3, near(way, 0))
            self.low = remote(buf.at[mine, 3], buf.at[theirs, 3], sem, 4, near(way, 0))
            self.gives_top, self.gives_low = self.gives & upper, self.gives & lower

        def rims(self):
            pl.when(lower)(self.down.start)
            pl.when(upper)(self.up.start)

        def ahead(self):
            pl.when(self.gives)(self.full.start)

        def corners(self):
            pl.when(self.gives_top)(self.top.start)
            pl.when(self.gives_low)(self.low.start)

        def wait_rims(self):
            pl.when(upper)(self.down.wait_recv)
            pl.when(lower)(self.up.wait_recv)

        def wait_ahead(self):
            pl.when(self.takes)(self.full.wait_recv)

        def wait_corners(self):
            pl.when(self.takes & upper)(self.top.wait_recv)
            pl.when(self.takes & lower)(self.low.wait_recv)

        def sent(self):
            pl.when(lower)(self.down.wait_send)
            pl.when(upper)(self.up.wait_send)
            pl.when(self.gives)(self.full.wait_send)
            pl.when(self.gives_top)(self.top.wait_send)
            pl.when(self.gives_low)(self.low.wait_send)

    class Shifts:
        def __init__(self, src, buf, dst, way, chan):
            self.own = 2 if way > 0 else 0
            self.src, self.buf, self.dst, self.chan = src, buf, dst, chan

        def make(self, frames, rows_of):
            chan, dst = self.chan, self.dst
            cell = lax.broadcasted_iota(jnp.int32, (W, chan), 0)
            first = self.own if frames == "own" else 2 - self.own
            for f in (first, first + 1):
                for r in rows_of:
                    if frames == "own" and 1 <= r <= 2:
                        v = self.src[f - self.own, r - 1]
                    else:
                        v = self.buf[f, r]
                    v = v.astype(F32)
                    dst[f, r, :, chan : 2 * chan] = v.astype(BF16)
                    left = jnp.where(cell == 0, 0.0, pltpu.roll(v, 1, 0))
                    right = jnp.where(cell == W - 1, 0.0, pltpu.roll(v, W - 1, 0))
                    dst[f, r, :, 0:chan] = left.astype(BF16)
                    dst[f, r, :, 2 * chan : 3 * chan] = right.astype(BF16)

    CENTRE, EDGE, PAST, CORNERS = (
        [(2, 1)], [(2, 0), (2, 2)], [(0, 1), (1, 1)], [(0, 0), (0, 2), (1, 0), (1, 2)],
    )

    def conv(acc, src, weight, chan, taps):
        for kt, kr in taps:
            at = (3 * kt + kr) * 3 * chan
            piece = src[kt : kt + 2, kr : kr + 2].reshape(CELLS, 3 * chan)
            term = dot(piece, weight[at : at + 3 * chan])
            acc = term if acc is None else acc + term
        return acc

    def back(acc, src, weight, chan, taps):
        for kt, kr in taps:
            for kc in range(3):
                at = (9 * kt + 3 * kr + kc) * chan
                piece = src[2 - kt : 4 - kt, 2 - kr : 4 - kr, :, (2 - kc) * chan : (3 - kc) * chan]
                term = dot(piece.reshape(CELLS, chan), weight[at : at + chan], 1, 1)
                acc = term if acc is None else acc + term
        return acc

    halo_c = Halo(cot, cbuf, -1, sem_c)
    halo_v = Halo(video, vbuf, 1, sem_v)
    shift_c = Shifts(cot, cbuf, us, -1, CB)
    shift_v = Shifts(video, vbuf, xs, 1, CA)

    loads[0].wait()
    loads[1].wait()
    shift_c.make("own", (1, 2))
    shift_v.make("own", (1, 2))
    loads[2].wait()
    loads[3].wait()
    back_b = back(None, us, kb, CB, CENTRE)
    loads[4].wait()
    pre = conv(None, xs, ka, CA, CENTRE)

    pl.semaphore_wait(barrier, len(peers))
    halo_c.rims()
    halo_v.rims()
    halo_c.ahead()
    halo_v.ahead()
    halo_c.wait_rims()
    halo_c.corners()
    halo_v.wait_rims()
    halo_v.corners()
    shift_c.make("own", (0, 3))
    back_b = back(back_b, us, kb, CB, EDGE)
    shift_v.make("own", (0, 3))
    pre = conv(pre, xs, ka, CA, EDGE)
    halo_c.wait_ahead()
    shift_c.make("other", (1, 2))
    back_b = back(back_b, us, kb, CB, PAST)
    halo_v.wait_ahead()
    shift_v.make("other", (1, 2))
    pre = conv(pre, xs, ka, CA, PAST)
    halo_c.wait_corners()
    shift_c.make("other", (0, 3))
    back_b = back(back_b, us, kb, CB, CORNERS)
    grad_mid = cot[...].reshape(CELLS, CB).astype(F32) + back_b
    mid_t = grad_mid.T
    for c in range(2):
        pick = [mid_t[16 * j + 8 * c : 16 * j + 8 * c + 8] for j in range(8)]
        qt[c] = jnp.concatenate(pick, 0).astype(BF16)
    grad_h = dot(grad_mid.astype(BF16), project[...], 1, 1)

    halo_v.wait_corners()
    shift_v.make("other", (0, 3))
    pre = conv(pre, xs, ka, CA, CORNERS)
    sig = jax.nn.sigmoid(pre)
    hidden = (pre * sig).astype(BF16)
    mid = dot(hidden, project[...])
    mown[...] = mid.astype(BF16).reshape(2, 2, W, CB)
    halo_m = Halo(mown, mbuf, 1, sem_m)
    halo_m.rims()
    halo_m.ahead()
    grad_pre = grad_h * sig * (1.0 + pre * (1.0 - sig))
    gown[...] = grad_pre.astype(BF16).reshape(2, 2, W, CA)
    halo_g = Halo(gown, gbuf, -1, sem_g)
    halo_g.rims()
    halo_g.ahead()
    out[...] = mid.reshape(2, 2, W, CB)
    grad_t = grad_pre.T
    for c in range(2):
        for j in range(8):
            gt[c, j] = grad_t[32 * j + 16 * c : 32 * j + 16 * c + 16].astype(BF16)

    def chunk_a(left, k):
        kt, kr = k // 3, k % 3
        return dot(left, xs[kt : kt + 2, kr : kr + 2].reshape(CELLS, 3 * CA))

    class Group:
        def __init__(self, s0x, q1x, r1x, s1x, r2y, s0y, q1y, r1y, s1y, r2x, sem1x, sem1y, sem2y, sem2x):
            self.s0x, self.q1x, self.r1x, self.s1x, self.r2y = s0x, q1x, r1x, s1x, r2y
            self.s0y, self.q1y, self.r1y, self.s1y, self.r2x = s0y, q1y, r1y, s1y, r2x
            self.sem1x, self.sem1y, self.sem2y, self.sem2x = sem1x, sem1y, sem2y, sem2x

        def x_far(self, yl, h):
            src = self.s0x.at[lax.rem(x + 2, 4), yl, h]
            return remote(src, self.q1x.at[yl, h], self.sem1x, 6 * yl + h, x_peer((1, 3)[h]))

        def x_near(self, yl, side, h):
            d = (1, 3)[side]
            src = self.s0x.at[lax.rem(x + d, 4), yl, h]
            return remote(src, self.r1x.at[side, yl, h], self.sem1x, 6 * yl + 2 + 2 * side + h, x_peer(d))

        def y_far(self, h):
            src = self.s0y.at[lax.rem(y + 2, 4), pl.ds(2 * h, 2)]
            return remote(src, self.q1y.at[h], self.sem1y, h, y_peer((1, 3)[h]))

        def y_near(self, side, h):
            d = (1, 3)[side]
            src = self.s0y.at[lax.rem(y + d, 4), pl.ds(2 * h, 2)]
            return remote(src, self.r1y.at[side, pl.ds(2 * h, 2)], self.sem1y, 2 + 2 * side + h, y_peer(d))

        def y2(self, d):
            return remote(self.s1x.at[lax.rem(y + d, 4)], self.r2y.at[d - 1], self.sem2y, d - 1, y_peer(d))

        def x2(self, d):
            return remote(self.s1y.at[lax.rem(x + d, 4)], self.r2x.at[d - 1], self.sem2x, d - 1, x_peer(d))

        def send_x(self, yl):
            self.x_far(yl, 0).start()
            self.x_far(yl, 1).start()
            self.x_near(yl, 0, 1).start()
            self.x_near(yl, 1, 0).start()

        def send_y(self):
            self.y_far(0).start()
            self.y_far(1).start()
            self.y_near(0, 1).start()
            self.y_near(1, 0).start()

        def relay_x(self, yl):
            for h in range(2):
                to = lax.rem(x + (1, 3)[h], 4)
                self.x_far(yl, h).wait_recv()
                both = self.s0x[to, yl, h].astype(F32) + self.q1x[yl, h].astype(F32)
                self.s0x[to, yl, h] = both.astype(BF16)
                self.x_near(yl, h, h).start()

        def relay_y(self):
            for h in range(2):
                to, part = lax.rem(y + (1, 3)[h], 4), slice(2 * h, 2 * h + 2)
                self.y_far(h).wait_recv()
                both = self.s0y[to, part].astype(F32) + self.q1y[h].astype(F32)
                self.s0y[to, part] = both.astype(BF16)
                self.y_near(h, h).start()

        def add_x(self, yl):
            for h in range(2):
                self.x_far(yl, h).wait_send()
                for side in range(2):
                    self.x_near(yl, side, h).wait()
            for yh in range(2):
                to = 2 * yh + yl
                acc = self.s0x[x, yl, yh].astype(F32)
                for side in range(2):
                    acc = acc + self.r1x[side, yl, yh].astype(F32)
                self.s1x[to] = acc.astype(BF16)
                d = lax.rem(to - y + 4, 4)

                @pl.when(d > 0)
                def _():
                    self.y2(d).start()

        def add_y(self):
            for h in range(2):
                self.y_far(h).wait_send()
                for side in range(2):
                    self.y_near(side, h).wait()
            for d in ORDER:
                to = lax.rem(x + d, 4)
                acc = self.s0y[y, to].astype(F32)
                for side in range(2):
                    acc = acc + self.r1y[side, to].astype(F32)
                self.s1y[to] = acc.astype(BF16)
                if d:
                    self.x2(d).start()

        def finish(self, t_ref, lx):
            for d in (1, 2, 3):
                self.y2(d).wait()
            acc = self.s1x[y].astype(F32)
            for s in range(3):
                acc = acc + self.r2y[s].astype(F32)
            t_ref[:, :lx] = acc
            for d in (1, 2, 3):
                self.x2(d).wait()
            acc = self.s1y[x].astype(F32)
            for s in range(3):
                acc = acc + self.r2x[s].astype(F32)
            t_ref[:, lx:] = acc

    group_a = Group(s0xa, q1xa, r1xa, s1xa, r2ya, s0ya, q1ya, r1ya, s1ya, r2xa, sem1xa, sem1ya, sem2ya, sem2xa)
    group_b = Group(s0xb, q1xb, r1xb, s1xb, r2yb, s0yb, q1yb, r1yb, s1yb, r2xb, sem1xb, sem1yb, sem2yb, sem2xb)

    left = jnp.concatenate([gt[1 - core].reshape(128, CELLS), gt[core].reshape(128, CELLS)], 0)
    cuts = sorted({768 * k for k in range(10)} | {0, XA, HALF_A, HALF_A + XA, 2 * HALF_A})
    copies_a = []
    for step in range(9 + LAG):
        if step < 9:
            value = chunk_a(left, step)
            send_a[step] = value[0:128].astype(BF16).reshape(8, 16, 768)
            cp = remote(send_a.at[step], recv_a.at[step], sem_a, step, partner)
            cp.start()
            copies_a.append(cp)
            own_a[step] = value[128:256]
        k = step - LAG
        if k < 0:
            continue
        copies_a[k].wait()
        value = (own_a[k] + recv_a[k].reshape(128, 768).astype(F32)).astype(BF16)
        inside = [c for c in cuts if 768 * k <= c <= 768 * k + 768]
        for lo, hi in zip(inside[:-1], inside[1:]):
            yl, at = lo // HALF_A, lo % HALF_A
            for j in range(8):
                cut = value[16 * j : 16 * j + 16, lo - 768 * k : hi - 768 * k]
                if at < XA:
                    s0xa[j % 4, yl, j // 4, :, at : at + hi - lo] = cut
                else:
                    s0ya[(j // 4) * 2 + yl, j % 4, :, at - XA : at - XA + hi - lo] = cut
            if hi % HALF_A == XA:
                group_a.send_x(yl)
    group_a.send_y()

    mid_own = mid.T.astype(BF16)
    for k in range(9):
        kt, kr = k // 3, k % 3
        value = dot(mid_own, us[2 - kt : 4 - kt, 2 - kr : 4 - kr].reshape(CELLS, 3 * CB))
        for kc in range(3):
            tap = value[:, (2 - kc) * CB : (3 - kc) * CB].T
            at = (3 * k + kc) * CB
            for c in range(2):
                for j in range(8):
                    part[c, j, :, at : at + CB] = tap[16 * j + 8 * c : 16 * j + 8 * c + 8]

    def packed(half):
        proj = dot(qt[half], hidden)
        for j in range(8):
            for yl in range(2):
                at = 13 * CB * yl
                upper_half = part[half, j, :, at : at + PB]
                lower_half = part[half, j, :, at + PB : at + 2 * PB]
                body = jnp.concatenate([upper_half, lower_half], 0)
                tail = proj[8 * j : 8 * j + 8, 128 * yl : 128 * yl + 128]
                tail = jnp.concatenate([tail, jnp.zeros((8, 128), F32)], 0)
                yield j, yl, jnp.concatenate([body, tail], 1)

    for j, yl, value in packed(1 - core):
        send_b[j, yl] = value.astype(BF16)
    copy_b = remote(send_b, recv_b, sem_b, 0, partner)
    copy_b.start()
    halo_m.wait_rims()
    halo_m.corners()
    halo_g.wait_rims()
    halo_g.corners()
    copy_b.wait()
    for j, yl, value in packed(core):
        value = (value + recv_b[j, yl].astype(F32)).astype(BF16)
        s0xb[j % 4, yl, j // 4] = value[:, :XB]
        s0yb[(j // 4) * 2 + yl, j % 4] = value[:, XB:]
    for yl in range(2):
        group_b.send_x(yl)
    group_b.send_y()
    for yl in range(2):
        group_a.relay_x(yl)
    group_a.relay_y()
    for yl in range(2):
        group_b.relay_x(yl)
    group_b.relay_y()
    group_a.add_x(0)
    every = CENTRE + EDGE + PAST + CORNERS
    shift_m = Shifts(mown, mbuf, ms, 1, CB)
    shift_m.make("own", (0, 1, 2, 3))
    halo_m.wait_ahead()
    halo_m.wait_corners()
    shift_m.make("other", (0, 1, 2, 3))
    out[...] = out[...] + conv(None, ms, kb, CB, every).reshape(2, 2, W, CB)
    done = [
        pltpu.make_async_copy(out, out_hbm, sem_o.at[0]),
        pltpu.make_async_copy(grad_video, grad_video_hbm, sem_o.at[1]),
    ]
    done[0].start()
    group_a.add_x(1)
    group_a.add_y()
    group_b.add_x(0)
    group_b.add_x(1)
    group_b.add_y()
    shift_g = Shifts(gown, gbuf, gs, -1, CA)
    shift_g.make("own", (0, 1, 2, 3))
    halo_g.wait_ahead()
    halo_g.wait_corners()
    shift_g.make("other", (0, 1, 2, 3))
    grad_video[...] = back(None, gs, ka, CA, every).reshape(2, 2, W, CA)
    done[1].start()
    group_a.finish(t_a, XA)
    group_b.finish(t_b, XB)

    part_b = jnp.concatenate([t_b[0:8, 0:PB], t_b[8:16, 0:PB]], 1)
    part_b = jnp.where(y_lo == 0, part_b[:, 0:1728], part_b[:, 64:1792])
    part_p = t_b[0:8, PB : PB + 128]
    for k in range(16):
        high = jnp.concatenate([t_a[:, 216 * k : 216 * k + 216], jnp.zeros((16, 40), F32)], 1)
        low = jnp.concatenate(
            [
                part_b[:, 108 * k : 108 * k + 108], jnp.zeros((8, 4), F32),
                part_p[:, 8 * k : 8 * k + 8], jnp.zeros((8, 8), F32),
            ], 1,
        )
        low = jnp.concatenate([low, jnp.zeros((8, 128), F32)], 0)
        msg[k] = jnp.concatenate([high, low], 1).astype(BF16)
    last = []
    for d in range(1, 16):
        cp = remote(msg.at[lax.rem(b + d, 16)], r3.at[d - 1], sem3, d - 1, z_peer(d))
        cp.start()
        last.append(cp)
    for cp in last:
        cp.wait()
    same = msg[b].astype(F32)
    for d in range(2, 16, 2):
        same = same + r3[d - 1].astype(F32)
    other = r3[0].astype(F32)
    for d in range(3, 16, 2):
        other = other + r3[d - 1].astype(F32)
    scale = 1.0 / (64 * 16 * W) ** 0.5
    total[core] = same * scale
    total[1 - core] = other * scale
    grad_a[...] = total[:, :, 0:216].reshape(32, 216)
    low = jnp.concatenate([total[0, 0:8, 256:384], total[1, 0:8, 256:384]], 0)
    grad_b[...] = low[:, 0:108]
    grad_p[...] = low.T[112:120]
    for halo in (halo_c, halo_v, halo_m, halo_g):
        halo.sent()
    for cp in done:
        cp.wait()


def written(*refs):
    took, gives, held, sem = refs[:5], refs[5:10], refs[10:15], refs[15]
    reads = [pltpu.make_async_copy(took[i], held[i], sem.at[0, i]) for i in range(5)]
    writes = [pltpu.make_async_copy(held[i], gives[i], sem.at[1, i]) for i in range(5)]
    for cp in reads:
        cp.start()
    for i in range(5):
        reads[i].wait()
        writes[i].start()
    for cp in writes:
        cp.wait()


def shards(video, kernel_a, project, kernel_b, cotangent):
    dma = pltpu.SemaphoreType.DMA
    vmem = pl.BlockSpec(memory_space=pltpu.VMEM)
    hbm = pl.BlockSpec(memory_space=pl.ANY)

    def group(lx, ly):
        return [
            pltpu.VMEM((4, 2, 2, 16, lx), BF16), pltpu.VMEM((4, 4, 16, ly), BF16),
            pltpu.VMEM((2, 2, 16, lx), BF16), pltpu.VMEM((2, 2, 16, ly), BF16),
            pltpu.VMEM((2, 2, 2, 16, lx), BF16), pltpu.VMEM((2, 4, 16, ly), BF16),
            pltpu.VMEM((4, 16, lx), BF16), pltpu.VMEM((4, 16, ly), BF16),
            pltpu.VMEM((3, 16, lx), BF16), pltpu.VMEM((3, 16, ly), BF16),
        ]

    results = pl.pallas_call(
        kernel,
        out_shape=[
            jax.ShapeDtypeStruct((2, 2, W, CB), F32),
            jax.ShapeDtypeStruct((2, 2, W, CA), F32),
            jax.ShapeDtypeStruct((32, 216), F32),
            jax.ShapeDtypeStruct((16, 108), F32),
            jax.ShapeDtypeStruct((8, 16), F32),
        ],
        in_specs=[hbm] * 5,
        out_specs=[hbm, hbm, vmem, vmem, vmem],
        scratch_shapes=[
            pltpu.VMEM((2, 2, W, CB), F32), pltpu.VMEM((2, 2, W, CA), F32),
            pltpu.VMEM((2, 2, W, CA), BF16), pltpu.VMEM((2, 2, W, CB), BF16), pltpu.VMEM((CA, CB), BF16),
            pltpu.VMEM((27 * CA, CA), BF16), pltpu.VMEM((27 * CB, CB), BF16),
            pltpu.VMEM((4, 4, W, CA), BF16), pltpu.VMEM((4, 4, W, CB), BF16),
            pltpu.VMEM((4, 4, W, CB), BF16), pltpu.VMEM((4, 4, W, CA), BF16),
            pltpu.VMEM((2, 2, W, CB), BF16), pltpu.VMEM((2, 2, W, CA), BF16),
            pltpu.VMEM((4, 4, W, 3 * CA), BF16), pltpu.VMEM((4, 4, W, 3 * CB), BF16),
            pltpu.VMEM((4, 4, W, 3 * CB), BF16), pltpu.VMEM((4, 4, W, 3 * CA), BF16),
            pltpu.VMEM((2, 8, 16, CELLS), BF16), pltpu.VMEM((2, 64, CELLS), BF16),
            pltpu.VMEM((9, 8, 16, 768), BF16), pltpu.VMEM((9, 8, 16, 768), BF16),
            pltpu.VMEM((9, 128, 768), F32),
            pltpu.VMEM((8, 2, 16, XB + YB), BF16), pltpu.VMEM((8, 2, 16, XB + YB), BF16),
            pltpu.VMEM((2, 8, 8, 27 * CB), F32),
            *group(XA, YA),
            *group(XB, YB),
            pltpu.VMEM((16, HALF_A), F32), pltpu.VMEM((16, XB + YB), F32),
            pltpu.VMEM((16, 16, 384), BF16), pltpu.VMEM((15, 16, 384), BF16),
            pltpu.VMEM((2, 16, 384), F32),
            dma((5,)), dma((2, 5)), dma((2, 5)), dma((2, 5)), dma((2, 5)), dma((2, 9)), dma((2, 1)),
            *[dma((2, n)) for n in (12, 6, 3, 3, 12, 6, 3, 3, 15)],
            dma((2,)),
        ],
        compiler_params=pltpu.CompilerParams(
            collective_id=0, has_side_effects=True, vmem_limit_bytes=56 * 1024 * 1024
        ),
    )(video, cotangent, kernel_a, project, kernel_b)
    results = pl.pallas_call(
        written,
        out_shape=[jax.ShapeDtypeStruct(r.shape, F32) for r in results],
        in_specs=[hbm] * 5,
        out_specs=[hbm] * 5,
        scratch_shapes=[*[pltpu.VMEM(r.shape, F32) for r in results], dma((2, 5))],
    )(*results)
    return results[0], results[1], results[2].T, results[3].T, results[4]


def solution(mesh):
    cells = P("tm", "rows", None, None)
    return jax.shard_map(
        shards,
        mesh=mesh,
        in_specs=(cells, P(), P(), P(), cells),
        out_specs=(cells, cells, P("tm", "rows"), P("tm", "rows"), P("tm", "rows")),
        check_vma=False,
    )
```

```python
import jax
import jax.numpy as jnp
from jax import lax
from jax.experimental import pallas as pl
from jax.experimental.pallas import tpu as pltpu
from jax.sharding import PartitionSpec as P

F32, BF16 = jnp.float32, jnp.bfloat16
MESH = pl.DeviceIdType.MESH
CA, CB, W = 256, 128, 96
CELLS = 4 * W
HALF_A = 27 * CA // 2
XA, YA = 1664, HALF_A - 1664
LAG = 3
ORDER = (1, 2, 3, 0)


def dot(a, b, ca=1, cb=0):
    return lax.dot_general(a, b, (((ca,), (cb,)), ((), ())), preferred_element_type=F32)


def kernel(
    video_hbm, cot_hbm, ka_hbm, project_hbm, kb_hbm,
    out_hbm, grad_video_hbm, grad_a, grad_b, grad_p,
    out, grad_video, video, cot, project, ka, kb, vbuf, cbuf, mbuf, gbuf, mown, gown, xs, us, ms, gs,
    gt, qt, send_a, recv_a, own_a, send_b, recv_b, part,
    s0xa, s0ya, r1xa, r1ya, s1xa, s1ya, r2ya, r2xa,
    s0b, r1b, s1b, r2b, tb, gb,
    t_a, msg, r3, total,
    sem_w, sem_v, sem_c, sem_m, sem_g, sem_a, sem_b,
    sem1xa, sem1ya, sem2ya, sem2xa, sem3, sem1b, sem2b, sem3b, sem_o,
):
    tm = lax.axis_index("tm")
    rows = lax.axis_index("rows")
    core = lax.rem(tm, 2)
    b = lax.rem(tm, 16)
    y_lo = tm // 16
    x = lax.rem(rows, 4)
    y = (rows // 4) * 2 + y_lo
    upper, lower = rows > 0, rows < 7
    since, until = tm > 0, tm < 31

    def x_peer(d):
        return (tm, (rows // 4) * 4 + lax.rem(x + d, 4))

    def y_peer(d):
        to = lax.rem(y + d, 4)
        return (lax.rem(to, 2) * 16 + b, (to // 2) * 4 + x)

    def z_peer(d):
        return (y_lo * 16 + lax.rem(b + d, 16), rows)

    def same_core(d):
        return (y_lo * 16 + lax.rem(b + 2 * d, 16), rows)

    def plane(dx, dy):
        to = lax.rem(y + dy, 4)
        return (lax.rem(to, 2) * 16 + b, (to // 2) * 4 + lax.rem(x + dx, 4))

    def near(dt, dr):
        return (lax.rem(tm + 32 + dt, 32), lax.rem(rows + 8 + dr, 8))

    partner = (tm + 1 - 2 * core, rows)

    def remote(src, dst, sem, slot, to):
        return pltpu.make_async_remote_copy(
            src_ref=src, dst_ref=dst, send_sem=sem.at[0, slot], recv_sem=sem.at[1, slot],
            device_id=to, device_id_type=MESH,
        )

    barrier = pltpu.get_barrier_semaphore()
    peers = [near(dt, dr) for dt in (-1, 0, 1) for dr in (-1, 0, 1) if dt or dr]
    peers += [plane(dx, dy) for dx in range(4) for dy in range(4) if dx or dy]
    peers += [z_peer(d) for d in range(1, 16)]
    for to in peers:
        pl.semaphore_signal(barrier, inc=1, device_id=to, device_id_type=MESH)

    loads = [
        pltpu.make_async_copy(src, dst, sem_w.at[i])
        for i, (src, dst) in enumerate(
            ((cot_hbm, cot), (video_hbm, video), (kb_hbm, kb), (project_hbm, project), (ka_hbm, ka))
        )
    ]
    for cp in loads:
        cp.start()

    for buf, chan in ((vbuf, CA), (cbuf, CB), (mbuf, CB), (gbuf, CA)):

        @pl.when(rows == 0)
        def _():
            buf[:, 0] = jnp.zeros((4, W, chan), BF16)

        @pl.when(rows == 7)
        def _():
            buf[:, 3] = jnp.zeros((4, W, chan), BF16)

    @pl.when(tm == 0)
    def _():
        vbuf[0:2] = jnp.zeros((2, 4, W, CA), BF16)
        mbuf[0:2] = jnp.zeros((2, 4, W, CB), BF16)

    @pl.when(tm == 31)
    def _():
        cbuf[2:4] = jnp.zeros((2, 4, W, CB), BF16)
        gbuf[2:4] = jnp.zeros((2, 4, W, CA), BF16)

    class Halo:
        def __init__(self, src, buf, way, sem, direct):
            own = 2 if way > 0 else 0
            mine, theirs = pl.ds(own, 2), pl.ds(2 - own, 2)
            self.gives, self.takes = (until, since) if way > 0 else (since, until)
            self.full = remote(src, buf.at[theirs, pl.ds(1, 2)], sem, 0, near(way, 0))
            self.down = remote(src.at[:, 1], buf.at[mine, 0], sem, 1, near(0, 1))
            self.up = remote(src.at[:, 0], buf.at[mine, 3], sem, 2, near(0, -1))
            if direct:
                self.top = remote(src.at[:, 1], buf.at[theirs, 0], sem, 3, near(way, 1))
                self.low = remote(src.at[:, 0], buf.at[theirs, 3], sem, 4, near(way, -1))
                self.gives_top, self.gives_low = self.gives & lower, self.gives & upper
            else:
                self.top = remote(buf.at[mine, 0], buf.at[theirs, 0], sem, 3, near(way, 0))
                self.low = remote(buf.at[mine, 3], buf.at[theirs, 3], sem, 4, near(way, 0))
                self.gives_top, self.gives_low = self.gives & upper, self.gives & lower

        def rims(self):
            pl.when(lower)(self.down.start)
            pl.when(upper)(self.up.start)

        def ahead(self):
            pl.when(self.gives)(self.full.start)

        def corners(self):
            pl.when(self.gives_top)(self.top.start)
            pl.when(self.gives_low)(self.low.start)

        def wait_rims(self):
            pl.when(upper)(self.down.wait_recv)
            pl.when(lower)(self.up.wait_recv)

        def wait_ahead(self):
            pl.when(self.takes)(self.full.wait_recv)

        def wait_corners(self):
            pl.when(self.takes & upper)(self.top.wait_recv)
            pl.when(self.takes & lower)(self.low.wait_recv)

        def sent(self):
            pl.when(lower)(self.down.wait_send)
            pl.when(upper)(self.up.wait_send)
            pl.when(self.gives)(self.full.wait_send)
            pl.when(self.gives_top)(self.top.wait_send)
            pl.when(self.gives_low)(self.low.wait_send)

    class Shifts:
        def __init__(self, src, buf, dst, way, chan):
            self.own = 2 if way > 0 else 0
            self.src, self.buf, self.dst, self.chan = src, buf, dst, chan

        def make(self, frames, rows_of):
            chan, dst = self.chan, self.dst
            cell = lax.broadcasted_iota(jnp.int32, (W, chan), 0)
            first = self.own if frames == "own" else 2 - self.own
            for f in (first, first + 1):
                for r in rows_of:
                    if frames == "own" and 1 <= r <= 2:
                        v = self.src[f - self.own, r - 1]
                    else:
                        v = self.buf[f, r]
                    v = v.astype(F32)
                    dst[f, r, :, chan : 2 * chan] = v.astype(BF16)
                    left = jnp.where(cell == 0, 0.0, pltpu.roll(v, 1, 0))
                    right = jnp.where(cell == W - 1, 0.0, pltpu.roll(v, W - 1, 0))
                    dst[f, r, :, 0:chan] = left.astype(BF16)
                    dst[f, r, :, 2 * chan : 3 * chan] = right.astype(BF16)

    CENTRE, EDGE, PAST, CORNERS = (
        [(2, 1)], [(2, 0), (2, 2)], [(0, 1), (1, 1)], [(0, 0), (0, 2), (1, 0), (1, 2)],
    )

    def conv(acc, src, weight, chan, taps):
        for kt, kr in taps:
            at = (3 * kt + kr) * 3 * chan
            piece = src[kt : kt + 2, kr : kr + 2].reshape(CELLS, 3 * chan)
            term = dot(piece, weight[at : at + 3 * chan])
            acc = term if acc is None else acc + term
        return acc

    def back(acc, src, weight, chan, taps):
        for kt, kr in taps:
            for kc in range(3):
                at = (9 * kt + 3 * kr + kc) * chan
                piece = src[2 - kt : 4 - kt, 2 - kr : 4 - kr, :, (2 - kc) * chan : (3 - kc) * chan]
                term = dot(piece.reshape(CELLS, chan), weight[at : at + chan], 1, 1)
                acc = term if acc is None else acc + term
        return acc

    halo_c = Halo(cot, cbuf, -1, sem_c, False)
    halo_v = Halo(video, vbuf, 1, sem_v, False)
    shift_c = Shifts(cot, cbuf, us, -1, CB)
    shift_v = Shifts(video, vbuf, xs, 1, CA)

    loads[0].wait()
    loads[1].wait()
    shift_c.make("own", (1, 2))
    shift_v.make("own", (1, 2))
    loads[2].wait()
    loads[3].wait()
    back_b = back(None, us, kb, CB, CENTRE)
    loads[4].wait()
    pre = conv(None, xs, ka, CA, CENTRE)

    pl.semaphore_wait(barrier, len(peers))
    halo_c.rims()
    halo_v.rims()
    halo_c.ahead()
    halo_v.ahead()
    halo_c.wait_rims()
    halo_c.corners()
    halo_v.wait_rims()
    halo_v.corners()
    shift_c.make("own", (0, 3))
    back_b = back(back_b, us, kb, CB, EDGE)
    shift_v.make("own", (0, 3))
    pre = conv(pre, xs, ka, CA, EDGE)
    halo_c.wait_ahead()
    shift_c.make("other", (1, 2))
    back_b = back(back_b, us, kb, CB, PAST)
    halo_v.wait_ahead()
    shift_v.make("other", (1, 2))
    pre = conv(pre, xs, ka, CA, PAST)
    halo_c.wait_corners()
    shift_c.make("other", (0, 3))
    back_b = back(back_b, us, kb, CB, CORNERS)
    grad_mid = cot[...].reshape(CELLS, CB).astype(F32) + back_b
    mid_t = grad_mid.T
    for c in range(2):
        pick = [mid_t[16 * j + 8 * c : 16 * j + 8 * c + 8] for j in range(8)]
        qt[c] = jnp.concatenate(pick, 0).astype(BF16)
    grad_h = dot(grad_mid.astype(BF16), project[...], 1, 1)

    halo_v.wait_corners()
    shift_v.make("other", (0, 3))
    pre = conv(pre, xs, ka, CA, CORNERS)
    sig = jax.nn.sigmoid(pre)
    hidden = (pre * sig).astype(BF16)
    mid = dot(hidden, project[...])
    mown[...] = mid.astype(BF16).reshape(2, 2, W, CB)
    halo_m = Halo(mown, mbuf, 1, sem_m, False)
    halo_m.rims()
    halo_m.ahead()
    grad_pre = grad_h * sig * (1.0 + pre * (1.0 - sig))
    gown[...] = grad_pre.astype(BF16).reshape(2, 2, W, CA)
    halo_g = Halo(gown, gbuf, -1, sem_g, True)
    halo_g.rims()
    halo_g.ahead()
    out[...] = mid.reshape(2, 2, W, CB)
    grad_t = grad_pre.T
    for c in range(2):
        for j in range(8):
            gt[c, j] = grad_t[32 * j + 16 * c : 32 * j + 16 * c + 16].astype(BF16)

    def chunk_a(left, k):
        kt, kr = k // 3, k % 3
        return dot(left, xs[kt : kt + 2, kr : kr + 2].reshape(CELLS, 3 * CA))

    class Group:
        def __init__(self, s0x, r1x, s1x, r2y, sem1x, sem2y, s0y, r1y, s1y, r2x, sem1y, sem2x):
            self.s0x, self.r1x, self.s1x, self.r2y, self.sem1x, self.sem2y = s0x, r1x, s1x, r2y, sem1x, sem2y
            self.s0y, self.r1y, self.s1y, self.r2x, self.sem1y, self.sem2x = s0y, r1y, s1y, r2x, sem1y, sem2x

        def x1(self, d, yl):
            src = self.s0x.at[lax.rem(x + d, 4), yl]
            return remote(src, self.r1x.at[d - 1, yl], self.sem1x, 2 * (d - 1) + yl, x_peer(d))

        def y1(self, d):
            return remote(self.s0y.at[lax.rem(y + d, 4)], self.r1y.at[d - 1], self.sem1y, d - 1, y_peer(d))

        def y2(self, d):
            return remote(self.s1x.at[lax.rem(y + d, 4)], self.r2y.at[d - 1], self.sem2y, d - 1, y_peer(d))

        def x2(self, d):
            return remote(self.s1y.at[lax.rem(x + d, 4)], self.r2x.at[d - 1], self.sem2x, d - 1, x_peer(d))

        def send_x(self, yl):
            for d in (2, 1, 3):
                self.x1(d, yl).start()

        def send_y(self, yl):
            for yh in range(2):
                d = lax.rem(2 * yh + yl - y + 4, 4)

                @pl.when(d > 0)
                def _():
                    self.y1(d).start()

        def add_x(self, yl):
            for d in (1, 2, 3):
                self.x1(d, yl).wait()
            for yh in range(2):
                to = 2 * yh + yl
                acc = self.s0x[x, yl, yh].astype(F32)
                for s in range(3):
                    acc = acc + self.r1x[s, yl, yh].astype(F32)
                self.s1x[to] = acc.astype(BF16)
                d = lax.rem(to - y + 4, 4)

                @pl.when(d > 0)
                def _():
                    self.y2(d).start()

        def add_y(self):
            for d in (1, 2, 3):
                self.y1(d).wait()
            for d in ORDER:
                to = lax.rem(x + d, 4)
                acc = self.s0y[y, to].astype(F32)
                for s in range(3):
                    acc = acc + self.r1y[s, to].astype(F32)
                self.s1y[to] = acc.astype(BF16)
                if d:
                    self.x2(d).start()

        def finish(self, t_ref, lx):
            for d in (1, 2, 3):
                self.y2(d).wait()
            acc = self.s1x[y].astype(F32)
            for s in range(3):
                acc = acc + self.r2y[s].astype(F32)
            t_ref[:, :lx] = acc
            for d in (1, 2, 3):
                self.x2(d).wait()
            acc = self.s1y[x].astype(F32)
            for s in range(3):
                acc = acc + self.r2x[s].astype(F32)
            t_ref[:, lx:] = acc

    group_a = Group(s0xa, r1xa, s1xa, r2ya, sem1xa, sem2ya, s0ya, r1ya, s1ya, r2xa, sem1ya, sem2xa)

    left = jnp.concatenate([gt[1 - core].reshape(128, CELLS), gt[core].reshape(128, CELLS)], 0)
    cuts = sorted({768 * k for k in range(10)} | {0, XA, HALF_A, HALF_A + XA, 2 * HALF_A})
    copies_a = []
    for step in range(9 + LAG):
        if step < 9:
            value = chunk_a(left, step)
            send_a[step] = value[0:128].astype(BF16).reshape(8, 16, 768)
            cp = remote(send_a.at[step], recv_a.at[step], sem_a, step, partner)
            cp.start()
            copies_a.append(cp)
            own_a[step] = value[128:256]
        k = step - LAG
        if k < 0:
            continue
        copies_a[k].wait()
        value = (own_a[k] + recv_a[k].reshape(128, 768).astype(F32)).astype(BF16)
        inside = [c for c in cuts if 768 * k <= c <= 768 * k + 768]
        for lo, hi in zip(inside[:-1], inside[1:]):
            yl, at = lo // HALF_A, lo % HALF_A
            for j in range(8):
                cut = value[16 * j : 16 * j + 16, lo - 768 * k : hi - 768 * k]
                if at < XA:
                    s0xa[j % 4, yl, j // 4, :, at : at + hi - lo] = cut
                else:
                    s0ya[(j // 4) * 2 + yl, j % 4, :, at - XA : at - XA + hi - lo] = cut
            if hi % HALF_A == XA:
                group_a.send_x(yl)
            if hi % HALF_A == 0:
                group_a.send_y(yl)

    mid_own = mid.T.astype(BF16)
    for k in range(9):
        kt, kr = k // 3, k % 3
        value = dot(mid_own, us[2 - kt : 4 - kt, 2 - kr : 4 - kr].reshape(CELLS, 3 * CB))
        for kc in range(3):
            tap = value[:, (2 - kc) * CB : (3 - kc) * CB].T
            at = (3 * k + kc) * CB
            for c in range(2):
                for j in range(8):
                    part[c, j, :, at : at + CB] = tap[16 * j + 8 * c : 16 * j + 8 * c + 8]

    def packed(half):
        proj = dot(qt[half], hidden)
        for j in range(8):
            for yl in range(2):
                for z in range(8):
                    both = []
                    for c in range(2):
                        at, to = 1728 * yl + 216 * z + 108 * c, 128 * yl + 16 * z + 8 * c
                        tail = proj[8 * j : 8 * j + 8, to : to + 8]
                        both.append(jnp.concatenate([part[half, j, :, at : at + 108], tail, jnp.zeros((8, 12), F32)], 1))
                    yield z, j, yl, jnp.concatenate(both, 0)

    for z, j, yl, value in packed(1 - core):
        send_b[z, j, yl] = value.astype(BF16)
    copy_b = remote(send_b, recv_b, sem_b, 0, partner)
    copy_b.start()
    halo_m.wait_rims()
    halo_m.corners()
    copy_b.wait()
    for z, j, yl, value in packed(core):
        s0b[z, j, yl] = (value + recv_b[z, j, yl].astype(F32)).astype(BF16)
    me_z = b // 2
    first_b = [
        remote(s0b.at[lax.rem(me_z + d, 8)], r1b.at[d - 1], sem1b, d - 1, same_core(d)) for d in range(1, 8)
    ]
    for d in (4, 3, 5, 2, 6, 1, 7):
        first_b[d - 1].start()

    group_a.add_x(0)
    every = CENTRE + EDGE + PAST + CORNERS
    shift_m = Shifts(mown, mbuf, ms, 1, CB)
    shift_m.make("own", (0, 1, 2, 3))
    halo_m.wait_ahead()
    halo_m.wait_corners()
    shift_m.make("other", (0, 1, 2, 3))
    out[...] = out[...] + conv(None, ms, kb, CB, every).reshape(2, 2, W, CB)
    done = [
        pltpu.make_async_copy(out, out_hbm, sem_o.at[0]),
        pltpu.make_async_copy(grad_video, grad_video_hbm, sem_o.at[1]),
    ]
    done[0].start()
    group_a.add_x(1)
    group_a.add_y()
    halo_g.corners()
    group_a.finish(t_a, XA)
    for k in range(16):
        high = jnp.concatenate([t_a[:, 216 * k : 216 * k + 216], jnp.zeros((16, 40), F32)], 1)
        msg[k] = high.astype(BF16)
    last = []
    for d in range(1, 16):
        cp = remote(msg.at[lax.rem(b + d, 16)], r3.at[d - 1], sem3, d - 1, z_peer(d))
        cp.start()
        last.append(cp)
    for cp in first_b:
        cp.wait()
    for j in range(8):
        acc = s0b[me_z, j].astype(F32)
        for s in range(7):
            acc = acc + r1b[s, j].astype(F32)
        s1b[j // 4, j % 4] = acc.astype(BF16)
    second_b = []
    for dx in range(4):
        for dy in range(4):
            if dx or dy:
                to = lax.rem(y + dy, 4)
                src = s1b.at[to // 2, lax.rem(x + dx, 4), lax.rem(to, 2)]
                slot = 4 * dx + dy - 1
                cp = remote(src, r2b.at[slot], sem2b, slot, plane(dx, dy))
                cp.start()
                second_b.append(cp)
    shift_g = Shifts(gown, gbuf, gs, -1, CA)
    halo_g.wait_rims()
    shift_g.make("own", (0, 1, 2, 3))
    halo_g.wait_ahead()
    halo_g.wait_corners()
    shift_g.make("other", (0, 1, 2, 3))
    grad_video[...] = back(None, gs, ka, CA, every).reshape(2, 2, W, CA)
    done[1].start()
    for cp in second_b:
        cp.wait()
    acc = s1b[y // 2, x, lax.rem(y, 2)].astype(F32)
    for s in range(15):
        acc = acc + r2b[s].astype(F32)
    scale = 1.0 / (64 * 16 * W) ** 0.5
    tb[...] = (acc * scale).reshape(2, 8, 128)
    swap = remote(tb.at[1 - core], gb.at[core], sem3b, 0, partner)
    swap.start()
    for cp in last:
        cp.wait()
    same = msg[b].astype(F32)
    for d in range(2, 16, 2):
        same = same + r3[d - 1].astype(F32)
    other = r3[0].astype(F32)
    for d in range(3, 16, 2):
        other = other + r3[d - 1].astype(F32)
    total[core] = same * scale
    total[1 - core] = other * scale
    grad_a[...] = total[:, :, 0:216].reshape(32, 216)
    swap.wait()
    gb[core] = tb[core]
    low = gb[...].reshape(16, 128)
    grad_b[...] = low[:, 0:108]
    grad_p[...] = low.T[108:116]
    for halo in (halo_c, halo_v, halo_m, halo_g):
        halo.sent()
    for cp in done:
        cp.wait()


def written(*refs):
    took, gives, held, sem = refs[:5], refs[5:10], refs[10:15], refs[15]
    reads = [pltpu.make_async_copy(took[i], held[i], sem.at[0, i]) for i in range(5)]
    writes = [pltpu.make_async_copy(held[i], gives[i], sem.at[1, i]) for i in range(5)]
    for cp in reads:
        cp.start()
    for i in range(5):
        reads[i].wait()
        writes[i].start()
    for cp in writes:
        cp.wait()


def shards(video, kernel_a, project, kernel_b, cotangent):
    dma = pltpu.SemaphoreType.DMA
    vmem = pl.BlockSpec(memory_space=pltpu.VMEM)
    hbm = pl.BlockSpec(memory_space=pl.ANY)

    def group(lx, ly):
        return [
            pltpu.VMEM((4, 2, 2, 16, lx), BF16), pltpu.VMEM((4, 4, 16, ly), BF16),
            pltpu.VMEM((3, 2, 2, 16, lx), BF16), pltpu.VMEM((3, 4, 16, ly), BF16),
            pltpu.VMEM((4, 16, lx), BF16), pltpu.VMEM((4, 16, ly), BF16),
            pltpu.VMEM((3, 16, lx), BF16), pltpu.VMEM((3, 16, ly), BF16),
        ]

    results = pl.pallas_call(
        kernel,
        out_shape=[
            jax.ShapeDtypeStruct((2, 2, W, CB), F32),
            jax.ShapeDtypeStruct((2, 2, W, CA), F32),
            jax.ShapeDtypeStruct((32, 216), F32),
            jax.ShapeDtypeStruct((16, 108), F32),
            jax.ShapeDtypeStruct((8, 16), F32),
        ],
        in_specs=[hbm] * 5,
        out_specs=[hbm, hbm, vmem, vmem, vmem],
        scratch_shapes=[
            pltpu.VMEM((2, 2, W, CB), F32), pltpu.VMEM((2, 2, W, CA), F32),
            pltpu.VMEM((2, 2, W, CA), BF16), pltpu.VMEM((2, 2, W, CB), BF16), pltpu.VMEM((CA, CB), BF16),
            pltpu.VMEM((27 * CA, CA), BF16), pltpu.VMEM((27 * CB, CB), BF16),
            pltpu.VMEM((4, 4, W, CA), BF16), pltpu.VMEM((4, 4, W, CB), BF16),
            pltpu.VMEM((4, 4, W, CB), BF16), pltpu.VMEM((4, 4, W, CA), BF16),
            pltpu.VMEM((2, 2, W, CB), BF16), pltpu.VMEM((2, 2, W, CA), BF16),
            pltpu.VMEM((4, 4, W, 3 * CA), BF16), pltpu.VMEM((4, 4, W, 3 * CB), BF16),
            pltpu.VMEM((4, 4, W, 3 * CB), BF16), pltpu.VMEM((4, 4, W, 3 * CA), BF16),
            pltpu.VMEM((2, 8, 16, CELLS), BF16), pltpu.VMEM((2, 64, CELLS), BF16),
            pltpu.VMEM((9, 8, 16, 768), BF16), pltpu.VMEM((9, 8, 16, 768), BF16),
            pltpu.VMEM((9, 128, 768), F32),
            pltpu.VMEM((8, 8, 2, 16, 128), BF16), pltpu.VMEM((8, 8, 2, 16, 128), BF16),
            pltpu.VMEM((2, 8, 8, 27 * CB), F32),
            *group(XA, YA),
            pltpu.VMEM((8, 8, 2, 16, 128), BF16), pltpu.VMEM((7, 8, 2, 16, 128), BF16),
            pltpu.VMEM((2, 4, 2, 16, 128), BF16), pltpu.VMEM((15, 16, 128), BF16),
            pltpu.VMEM((2, 8, 128), F32), pltpu.VMEM((2, 8, 128), F32),
            pltpu.VMEM((16, HALF_A), F32),
            pltpu.VMEM((16, 16, 256), BF16), pltpu.VMEM((15, 16, 256), BF16),
            pltpu.VMEM((2, 16, 256), F32),
            dma((5,)), dma((2, 5)), dma((2, 5)), dma((2, 5)), dma((2, 5)), dma((2, 9)), dma((2, 1)),
            *[dma((2, n)) for n in (6, 3, 3, 3, 15, 7, 15, 1)],
            dma((2,)),
        ],
        compiler_params=pltpu.CompilerParams(
            collective_id=0, has_side_effects=True, vmem_limit_bytes=56 * 1024 * 1024
        ),
    )(video, cotangent, kernel_a, project, kernel_b)
    results = pl.pallas_call(
        written,
        out_shape=[jax.ShapeDtypeStruct(r.shape, F32) for r in results],
        in_specs=[hbm] * 5,
        out_specs=[hbm] * 5,
        scratch_shapes=[*[pltpu.VMEM(r.shape, F32) for r in results], dma((2, 5))],
    )(*results)
    return results[0], results[1], results[2].T, results[3].T, results[4]


def solution(mesh):
    cells = P("tm", "rows", None, None)
    return jax.shard_map(
        shards,
        mesh=mesh,
        in_specs=(cells, P(), P(), P(), cells),
        out_specs=(cells, cells, P("tm", "rows"), P("tm", "rows"), P("tm", "rows")),
        check_vma=False,
    )
```

```python
import jax
import jax.numpy as jnp
from jax import lax
from jax.experimental import pallas as pl
from jax.experimental.pallas import tpu as pltpu
from jax.sharding import PartitionSpec as P

F32, BF16 = jnp.float32, jnp.bfloat16
MESH = pl.DeviceIdType.MESH
CA, CB, W = 256, 128, 96
CELLS = 4 * W
HALF_A = 27 * CA // 2
XA, YA = 1792, HALF_A - 1792
XB, YB = 512, 512
PB = 896
LAG = 3
ORDER = (1, 2, 3, 0)


def dot(a, b, ca=1, cb=0):
    return lax.dot_general(a, b, (((ca,), (cb,)), ((), ())), preferred_element_type=F32)


def kernel(
    video_hbm, cot_hbm, ka_hbm, project_hbm, kb_hbm,
    out_hbm, grad_video_hbm, grad_a, grad_b, grad_p,
    out, grad_video, video, cot, project, ka, kb, vbuf, cbuf, mbuf, gbuf, mown, gown, xs, us, ms, gs,
    gt, qt, send_a, recv_a, own_a, send_b, recv_b, part,
    s0xa, s0ya, q1xa, q1ya, r1xa, r1ya, s1xa, s1ya, r2ya, r2xa,
    s0xb, s0yb, q1xb, q1yb, r1xb, r1yb, s1xb, s1yb, r2yb, r2xb,
    t_a, t_b, msg_a, r3a, total_a, msg_b, r3b, total_b,
    sem_w, sem_v, sem_c, sem_m, sem_g, sem_a, sem_b,
    sem1xa, sem1ya, sem2ya, sem2xa, sem1xb, sem1yb, sem2yb, sem2xb, sem3a, sem3b, sem_o,
):
    tm = lax.axis_index("tm")
    rows = lax.axis_index("rows")
    core = lax.rem(tm, 2)
    b = lax.rem(tm, 16)
    y_lo = tm // 16
    x = lax.rem(rows, 4)
    y = (rows // 4) * 2 + y_lo
    upper, lower = rows > 0, rows < 7
    since, until = tm > 0, tm < 31

    def x_peer(d):
        return (tm, (rows // 4) * 4 + lax.rem(x + d, 4))

    def y_peer(d):
        to = lax.rem(y + d, 4)
        return (lax.rem(to, 2) * 16 + b, (to // 2) * 4 + x)

    def z_peer(d):
        return (y_lo * 16 + lax.rem(b + d, 16), rows)

    def near(dt, dr):
        return (lax.rem(tm + 32 + dt, 32), lax.rem(rows + 8 + dr, 8))

    partner = (tm + 1 - 2 * core, rows)

    def remote(src, dst, sem, slot, to):
        return pltpu.make_async_remote_copy(
            src_ref=src, dst_ref=dst, send_sem=sem.at[0, slot], recv_sem=sem.at[1, slot],
            device_id=to, device_id_type=MESH,
        )

    barrier = pltpu.get_barrier_semaphore()
    peers = [z_peer(d) for d in (8, 9, 7, 10, 6, 11, 5, 12, 4, 13, 3, 14, 2, 15, 1)]
    peers += [near(dt, dr) for dt, dr in ((0, 1), (0, -1), (1, 0), (-1, 0))]
    peers += [y_peer(d) for d in (2, 1, 3)] + [x_peer(d) for d in (2, 1, 3)]
    for to in peers:
        pl.semaphore_signal(barrier, inc=1, device_id=to, device_id_type=MESH)

    loads = [
        pltpu.make_async_copy(src, dst, sem_w.at[i])
        for i, (src, dst) in enumerate(
            ((cot_hbm, cot), (video_hbm, video), (kb_hbm, kb), (project_hbm, project), (ka_hbm, ka))
        )
    ]
    for cp in loads:
        cp.start()

    for buf, chan in ((vbuf, CA), (cbuf, CB), (mbuf, CB), (gbuf, CA)):

        @pl.when(rows == 0)
        def _():
            buf[:, 0] = jnp.zeros((4, W, chan), BF16)

        @pl.when(rows == 7)
        def _():
            buf[:, 3] = jnp.zeros((4, W, chan), BF16)

    @pl.when(tm == 0)
    def _():
        vbuf[0:2] = jnp.zeros((2, 4, W, CA), BF16)
        mbuf[0:2] = jnp.zeros((2, 4, W, CB), BF16)

    @pl.when(tm == 31)
    def _():
        cbuf[2:4] = jnp.zeros((2, 4, W, CB), BF16)
        gbuf[2:4] = jnp.zeros((2, 4, W, CA), BF16)

    class Halo:
        def __init__(self, src, buf, way, sem):
            own = 2 if way > 0 else 0
            mine, theirs = pl.ds(own, 2), pl.ds(2 - own, 2)
            self.gives, self.takes = (until, since) if way > 0 else (since, until)
            self.full = remote(src, buf.at[theirs, pl.ds(1, 2)], sem, 0, near(way, 0))
            self.down = remote(src.at[:, 1], buf.at[mine, 0], sem, 1, near(0, 1))
            self.up = remote(src.at[:, 0], buf.at[mine, 3], sem, 2, near(0, -1))
            self.top = remote(buf.at[mine, 0], buf.at[theirs, 0], sem, 3, near(way, 0))
            self.low = remote(buf.at[mine, 3], buf.at[theirs, 3], sem, 4, near(way, 0))
            self.gives_top, self.gives_low = self.gives & upper, self.gives & lower

        def rims(self):
            pl.when(lower)(self.down.start)
            pl.when(upper)(self.up.start)

        def ahead(self):
            pl.when(self.gives)(self.full.start)

        def corners(self):
            pl.when(self.gives_top)(self.top.start)
            pl.when(self.gives_low)(self.low.start)

        def wait_rims(self):
            pl.when(upper)(self.down.wait_recv)
            pl.when(lower)(self.up.wait_recv)

        def wait_ahead(self):
            pl.when(self.takes)(self.full.wait_recv)

        def wait_corners(self):
            pl.when(self.takes & upper)(self.top.wait_recv)
            pl.when(self.takes & lower)(self.low.wait_recv)

        def sent(self):
            pl.when(lower)(self.down.wait_send)
            pl.when(upper)(self.up.wait_send)
            pl.when(self.gives)(self.full.wait_send)
            pl.when(self.gives_top)(self.top.wait_send)
            pl.when(self.gives_low)(self.low.wait_send)

    class Shifts:
        def __init__(self, src, buf, dst, way, chan):
            self.own = 2 if way > 0 else 0
            self.src, self.buf, self.dst, self.chan = src, buf, dst, chan

        def make(self, frames, rows_of):
            chan, dst = self.chan, self.dst
            cell = lax.broadcasted_iota(jnp.int32, (W, chan), 0)
            first = self.own if frames == "own" else 2 - self.own
            for f in (first, first + 1):
                for r in rows_of:
                    if frames == "own" and 1 <= r <= 2:
                        v = self.src[f - self.own, r - 1]
                    else:
                        v = self.buf[f, r]
                    v = v.astype(F32)
                    dst[f, r, :, chan : 2 * chan] = v.astype(BF16)
                    left = jnp.where(cell == 0, 0.0, pltpu.roll(v, 1, 0))
                    right = jnp.where(cell == W - 1, 0.0, pltpu.roll(v, W - 1, 0))
                    dst[f, r, :, 0:chan] = left.astype(BF16)
                    dst[f, r, :, 2 * chan : 3 * chan] = right.astype(BF16)

    CENTRE, EDGE, PAST, CORNERS = (
        [(2, 1)], [(2, 0), (2, 2)], [(0, 1), (1, 1)], [(0, 0), (0, 2), (1, 0), (1, 2)],
    )

    def conv(acc, src, weight, chan, taps):
        for kt, kr in taps:
            at = (3 * kt + kr) * 3 * chan
            piece = src[kt : kt + 2, kr : kr + 2].reshape(CELLS, 3 * chan)
            term = dot(piece, weight[at : at + 3 * chan])
            acc = term if acc is None else acc + term
        return acc

    def back(acc, src, weight, chan, taps):
        for kt, kr in taps:
            for kc in range(3):
                at = (9 * kt + 3 * kr + kc) * chan
                piece = src[2 - kt : 4 - kt, 2 - kr : 4 - kr, :, (2 - kc) * chan : (3 - kc) * chan]
                term = dot(piece.reshape(CELLS, chan), weight[at : at + chan], 1, 1)
                acc = term if acc is None else acc + term
        return acc

    halo_c = Halo(cot_hbm, cbuf, -1, sem_c)
    halo_v = Halo(video_hbm, vbuf, 1, sem_v)
    shift_c = Shifts(cot, cbuf, us, -1, CB)
    shift_v = Shifts(video, vbuf, xs, 1, CA)

    pl.semaphore_wait(barrier, len(peers))
    halo_c.rims()
    halo_v.rims()
    halo_c.ahead()
    halo_v.ahead()
    loads[0].wait()
    loads[1].wait()
    shift_c.make("own", (1, 2))
    shift_v.make("own", (1, 2))
    loads[2].wait()
    loads[3].wait()
    back_b = back(None, us, kb, CB, CENTRE)
    loads[4].wait()
    pre = conv(None, xs, ka, CA, CENTRE)

    halo_c.wait_rims()
    halo_c.corners()
    halo_v.wait_rims()
    halo_v.corners()
    shift_c.make("own", (0, 3))
    back_b = back(back_b, us, kb, CB, EDGE)
    shift_v.make("own", (0, 3))
    pre = conv(pre, xs, ka, CA, EDGE)
    halo_c.wait_ahead()
    shift_c.make("other", (1, 2))
    back_b = back(back_b, us, kb, CB, PAST)
    halo_v.wait_ahead()
    shift_v.make("other", (1, 2))
    pre = conv(pre, xs, ka, CA, PAST)
    halo_c.wait_corners()
    shift_c.make("other", (0, 3))
    back_b = back(back_b, us, kb, CB, CORNERS)
    grad_mid = cot[...].reshape(CELLS, CB).astype(F32) + back_b
    mid_t = grad_mid.T
    for c in range(2):
        pick = [mid_t[16 * j + 8 * c : 16 * j + 8 * c + 8] for j in range(8)]
        qt[c] = jnp.concatenate(pick, 0).astype(BF16)
    grad_h = dot(grad_mid.astype(BF16), project[...], 1, 1)

    halo_v.wait_corners()
    shift_v.make("other", (0, 3))
    pre = conv(pre, xs, ka, CA, CORNERS)
    sig = jax.nn.sigmoid(pre)
    hidden = (pre * sig).astype(BF16)
    mid = dot(hidden, project[...])
    mown[...] = mid.astype(BF16).reshape(2, 2, W, CB)
    halo_m = Halo(mown, mbuf, 1, sem_m)
    halo_m.rims()
    halo_m.ahead()
    grad_pre = grad_h * sig * (1.0 + pre * (1.0 - sig))
    gown[...] = grad_pre.astype(BF16).reshape(2, 2, W, CA)
    halo_g = Halo(gown, gbuf, -1, sem_g)
    halo_g.rims()
    halo_g.ahead()
    out[...] = mid.reshape(2, 2, W, CB)
    grad_t = grad_pre.T
    for c in range(2):
        for j in range(8):
            gt[c, j] = grad_t[32 * j + 16 * c : 32 * j + 16 * c + 16].astype(BF16)

    def chunk_a(left, k):
        kt, kr = k // 3, k % 3
        return dot(left, xs[kt : kt + 2, kr : kr + 2].reshape(CELLS, 3 * CA))

    class Group:
        def __init__(self, s0x, q1x, r1x, s1x, r2y, s0y, q1y, r1y, s1y, r2x, sem1x, sem1y, sem2y, sem2x):
            self.s0x, self.q1x, self.r1x, self.s1x, self.r2y = s0x, q1x, r1x, s1x, r2y
            self.s0y, self.q1y, self.r1y, self.s1y, self.r2x = s0y, q1y, r1y, s1y, r2x
            self.sem1x, self.sem1y, self.sem2y, self.sem2x = sem1x, sem1y, sem2y, sem2x

        def x_far(self, yl, h):
            src = self.s0x.at[lax.rem(x + 2, 4), yl, h]
            return remote(src, self.q1x.at[yl, h], self.sem1x, 6 * yl + h, x_peer((1, 3)[h]))

        def x_near(self, yl, side, h):
            d = (1, 3)[side]
            src = self.s0x.at[lax.rem(x + d, 4), yl, h]
            return remote(src, self.r1x.at[side, yl, h], self.sem1x, 6 * yl + 2 + 2 * side + h, x_peer(d))

        def y_far(self, h):
            src = self.s0y.at[lax.rem(y + 2, 4), pl.ds(2 * h, 2)]
            return remote(src, self.q1y.at[h], self.sem1y, h, y_peer((1, 3)[h]))

        def y_near(self, side, h):
            d = (1, 3)[side]
            src = self.s0y.at[lax.rem(y + d, 4), pl.ds(2 * h, 2)]
            return remote(src, self.r1y.at[side, pl.ds(2 * h, 2)], self.sem1y, 2 + 2 * side + h, y_peer(d))

        def y2(self, d):
            return remote(self.s1x.at[lax.rem(y + d, 4)], self.r2y.at[d - 1], self.sem2y, d - 1, y_peer(d))

        def x2(self, d):
            return remote(self.s1y.at[lax.rem(x + d, 4)], self.r2x.at[d - 1], self.sem2x, d - 1, x_peer(d))

        def send_x(self, yl):
            self.x_far(yl, 0).start()
            self.x_far(yl, 1).start()
            self.x_near(yl, 0, 1).start()
            self.x_near(yl, 1, 0).start()

        def send_y(self, yl):
            @pl.when(y_lo == yl)
            def _():
                self.y_far(0).start()
                self.y_far(1).start()

            @pl.when(y_lo != yl)
            def _():
                self.y_near(0, 1).start()
                self.y_near(1, 0).start()

        def relay_x(self, yl):
            for h in range(2):
                to = lax.rem(x + (1, 3)[h], 4)
                self.x_far(yl, h).wait_recv()
                both = self.s0x[to, yl, h].astype(F32) + self.q1x[yl, h].astype(F32)
                self.s0x[to, yl, h] = both.astype(BF16)
                self.x_near(yl, h, h).start()

        def relay_y(self):
            for h in range(2):
                to, part = lax.rem(y + (1, 3)[h], 4), slice(2 * h, 2 * h + 2)
                self.y_far(h).wait_recv()
                both = self.s0y[to, part].astype(F32) + self.q1y[h].astype(F32)
                self.s0y[to, part] = both.astype(BF16)
                self.y_near(h, h).start()

        def add_x(self, yl):
            for h in range(2):
                self.x_far(yl, h).wait_send()
                for side in range(2):
                    self.x_near(yl, side, h).wait()
            for yh in range(2):
                to = 2 * yh + yl
                acc = self.s0x[x, yl, yh].astype(F32)
                for side in range(2):
                    acc = acc + self.r1x[side, yl, yh].astype(F32)
                self.s1x[to] = acc.astype(BF16)
                d = lax.rem(to - y + 4, 4)

                @pl.when(d > 0)
                def _():
                    self.y2(d).start()

        def add_y(self):
            for h in range(2):
                self.y_far(h).wait_send()
                for side in range(2):
                    self.y_near(side, h).wait()
            for d in ORDER:
                to = lax.rem(x + d, 4)
                acc = self.s0y[y, to].astype(F32)
                for side in range(2):
                    acc = acc + self.r1y[side, to].astype(F32)
                self.s1y[to] = acc.astype(BF16)
                if d:
                    self.x2(d).start()

        def finish_x(self, t_ref, lx):
            for d in (1, 2, 3):
                self.y2(d).wait()
            acc = self.s1x[y].astype(F32)
            for s in range(3):
                acc = acc + self.r2y[s].astype(F32)
            t_ref[:, :lx] = acc

        def finish_y(self, t_ref, lx):
            for d in (1, 2, 3):
                self.x2(d).wait()
            acc = self.s1y[x].astype(F32)
            for s in range(3):
                acc = acc + self.r2x[s].astype(F32)
            t_ref[:, lx:] = acc

    group_a = Group(s0xa, q1xa, r1xa, s1xa, r2ya, s0ya, q1ya, r1ya, s1ya, r2xa, sem1xa, sem1ya, sem2ya, sem2xa)
    group_b = Group(s0xb, q1xb, r1xb, s1xb, r2yb, s0yb, q1yb, r1yb, s1yb, r2xb, sem1xb, sem1yb, sem2yb, sem2xb)

    left = jnp.concatenate([gt[1 - core].reshape(128, CELLS), gt[core].reshape(128, CELLS)], 0)
    cuts = sorted({768 * k for k in range(10)} | {0, XA, HALF_A, HALF_A + XA, 2 * HALF_A})
    copies_a = []
    for step in range(9 + LAG):
        if step < 9:
            value = chunk_a(left, step)
            send_a[step] = value[0:128].astype(BF16).reshape(8, 16, 768)
            cp = remote(send_a.at[step], recv_a.at[step], sem_a, step, partner)
            cp.start()
            copies_a.append(cp)
            own_a[step] = value[128:256]
        k = step - LAG
        if k < 0:
            continue
        copies_a[k].wait()
        value = (own_a[k] + recv_a[k].reshape(128, 768).astype(F32)).astype(BF16)
        inside = [c for c in cuts if 768 * k <= c <= 768 * k + 768]
        for lo, hi in zip(inside[:-1], inside[1:]):
            yl, at = lo // HALF_A, lo % HALF_A
            for j in range(8):
                cut = value[16 * j : 16 * j + 16, lo - 768 * k : hi - 768 * k]
                if at < XA:
                    s0xa[j % 4, yl, j // 4, :, at : at + hi - lo] = cut
                else:
                    s0ya[(j // 4) * 2 + yl, j % 4, :, at - XA : at - XA + hi - lo] = cut
            if hi % HALF_A == XA:
                group_a.send_x(yl)
            if hi % HALF_A == 0:
                group_a.send_y(yl)

    halo_m.wait_rims()
    halo_m.corners()
    halo_g.wait_rims()
    halo_g.corners()
    mid_own = mid.T.astype(BF16)
    for k in range(9):
        kt, kr = k // 3, k % 3
        value = dot(mid_own, us[2 - kt : 4 - kt, 2 - kr : 4 - kr].reshape(CELLS, 3 * CB))
        for kc in range(3):
            tap = value[:, (2 - kc) * CB : (3 - kc) * CB].T
            at = (3 * k + kc) * CB
            for c in range(2):
                for j in range(8):
                    part[c, j, :, at : at + CB] = tap[16 * j + 8 * c : 16 * j + 8 * c + 8]

    def packed(half):
        proj = dot(qt[half], hidden)
        for j in range(8):
            for yl in range(2):
                at = 13 * CB * yl
                upper_half = part[half, j, :, at : at + PB]
                lower_half = part[half, j, :, at + PB : at + 2 * PB]
                body = jnp.concatenate([upper_half, lower_half], 0)
                tail = proj[8 * j : 8 * j + 8, 128 * yl : 128 * yl + 128]
                tail = jnp.concatenate([tail, jnp.zeros((8, 128), F32)], 0)
                yield j, yl, jnp.concatenate([body, tail], 1)

    for j, yl, value in packed(1 - core):
        send_b[j, yl] = value.astype(BF16)
    copy_b = remote(send_b, recv_b, sem_b, 0, partner)
    copy_b.start()
    copy_b.wait()
    for j, yl, value in packed(core):
        value = (value + recv_b[j, yl].astype(F32)).astype(BF16)
        s0xb[j % 4, yl, j // 4] = value[:, :XB]
        s0yb[(j // 4) * 2 + yl, j % 4] = value[:, XB:]
    for yl in range(2):
        group_b.send_x(yl)
    for yl in range(2):
        group_b.send_y(yl)
    for yl in range(2):
        group_a.relay_x(yl)
    group_a.relay_y()
    for yl in range(2):
        group_b.relay_x(yl)
    group_b.relay_y()
    every = CENTRE + EDGE + PAST + CORNERS
    shift_m = Shifts(mown, mbuf, ms, 1, CB)
    shift_m.make("own", (0, 1, 2, 3))
    halo_m.wait_ahead()
    halo_m.wait_corners()
    shift_m.make("other", (0, 1, 2, 3))
    out[...] = out[...] + conv(None, ms, kb, CB, every).reshape(2, 2, W, CB)
    done = [
        pltpu.make_async_copy(out, out_hbm, sem_o.at[0]),
        pltpu.make_async_copy(grad_video, grad_video_hbm, sem_o.at[1]),
    ]
    done[0].start()
    group_a.add_x(0)
    group_a.add_x(1)
    group_a.add_y()
    group_b.add_x(0)
    group_b.add_x(1)
    group_b.add_y()
    def give(msg, r3, sem, k):
        d = lax.rem(k - b + 16, 16)

        @pl.when(d > 0)
        def _():
            remote(msg.at[k], r3.at[d - 1], sem, d - 1, z_peer(d)).start()

    for k in range(16):
        if k == 0:
            group_a.finish_x(t_a, XA)
        if k == 8:
            group_a.finish_y(t_a, XA)
        block = t_a[:, 216 * k : 216 * k + 216]
        msg_a[k] = jnp.concatenate([block, jnp.zeros((16, 40), F32)], 1).astype(BF16)
        give(msg_a, r3a, sem3a, k)
    group_b.finish_x(t_b, XB)
    group_b.finish_y(t_b, XB)
    part_b = jnp.concatenate([t_b[0:8, 0:PB], t_b[8:16, 0:PB]], 1)
    part_b = jnp.where(y_lo == 0, part_b[:, 0:1728], part_b[:, 64:1792])
    part_p = t_b[0:8, PB : PB + 128]
    for k in range(16):
        low = jnp.concatenate(
            [
                part_b[:, 108 * k : 108 * k + 108], jnp.zeros((8, 4), F32),
                part_p[:, 8 * k : 8 * k + 8], jnp.zeros((8, 8), F32),
            ], 1,
        )
        msg_b[k] = jnp.concatenate([low, jnp.zeros((8, 128), F32)], 0).astype(BF16)
        give(msg_b, r3b, sem3b, k)
    shift_g = Shifts(gown, gbuf, gs, -1, CA)
    shift_g.make("own", (0, 1, 2, 3))
    halo_g.wait_ahead()
    halo_g.wait_corners()
    shift_g.make("other", (0, 1, 2, 3))
    grad_video[...] = back(None, gs, ka, CA, every).reshape(2, 2, W, CA)
    done[1].start()
    scale = 1.0 / (64 * 16 * W) ** 0.5

    def gathered(msg, r3, sem, total):
        for d in range(1, 16):
            remote(msg.at[lax.rem(b + d, 16)], r3.at[d - 1], sem, d - 1, z_peer(d)).wait()
        same = msg[b].astype(F32)
        for d in range(2, 16, 2):
            same = same + r3[d - 1].astype(F32)
        other = r3[0].astype(F32)
        for d in range(3, 16, 2):
            other = other + r3[d - 1].astype(F32)
        total[core] = same * scale
        total[1 - core] = other * scale

    gathered(msg_a, r3a, sem3a, total_a)
    grad_a[...] = total_a[:, :, 0:216].reshape(32, 216)
    gathered(msg_b, r3b, sem3b, total_b)
    low = jnp.concatenate([total_b[0, 0:8], total_b[1, 0:8]], 0)
    grad_b[...] = low[:, 0:108]
    grad_p[...] = low.T[112:120]
    for halo in (halo_c, halo_v, halo_m, halo_g):
        halo.sent()
    for cp in done:
        cp.wait()


def written(*refs):
    took, gives, held, sem = refs[:5], refs[5:10], refs[10:15], refs[15]
    reads = [pltpu.make_async_copy(took[i], held[i], sem.at[0, i]) for i in range(5)]
    writes = [pltpu.make_async_copy(held[i], gives[i], sem.at[1, i]) for i in range(5)]
    for cp in reads:
        cp.start()
    for i in range(5):
        reads[i].wait()
        writes[i].start()
    for cp in writes:
        cp.wait()


def shards(video, kernel_a, project, kernel_b, cotangent):
    dma = pltpu.SemaphoreType.DMA
    vmem = pl.BlockSpec(memory_space=pltpu.VMEM)
    hbm = pl.BlockSpec(memory_space=pl.ANY)

    def group(lx, ly):
        return [
            pltpu.VMEM((4, 2, 2, 16, lx), BF16), pltpu.VMEM((4, 4, 16, ly), BF16),
            pltpu.VMEM((2, 2, 16, lx), BF16), pltpu.VMEM((2, 2, 16, ly), BF16),
            pltpu.VMEM((2, 2, 2, 16, lx), BF16), pltpu.VMEM((2, 4, 16, ly), BF16),
            pltpu.VMEM((4, 16, lx), BF16), pltpu.VMEM((4, 16, ly), BF16),
            pltpu.VMEM((3, 16, lx), BF16), pltpu.VMEM((3, 16, ly), BF16),
        ]

    results = pl.pallas_call(
        kernel,
        out_shape=[
            jax.ShapeDtypeStruct((2, 2, W, CB), F32),
            jax.ShapeDtypeStruct((2, 2, W, CA), F32),
            jax.ShapeDtypeStruct((32, 216), F32),
            jax.ShapeDtypeStruct((16, 108), F32),
            jax.ShapeDtypeStruct((8, 16), F32),
        ],
        in_specs=[hbm] * 5,
        out_specs=[hbm, hbm, vmem, vmem, vmem],
        scratch_shapes=[
            pltpu.VMEM((2, 2, W, CB), F32), pltpu.VMEM((2, 2, W, CA), F32),
            pltpu.VMEM((2, 2, W, CA), BF16), pltpu.VMEM((2, 2, W, CB), BF16), pltpu.VMEM((CA, CB), BF16),
            pltpu.VMEM((27 * CA, CA), BF16), pltpu.VMEM((27 * CB, CB), BF16),
            pltpu.VMEM((4, 4, W, CA), BF16), pltpu.VMEM((4, 4, W, CB), BF16),
            pltpu.VMEM((4, 4, W, CB), BF16), pltpu.VMEM((4, 4, W, CA), BF16),
            pltpu.VMEM((2, 2, W, CB), BF16), pltpu.VMEM((2, 2, W, CA), BF16),
            pltpu.VMEM((4, 4, W, 3 * CA), BF16), pltpu.VMEM((4, 4, W, 3 * CB), BF16),
            pltpu.VMEM((4, 4, W, 3 * CB), BF16), pltpu.VMEM((4, 4, W, 3 * CA), BF16),
            pltpu.VMEM((2, 8, 16, CELLS), BF16), pltpu.VMEM((2, 64, CELLS), BF16),
            pltpu.VMEM((9, 8, 16, 768), BF16), pltpu.VMEM((9, 8, 16, 768), BF16),
            pltpu.VMEM((9, 128, 768), F32),
            pltpu.VMEM((8, 2, 16, XB + YB), BF16), pltpu.VMEM((8, 2, 16, XB + YB), BF16),
            pltpu.VMEM((2, 8, 8, 27 * CB), F32),
            *group(XA, YA),
            *group(XB, YB),
            pltpu.VMEM((16, HALF_A), F32), pltpu.VMEM((16, XB + YB), F32),
            pltpu.VMEM((16, 16, 256), BF16), pltpu.VMEM((15, 16, 256), BF16), pltpu.VMEM((2, 16, 256), F32),
            pltpu.VMEM((16, 16, 128), BF16), pltpu.VMEM((15, 16, 128), BF16), pltpu.VMEM((2, 16, 128), F32),
            dma((5,)), dma((2, 5)), dma((2, 5)), dma((2, 5)), dma((2, 5)), dma((2, 9)), dma((2, 1)),
            *[dma((2, n)) for n in (12, 6, 3, 3, 12, 6, 3, 3, 15, 15)],
            dma((2,)),
        ],
        compiler_params=pltpu.CompilerParams(
            collective_id=0, has_side_effects=True, vmem_limit_bytes=56 * 1024 * 1024
        ),
    )(video, cotangent, kernel_a, project, kernel_b)
    results = pl.pallas_call(
        written,
        out_shape=[jax.ShapeDtypeStruct(r.shape, F32) for r in results],
        in_specs=[hbm] * 5,
        out_specs=[hbm] * 5,
        scratch_shapes=[*[pltpu.VMEM(r.shape, F32) for r in results], dma((2, 5))],
    )(*results)
    return results[0], results[1], results[2].T, results[3].T, results[4]


def solution(mesh):
    cells = P("tm", "rows", None, None)
    return jax.shard_map(
        shards,
        mesh=mesh,
        in_specs=(cells, P(), P(), P(), cells),
        out_specs=(cells, cells, P("tm", "rows"), P("tm", "rows"), P("tm", "rows")),
        check_vma=False,
    )
```

```python
import jax
import jax.numpy as jnp
from jax import lax
from jax.experimental import pallas as pl
from jax.experimental.pallas import tpu as pltpu
from jax.sharding import PartitionSpec as P

F32, BF16 = jnp.float32, jnp.bfloat16
MESH = pl.DeviceIdType.MESH
CA, CB, W = 256, 128, 96
CELLS = 4 * W
HALF_A = 27 * CA // 2
XA, YA = 1792, HALF_A - 1792
XB, YB = 512, 512
PB = 896
LAG = 3
ORDER = (1, 2, 3, 0)


def dot(a, b, ca=1, cb=0):
    return lax.dot_general(a, b, (((ca,), (cb,)), ((), ())), preferred_element_type=F32)


def kernel(
    video_hbm, cot_hbm, ka_hbm, project_hbm, kb_hbm,
    out_hbm, grad_video_hbm, grad_a, grad_b, grad_p,
    out, grad_video, video, cot, project, ka, kb, vbuf, cbuf, mbuf, gbuf, mown, gown, xs, us, ms, gs,
    gt, qt, send_a, recv_a, own_a, send_b, recv_b, part,
    s0xa, s0ya, q1xa, q1ya, r1xa, r1ya, s1xa, s1ya, r2ya, r2xa,
    s0xb, s0yb, q1xb, q1yb, r1xb, r1yb, s1xb, s1yb, r2yb, r2xb,
    t_a, t_b, msg_a, r3a, total_a, msg_b, r3b, total_b,
    sem_w, sem_v, sem_c, sem_m, sem_g, sem_a, sem_b,
    sem1xa, sem1ya, sem2ya, sem2xa, sem1xb, sem1yb, sem2yb, sem2xb, sem3a, sem3b, sem_o,
):
    tm = lax.axis_index("tm")
    rows = lax.axis_index("rows")
    core = lax.rem(tm, 2)
    b = lax.rem(tm, 16)
    y_lo = tm // 16
    x = lax.rem(rows, 4)
    y = (rows // 4) * 2 + y_lo
    upper, lower = rows > 0, rows < 7
    since, until = tm > 0, tm < 31

    def x_peer(d):
        return (tm, (rows // 4) * 4 + lax.rem(x + d, 4))

    def y_peer(d):
        to = lax.rem(y + d, 4)
        return (lax.rem(to, 2) * 16 + b, (to // 2) * 4 + x)

    def z_peer(d):
        return (y_lo * 16 + lax.rem(b + d, 16), rows)

    def near(dt, dr):
        return (lax.rem(tm + 32 + dt, 32), lax.rem(rows + 8 + dr, 8))

    partner = (tm + 1 - 2 * core, rows)

    def remote(src, dst, sem, slot, to):
        return pltpu.make_async_remote_copy(
            src_ref=src, dst_ref=dst, send_sem=sem.at[0, slot], recv_sem=sem.at[1, slot],
            device_id=to, device_id_type=MESH,
        )

    barrier = pltpu.get_barrier_semaphore()
    peers = [z_peer(d) for d in (8, 9, 7, 10, 6, 11, 5, 12, 4, 13, 3, 14, 2, 15, 1)]
    peers += [near(dt, dr) for dt, dr in ((0, 1), (0, -1), (1, 0), (-1, 0))]
    peers += [y_peer(d) for d in (2, 1, 3)] + [x_peer(d) for d in (2, 1, 3)]
    for to in peers:
        pl.semaphore_signal(barrier, inc=1, device_id=to, device_id_type=MESH)

    loads = [
        pltpu.make_async_copy(src, dst, sem_w.at[i])
        for i, (src, dst) in enumerate(
            ((cot_hbm, cot), (video_hbm, video), (kb_hbm, kb), (project_hbm, project), (ka_hbm, ka))
        )
    ]
    for cp in loads:
        cp.start()

    for buf, chan in ((vbuf, CA), (cbuf, CB), (mbuf, CB), (gbuf, CA)):

        @pl.when(rows == 0)
        def _():
            buf[:, 0] = jnp.zeros((4, W, chan), BF16)

        @pl.when(rows == 7)
        def _():
            buf[:, 3] = jnp.zeros((4, W, chan), BF16)

    @pl.when(tm == 0)
    def _():
        vbuf[0:2] = jnp.zeros((2, 4, W, CA), BF16)
        mbuf[0:2] = jnp.zeros((2, 4, W, CB), BF16)

    @pl.when(tm == 31)
    def _():
        cbuf[2:4] = jnp.zeros((2, 4, W, CB), BF16)
        gbuf[2:4] = jnp.zeros((2, 4, W, CA), BF16)

    class Halo:
        def __init__(self, src, buf, way, sem):
            own = 2 if way > 0 else 0
            mine, theirs = pl.ds(own, 2), pl.ds(2 - own, 2)
            self.gives, self.takes = (until, since) if way > 0 else (since, until)
            self.full = remote(src, buf.at[theirs, pl.ds(1, 2)], sem, 0, near(way, 0))
            self.down = remote(src.at[:, 1], buf.at[mine, 0], sem, 1, near(0, 1))
            self.up = remote(src.at[:, 0], buf.at[mine, 3], sem, 2, near(0, -1))
            self.top = remote(buf.at[mine, 0], buf.at[theirs, 0], sem, 3, near(way, 0))
            self.low = remote(buf.at[mine, 3], buf.at[theirs, 3], sem, 4, near(way, 0))
            self.gives_top, self.gives_low = self.gives & upper, self.gives & lower

        def rims(self):
            pl.when(lower)(self.down.start)
            pl.when(upper)(self.up.start)

        def ahead(self):
            pl.when(self.gives)(self.full.start)

        def corners(self):
            pl.when(self.gives_top)(self.top.start)
            pl.when(self.gives_low)(self.low.start)

        def wait_rims(self):
            pl.when(upper)(self.down.wait_recv)
            pl.when(lower)(self.up.wait_recv)

        def wait_ahead(self):
            pl.when(self.takes)(self.full.wait_recv)

        def wait_corners(self):
            pl.when(self.takes & upper)(self.top.wait_recv)
            pl.when(self.takes & lower)(self.low.wait_recv)

        def sent(self):
            pl.when(lower)(self.down.wait_send)
            pl.when(upper)(self.up.wait_send)
            pl.when(self.gives)(self.full.wait_send)
            pl.when(self.gives_top)(self.top.wait_send)
            pl.when(self.gives_low)(self.low.wait_send)

    class Shifts:
        def __init__(self, src, buf, dst, way, chan):
            self.own = 2 if way > 0 else 0
            self.src, self.buf, self.dst, self.chan = src, buf, dst, chan

        def make(self, frames, rows_of):
            chan, dst = self.chan, self.dst
            cell = lax.broadcasted_iota(jnp.int32, (W, chan), 0)
            first = self.own if frames == "own" else 2 - self.own
            for f in (first, first + 1):
                for r in rows_of:
                    if frames == "own" and 1 <= r <= 2:
                        v = self.src[f - self.own, r - 1]
                    else:
                        v = self.buf[f, r]
                    v = v.astype(F32)
                    dst[f, r, :, chan : 2 * chan] = v.astype(BF16)
                    left = jnp.where(cell == 0, 0.0, pltpu.roll(v, 1, 0))
                    right = jnp.where(cell == W - 1, 0.0, pltpu.roll(v, W - 1, 0))
                    dst[f, r, :, 0:chan] = left.astype(BF16)
                    dst[f, r, :, 2 * chan : 3 * chan] = right.astype(BF16)

    CENTRE, EDGE, PAST, CORNERS = (
        [(2, 1)], [(2, 0), (2, 2)], [(0, 1), (1, 1)], [(0, 0), (0, 2), (1, 0), (1, 2)],
    )

    def conv(acc, src, weight, chan, taps):
        for kt, kr in taps:
            at = (3 * kt + kr) * 3 * chan
            piece = src[kt : kt + 2, kr : kr + 2].reshape(CELLS, 3 * chan)
            term = dot(piece, weight[at : at + 3 * chan])
            acc = term if acc is None else acc + term
        return acc

    def back(acc, src, weight, chan, taps):
        for kt, kr in taps:
            for kc in range(3):
                at = (9 * kt + 3 * kr + kc) * chan
                piece = src[2 - kt : 4 - kt, 2 - kr : 4 - kr, :, (2 - kc) * chan : (3 - kc) * chan]
                term = dot(piece.reshape(CELLS, chan), weight[at : at + chan], 1, 1)
                acc = term if acc is None else acc + term
        return acc

    halo_c = Halo(cot_hbm, cbuf, -1, sem_c)
    halo_v = Halo(video_hbm, vbuf, 1, sem_v)
    shift_c = Shifts(cot, cbuf, us, -1, CB)
    shift_v = Shifts(video, vbuf, xs, 1, CA)

    pl.semaphore_wait(barrier, len(peers))
    halo_c.rims()
    halo_v.rims()
    halo_c.ahead()
    halo_v.ahead()
    loads[0].wait()
    loads[1].wait()
    shift_c.make("own", (1, 2))
    shift_v.make("own", (1, 2))
    loads[2].wait()
    loads[3].wait()
    back_b = back(None, us, kb, CB, CENTRE)
    loads[4].wait()
    pre = conv(None, xs, ka, CA, CENTRE)

    halo_c.wait_rims()
    halo_c.corners()
    halo_v.wait_rims()
    halo_v.corners()
    shift_c.make("own", (0, 3))
    back_b = back(back_b, us, kb, CB, EDGE)
    shift_v.make("own", (0, 3))
    pre = conv(pre, xs, ka, CA, EDGE)
    halo_c.wait_ahead()
    shift_c.make("other", (1, 2))
    back_b = back(back_b, us, kb, CB, PAST)
    halo_v.wait_ahead()
    shift_v.make("other", (1, 2))
    pre = conv(pre, xs, ka, CA, PAST)
    halo_c.wait_corners()
    shift_c.make("other", (0, 3))
    back_b = back(back_b, us, kb, CB, CORNERS)
    grad_mid = cot[...].reshape(CELLS, CB).astype(F32) + back_b
    mid_t = grad_mid.T
    for c in range(2):
        pick = [mid_t[16 * j + 8 * c : 16 * j + 8 * c + 8] for j in range(8)]
        qt[c] = jnp.concatenate(pick, 0).astype(BF16)
    grad_h = dot(grad_mid.astype(BF16), project[...], 1, 1)

    halo_v.wait_corners()
    shift_v.make("other", (0, 3))
    pre = conv(pre, xs, ka, CA, CORNERS)
    sig = jax.nn.sigmoid(pre)
    hidden = (pre * sig).astype(BF16)
    grad_pre = grad_h * sig * (1.0 + pre * (1.0 - sig))
    grad_t = grad_pre.T
    for c in range(2):
        for j in range(8):
            gt[c, j] = grad_t[32 * j + 16 * c : 32 * j + 16 * c + 16].astype(BF16)

    def chunk_a(left, k):
        kt, kr = k // 3, k % 3
        return dot(left, xs[kt : kt + 2, kr : kr + 2].reshape(CELLS, 3 * CA))

    class Group:
        def __init__(self, s0x, q1x, r1x, s1x, r2y, s0y, q1y, r1y, s1y, r2x, sem1x, sem1y, sem2y, sem2x):
            self.s0x, self.q1x, self.r1x, self.s1x, self.r2y = s0x, q1x, r1x, s1x, r2y
            self.s0y, self.q1y, self.r1y, self.s1y, self.r2x = s0y, q1y, r1y, s1y, r2x
            self.sem1x, self.sem1y, self.sem2y, self.sem2x = sem1x, sem1y, sem2y, sem2x

        def x_far(self, yl, h):
            src = self.s0x.at[lax.rem(x + 2, 4), yl, h]
            return remote(src, self.q1x.at[yl, h], self.sem1x, 6 * yl + h, x_peer((1, 3)[h]))

        def x_near(self, yl, side, h):
            d = (1, 3)[side]
            src = self.s0x.at[lax.rem(x + d, 4), yl, h]
            return remote(src, self.r1x.at[side, yl, h], self.sem1x, 6 * yl + 2 + 2 * side + h, x_peer(d))

        def y_far(self, h):
            src = self.s0y.at[lax.rem(y + 2, 4), pl.ds(2 * h, 2)]
            return remote(src, self.q1y.at[h], self.sem1y, h, y_peer((1, 3)[h]))

        def y_near(self, side, h):
            d = (1, 3)[side]
            src = self.s0y.at[lax.rem(y + d, 4), pl.ds(2 * h, 2)]
            return remote(src, self.r1y.at[side, pl.ds(2 * h, 2)], self.sem1y, 2 + 2 * side + h, y_peer(d))

        def y2(self, d):
            return remote(self.s1x.at[lax.rem(y + d, 4)], self.r2y.at[d - 1], self.sem2y, d - 1, y_peer(d))

        def x2(self, d):
            return remote(self.s1y.at[lax.rem(x + d, 4)], self.r2x.at[d - 1], self.sem2x, d - 1, x_peer(d))

        def send_x(self, yl):
            self.x_far(yl, 0).start()
            self.x_far(yl, 1).start()
            self.x_near(yl, 0, 1).start()
            self.x_near(yl, 1, 0).start()

        def send_y(self, yl):
            @pl.when(y_lo == yl)
            def _():
                self.y_far(0).start()
                self.y_far(1).start()

            @pl.when(y_lo != yl)
            def _():
                self.y_near(0, 1).start()
                self.y_near(1, 0).start()

        def relay_x(self, yl):
            for h in range(2):
                to = lax.rem(x + (1, 3)[h], 4)
                self.x_far(yl, h).wait_recv()
                both = self.s0x[to, yl, h].astype(F32) + self.q1x[yl, h].astype(F32)
                self.s0x[to, yl, h] = both.astype(BF16)
                self.x_near(yl, h, h).start()

        def relay_y(self):
            for h in range(2):
                to, part = lax.rem(y + (1, 3)[h], 4), slice(2 * h, 2 * h + 2)
                self.y_far(h).wait_recv()
                both = self.s0y[to, part].astype(F32) + self.q1y[h].astype(F32)
                self.s0y[to, part] = both.astype(BF16)
                self.y_near(h, h).start()

        def add_x(self, yl):
            for h in range(2):
                self.x_far(yl, h).wait_send()
                for side in range(2):
                    self.x_near(yl, side, h).wait()
            for yh in range(2):
                to = 2 * yh + yl
                acc = self.s0x[x, yl, yh].astype(F32)
                for side in range(2):
                    acc = acc + self.r1x[side, yl, yh].astype(F32)
                self.s1x[to] = acc.astype(BF16)
                d = lax.rem(to - y + 4, 4)

                @pl.when(d > 0)
                def _():
                    self.y2(d).start()

        def add_y(self):
            for h in range(2):
                self.y_far(h).wait_send()
                for side in range(2):
                    self.y_near(side, h).wait()
            for d in ORDER:
                to = lax.rem(x + d, 4)
                acc = self.s0y[y, to].astype(F32)
                for side in range(2):
                    acc = acc + self.r1y[side, to].astype(F32)
                self.s1y[to] = acc.astype(BF16)
                if d:
                    self.x2(d).start()

        def finish_x(self, t_ref, lx):
            for d in (1, 2, 3):
                self.y2(d).wait()
            acc = self.s1x[y].astype(F32)
            for s in range(3):
                acc = acc + self.r2y[s].astype(F32)
            t_ref[:, :lx] = acc

        def finish_y(self, t_ref, lx):
            for d in (1, 2, 3):
                self.x2(d).wait()
            acc = self.s1y[x].astype(F32)
            for s in range(3):
                acc = acc + self.r2x[s].astype(F32)
            t_ref[:, lx:] = acc

    group_a = Group(s0xa, q1xa, r1xa, s1xa, r2ya, s0ya, q1ya, r1ya, s1ya, r2xa, sem1xa, sem1ya, sem2ya, sem2xa)
    group_b = Group(s0xb, q1xb, r1xb, s1xb, r2yb, s0yb, q1yb, r1yb, s1yb, r2xb, sem1xb, sem1yb, sem2yb, sem2xb)

    left = jnp.concatenate([gt[1 - core].reshape(128, CELLS), gt[core].reshape(128, CELLS)], 0)
    cuts = sorted({768 * k for k in range(10)} | {0, XA, HALF_A, HALF_A + XA, 2 * HALF_A})
    copies_a = []
    mid = dot(hidden, project[...])
    mown[...] = mid.astype(BF16).reshape(2, 2, W, CB)
    halo_m = Halo(mown, mbuf, 1, sem_m)
    halo_m.rims()
    halo_m.ahead()
    gown[...] = grad_pre.astype(BF16).reshape(2, 2, W, CA)
    halo_g = Halo(gown, gbuf, -1, sem_g)
    halo_g.rims()
    halo_g.ahead()
    out[...] = mid.reshape(2, 2, W, CB)
    for step in range(9 + LAG):
        if step < 9:
            value = chunk_a(left, step)
            send_a[step] = value[0:128].astype(BF16).reshape(8, 16, 768)
            cp = remote(send_a.at[step], recv_a.at[step], sem_a, step, partner)
            cp.start()
            copies_a.append(cp)
            own_a[step] = value[128:256]
        k = step - LAG
        if k < 0:
            continue
        copies_a[k].wait()
        value = (own_a[k] + recv_a[k].reshape(128, 768).astype(F32)).astype(BF16)
        inside = [c for c in cuts if 768 * k <= c <= 768 * k + 768]
        for lo, hi in zip(inside[:-1], inside[1:]):
            yl, at = lo // HALF_A, lo % HALF_A
            for j in range(8):
                cut = value[16 * j : 16 * j + 16, lo - 768 * k : hi - 768 * k]
                if at < XA:
                    s0xa[j % 4, yl, j // 4, :, at : at + hi - lo] = cut
                else:
                    s0ya[(j // 4) * 2 + yl, j % 4, :, at - XA : at - XA + hi - lo] = cut
            if hi % HALF_A == XA:
                group_a.send_x(yl)
            if hi % HALF_A == 0:
                group_a.send_y(yl)

    mid_own = mid.T.astype(BF16)
    for k in range(9):
        kt, kr = k // 3, k % 3
        value = dot(mid_own, us[2 - kt : 4 - kt, 2 - kr : 4 - kr].reshape(CELLS, 3 * CB))
        for kc in range(3):
            tap = value[:, (2 - kc) * CB : (3 - kc) * CB].T
            at = (3 * k + kc) * CB
            for c in range(2):
                for j in range(8):
                    part[c, j, :, at : at + CB] = tap[16 * j + 8 * c : 16 * j + 8 * c + 8]

    def packed(half):
        proj = dot(qt[half], hidden)
        for j in range(8):
            for yl in range(2):
                at = 13 * CB * yl
                upper_half = part[half, j, :, at : at + PB]
                lower_half = part[half, j, :, at + PB : at + 2 * PB]
                body = jnp.concatenate([upper_half, lower_half], 0)
                tail = proj[8 * j : 8 * j + 8, 128 * yl : 128 * yl + 128]
                tail = jnp.concatenate([tail, jnp.zeros((8, 128), F32)], 0)
                yield j, yl, jnp.concatenate([body, tail], 1)

    for j, yl, value in packed(1 - core):
        send_b[j, yl] = value.astype(BF16)
    copy_b = remote(send_b, recv_b, sem_b, 0, partner)
    copy_b.start()
    copy_b.wait()
    for j, yl, value in packed(core):
        value = (value + recv_b[j, yl].astype(F32)).astype(BF16)
        s0xb[j % 4, yl, j // 4] = value[:, :XB]
        s0yb[(j // 4) * 2 + yl, j % 4] = value[:, XB:]
    for yl in range(2):
        group_b.send_x(yl)
    for yl in range(2):
        group_b.send_y(yl)
    halo_m.wait_rims()
    halo_m.corners()
    halo_g.wait_rims()
    halo_g.corners()
    for yl in range(2):
        group_a.relay_x(yl)
    group_a.relay_y()
    for yl in range(2):
        group_b.relay_x(yl)
    group_b.relay_y()
    every = CENTRE + EDGE + PAST + CORNERS
    shift_m = Shifts(mown, mbuf, ms, 1, CB)
    shift_m.make("own", (0, 1, 2, 3))
    halo_m.wait_ahead()
    halo_m.wait_corners()
    shift_m.make("other", (0, 1, 2, 3))
    out[...] = out[...] + conv(None, ms, kb, CB, every).reshape(2, 2, W, CB)
    done = [
        pltpu.make_async_copy(out, out_hbm, sem_o.at[0]),
        pltpu.make_async_copy(grad_video, grad_video_hbm, sem_o.at[1]),
    ]
    done[0].start()
    group_a.add_x(0)
    group_a.add_x(1)
    group_a.add_y()
    group_b.add_x(0)
    group_b.add_x(1)
    group_b.add_y()
    def give(msg, r3, sem, k):
        d = lax.rem(k - b + 16, 16)

        @pl.when(d > 0)
        def _():
            remote(msg.at[k], r3.at[d - 1], sem, d - 1, z_peer(d)).start()

    for k in range(16):
        if k == 0:
            group_a.finish_x(t_a, XA)
        if k == 8:
            group_a.finish_y(t_a, XA)
        block = t_a[:, 216 * k : 216 * k + 216]
        msg_a[k] = jnp.concatenate([block, jnp.zeros((16, 40), F32)], 1).astype(BF16)
        give(msg_a, r3a, sem3a, k)
    group_b.finish_x(t_b, XB)
    group_b.finish_y(t_b, XB)
    part_b = jnp.concatenate([t_b[0:8, 0:PB], t_b[8:16, 0:PB]], 1)
    part_b = jnp.where(y_lo == 0, part_b[:, 0:1728], part_b[:, 64:1792])
    part_p = t_b[0:8, PB : PB + 128]
    for k in range(16):
        low = jnp.concatenate(
            [
                part_b[:, 108 * k : 108 * k + 108], jnp.zeros((8, 4), F32),
                part_p[:, 8 * k : 8 * k + 8], jnp.zeros((8, 8), F32),
            ], 1,
        )
        msg_b[k] = jnp.concatenate([low, jnp.zeros((8, 128), F32)], 0).astype(BF16)
        give(msg_b, r3b, sem3b, k)
    shift_g = Shifts(gown, gbuf, gs, -1, CA)
    shift_g.make("own", (0, 1, 2, 3))
    halo_g.wait_ahead()
    halo_g.wait_corners()
    shift_g.make("other", (0, 1, 2, 3))
    grad_video[...] = back(None, gs, ka, CA, every).reshape(2, 2, W, CA)
    done[1].start()
    scale = 1.0 / (64 * 16 * W) ** 0.5

    def gathered(msg, r3, sem, total):
        for d in range(1, 16):
            remote(msg.at[lax.rem(b + d, 16)], r3.at[d - 1], sem, d - 1, z_peer(d)).wait()
        same = msg[b].astype(F32)
        for d in range(2, 16, 2):
            same = same + r3[d - 1].astype(F32)
        other = r3[0].astype(F32)
        for d in range(3, 16, 2):
            other = other + r3[d - 1].astype(F32)
        total[core] = same * scale
        total[1 - core] = other * scale

    gathered(msg_a, r3a, sem3a, total_a)
    grad_a[...] = total_a[:, :, 0:216].reshape(32, 216)
    gathered(msg_b, r3b, sem3b, total_b)
    low = jnp.concatenate([total_b[0, 0:8], total_b[1, 0:8]], 0)
    grad_b[...] = low[:, 0:108]
    grad_p[...] = low.T[112:120]
    for halo in (halo_c, halo_v, halo_m, halo_g):
        halo.sent()
    for cp in done:
        cp.wait()


def written(*refs):
    took, gives, held, sem = refs[:5], refs[5:10], refs[10:15], refs[15]
    reads = [pltpu.make_async_copy(took[i], held[i], sem.at[0, i]) for i in range(5)]
    writes = [pltpu.make_async_copy(held[i], gives[i], sem.at[1, i]) for i in range(5)]
    for cp in reads:
        cp.start()
    for i in range(5):
        reads[i].wait()
        writes[i].start()
    for cp in writes:
        cp.wait()


def shards(video, kernel_a, project, kernel_b, cotangent):
    dma = pltpu.SemaphoreType.DMA
    vmem = pl.BlockSpec(memory_space=pltpu.VMEM)
    hbm = pl.BlockSpec(memory_space=pl.ANY)

    def group(lx, ly):
        return [
            pltpu.VMEM((4, 2, 2, 16, lx), BF16), pltpu.VMEM((4, 4, 16, ly), BF16),
            pltpu.VMEM((2, 2, 16, lx), BF16), pltpu.VMEM((2, 2, 16, ly), BF16),
            pltpu.VMEM((2, 2, 2, 16, lx), BF16), pltpu.VMEM((2, 4, 16, ly), BF16),
            pltpu.VMEM((4, 16, lx), BF16), pltpu.VMEM((4, 16, ly), BF16),
            pltpu.VMEM((3, 16, lx), BF16), pltpu.VMEM((3, 16, ly), BF16),
        ]

    results = pl.pallas_call(
        kernel,
        out_shape=[
            jax.ShapeDtypeStruct((2, 2, W, CB), F32),
            jax.ShapeDtypeStruct((2, 2, W, CA), F32),
            jax.ShapeDtypeStruct((32, 216), F32),
            jax.ShapeDtypeStruct((16, 108), F32),
            jax.ShapeDtypeStruct((8, 16), F32),
        ],
        in_specs=[hbm] * 5,
        out_specs=[hbm, hbm, vmem, vmem, vmem],
        scratch_shapes=[
            pltpu.VMEM((2, 2, W, CB), F32), pltpu.VMEM((2, 2, W, CA), F32),
            pltpu.VMEM((2, 2, W, CA), BF16), pltpu.VMEM((2, 2, W, CB), BF16), pltpu.VMEM((CA, CB), BF16),
            pltpu.VMEM((27 * CA, CA), BF16), pltpu.VMEM((27 * CB, CB), BF16),
            pltpu.VMEM((4, 4, W, CA), BF16), pltpu.VMEM((4, 4, W, CB), BF16),
            pltpu.VMEM((4, 4, W, CB), BF16), pltpu.VMEM((4, 4, W, CA), BF16),
            pltpu.VMEM((2, 2, W, CB), BF16), pltpu.VMEM((2, 2, W, CA), BF16),
            pltpu.VMEM((4, 4, W, 3 * CA), BF16), pltpu.VMEM((4, 4, W, 3 * CB), BF16),
            pltpu.VMEM((4, 4, W, 3 * CB), BF16), pltpu.VMEM((4, 4, W, 3 * CA), BF16),
            pltpu.VMEM((2, 8, 16, CELLS), BF16), pltpu.VMEM((2, 64, CELLS), BF16),
            pltpu.VMEM((9, 8, 16, 768), BF16), pltpu.VMEM((9, 8, 16, 768), BF16),
            pltpu.VMEM((9, 128, 768), F32),
            pltpu.VMEM((8, 2, 16, XB + YB), BF16), pltpu.VMEM((8, 2, 16, XB + YB), BF16),
            pltpu.VMEM((2, 8, 8, 27 * CB), F32),
            *group(XA, YA),
            *group(XB, YB),
            pltpu.VMEM((16, HALF_A), F32), pltpu.VMEM((16, XB + YB), F32),
            pltpu.VMEM((16, 16, 256), BF16), pltpu.VMEM((15, 16, 256), BF16), pltpu.VMEM((2, 16, 256), F32),
            pltpu.VMEM((16, 16, 128), BF16), pltpu.VMEM((15, 16, 128), BF16), pltpu.VMEM((2, 16, 128), F32),
            dma((5,)), dma((2, 5)), dma((2, 5)), dma((2, 5)), dma((2, 5)), dma((2, 9)), dma((2, 1)),
            *[dma((2, n)) for n in (12, 6, 3, 3, 12, 6, 3, 3, 15, 15)],
            dma((2,)),
        ],
        compiler_params=pltpu.CompilerParams(
            collective_id=0, has_side_effects=True, vmem_limit_bytes=56 * 1024 * 1024
        ),
    )(video, cotangent, kernel_a, project, kernel_b)
    results = pl.pallas_call(
        written,
        out_shape=[jax.ShapeDtypeStruct(r.shape, F32) for r in results],
        in_specs=[hbm] * 5,
        out_specs=[hbm] * 5,
        scratch_shapes=[*[pltpu.VMEM(r.shape, F32) for r in results], dma((2, 5))],
    )(*results)
    return results[0], results[1], results[2].T, results[3].T, results[4]


def solution(mesh):
    cells = P("tm", "rows", None, None)
    return jax.shard_map(
        shards,
        mesh=mesh,
        in_specs=(cells, P(), P(), P(), cells),
        out_specs=(cells, cells, P("tm", "rows"), P("tm", "rows"), P("tm", "rows")),
        check_vma=False,
    )
```

```python
import jax
import jax.numpy as jnp
from jax import lax
from jax.experimental import pallas as pl
from jax.experimental.pallas import tpu as pltpu
from jax.sharding import PartitionSpec as P

F32, BF16 = jnp.float32, jnp.bfloat16
MESH = pl.DeviceIdType.MESH
CA, CB, W = 256, 128, 96
CELLS = 4 * W
HALF_A = 27 * CA // 2
XA, YA = 1792, HALF_A - 1792
XB, YB = 512, 512
PB = 896
LAG = 3
ORDER = (1, 2, 3, 0)


def dot(a, b, ca=1, cb=0):
    return lax.dot_general(a, b, (((ca,), (cb,)), ((), ())), preferred_element_type=F32)


def kernel(
    video_hbm, cot_hbm, ka_hbm, project_hbm, kb_hbm,
    out_hbm, grad_video_hbm, grad_a, grad_b, grad_p,
    out, grad_video, video, cot, project, ka, kb, vbuf, cbuf, mbuf, gbuf, mown, gown, xs, us, ms, gs,
    gt, qt, send_a, recv_a, own_a, send_b, recv_b, part,
    s0xa, s0ya, q1xa, q1ya, r1xa, r1ya, s1xa, s1ya, r2ya, r2xa,
    s0xb, s0yb, q1xb, q1yb, r1xb, r1yb, s1xb, s1yb, r2yb, r2xb,
    t_a, t_b, msg_a, r3a, total_a, msg_b, r3b, total_b,
    sem_w, sem_v, sem_c, sem_m, sem_g, sem_a, sem_b,
    sem1xa, sem1ya, sem2ya, sem2xa, sem1xb, sem1yb, sem2yb, sem2xb, sem3a, sem3b, sem_o,
):
    tm = lax.axis_index("tm")
    rows = lax.axis_index("rows")
    core = lax.rem(tm, 2)
    b = lax.rem(tm, 16)
    y_lo = tm // 16
    x = lax.rem(rows, 4)
    y = (rows // 4) * 2 + y_lo
    upper, lower = rows > 0, rows < 7
    since, until = tm > 0, tm < 31

    def x_peer(d):
        return (tm, (rows // 4) * 4 + lax.rem(x + d, 4))

    def y_peer(d):
        to = lax.rem(y + d, 4)
        return (lax.rem(to, 2) * 16 + b, (to // 2) * 4 + x)

    def z_peer(d):
        return (y_lo * 16 + lax.rem(b + d, 16), rows)

    def near(dt, dr):
        return (lax.rem(tm + 32 + dt, 32), lax.rem(rows + 8 + dr, 8))

    partner = (tm + 1 - 2 * core, rows)

    def remote(src, dst, sem, slot, to):
        return pltpu.make_async_remote_copy(
            src_ref=src, dst_ref=dst, send_sem=sem.at[0, slot], recv_sem=sem.at[1, slot],
            device_id=to, device_id_type=MESH,
        )

    barrier = pltpu.get_barrier_semaphore()
    peers = [z_peer(d) for d in (8, 9, 7, 10, 6, 11, 5, 12, 4, 13, 3, 14, 2, 15, 1)]
    peers += [near(dt, dr) for dt, dr in ((0, 1), (0, -1), (1, 0), (-1, 0))]
    peers += [y_peer(d) for d in (2, 1, 3)] + [x_peer(d) for d in (2, 1, 3)]
    for to in peers:
        pl.semaphore_signal(barrier, inc=1, device_id=to, device_id_type=MESH)

    loads = [
        pltpu.make_async_copy(src, dst, sem_w.at[i])
        for i, (src, dst) in enumerate(
            ((cot_hbm, cot), (video_hbm, video), (kb_hbm, kb), (project_hbm, project), (ka_hbm, ka))
        )
    ]
    for cp in loads:
        cp.start()

    for buf, chan in ((vbuf, CA), (cbuf, CB), (mbuf, CB), (gbuf, CA)):

        @pl.when(rows == 0)
        def _():
            buf[:, 0] = jnp.zeros((4, W, chan), BF16)

        @pl.when(rows == 7)
        def _():
            buf[:, 3] = jnp.zeros((4, W, chan), BF16)

    @pl.when(tm == 0)
    def _():
        vbuf[0:2] = jnp.zeros((2, 4, W, CA), BF16)
        mbuf[0:2] = jnp.zeros((2, 4, W, CB), BF16)

    @pl.when(tm == 31)
    def _():
        cbuf[2:4] = jnp.zeros((2, 4, W, CB), BF16)
        gbuf[2:4] = jnp.zeros((2, 4, W, CA), BF16)

    class Halo:
        def __init__(self, src, buf, way, sem):
            own = 2 if way > 0 else 0
            mine, theirs = pl.ds(own, 2), pl.ds(2 - own, 2)
            self.gives, self.takes = (until, since) if way > 0 else (since, until)
            self.full = remote(src, buf.at[theirs, pl.ds(1, 2)], sem, 0, near(way, 0))
            self.down = remote(src.at[:, 1], buf.at[mine, 0], sem, 1, near(0, 1))
            self.up = remote(src.at[:, 0], buf.at[mine, 3], sem, 2, near(0, -1))
            self.top = remote(buf.at[mine, 0], buf.at[theirs, 0], sem, 3, near(way, 0))
            self.low = remote(buf.at[mine, 3], buf.at[theirs, 3], sem, 4, near(way, 0))
            self.gives_top, self.gives_low = self.gives & upper, self.gives & lower

        def rims(self):
            pl.when(lower)(self.down.start)
            pl.when(upper)(self.up.start)

        def ahead(self):
            pl.when(self.gives)(self.full.start)

        def corners(self):
            pl.when(self.gives_top)(self.top.start)
            pl.when(self.gives_low)(self.low.start)

        def wait_rims(self):
            pl.when(upper)(self.down.wait_recv)
            pl.when(lower)(self.up.wait_recv)

        def wait_ahead(self):
            pl.when(self.takes)(self.full.wait_recv)

        def wait_corners(self):
            pl.when(self.takes & upper)(self.top.wait_recv)
            pl.when(self.takes & lower)(self.low.wait_recv)

        def sent(self):
            pl.when(lower)(self.down.wait_send)
            pl.when(upper)(self.up.wait_send)
            pl.when(self.gives)(self.full.wait_send)
            pl.when(self.gives_top)(self.top.wait_send)
            pl.when(self.gives_low)(self.low.wait_send)

    class Shifts:
        def __init__(self, src, buf, dst, way, chan):
            self.own = 2 if way > 0 else 0
            self.src, self.buf, self.dst, self.chan = src, buf, dst, chan

        def make(self, frames, rows_of):
            chan, dst = self.chan, self.dst
            cell = lax.broadcasted_iota(jnp.int32, (W, chan), 0)
            first = self.own if frames == "own" else 2 - self.own
            for f in (first, first + 1):
                for r in rows_of:
                    if frames == "own" and 1 <= r <= 2:
                        v = self.src[f - self.own, r - 1]
                    else:
                        v = self.buf[f, r]
                    v = v.astype(F32)
                    dst[f, r, :, chan : 2 * chan] = v.astype(BF16)
                    left = jnp.where(cell == 0, 0.0, pltpu.roll(v, 1, 0))
                    right = jnp.where(cell == W - 1, 0.0, pltpu.roll(v, W - 1, 0))
                    dst[f, r, :, 0:chan] = left.astype(BF16)
                    dst[f, r, :, 2 * chan : 3 * chan] = right.astype(BF16)

    CENTRE, EDGE, PAST, CORNERS = (
        [(2, 1)], [(2, 0), (2, 2)], [(0, 1), (1, 1)], [(0, 0), (0, 2), (1, 0), (1, 2)],
    )

    def conv(acc, src, weight, chan, taps):
        for kt, kr in taps:
            at = (3 * kt + kr) * 3 * chan
            piece = src[kt : kt + 2, kr : kr + 2].reshape(CELLS, 3 * chan)
            term = dot(piece, weight[at : at + 3 * chan])
            acc = term if acc is None else acc + term
        return acc

    def back(acc, src, weight, chan, taps):
        for kt, kr in taps:
            for kc in range(3):
                at = (9 * kt + 3 * kr + kc) * chan
                piece = src[2 - kt : 4 - kt, 2 - kr : 4 - kr, :, (2 - kc) * chan : (3 - kc) * chan]
                term = dot(piece.reshape(CELLS, chan), weight[at : at + chan], 1, 1)
                acc = term if acc is None else acc + term
        return acc

    halo_c = Halo(cot_hbm, cbuf, -1, sem_c)
    halo_v = Halo(video_hbm, vbuf, 1, sem_v)
    shift_c = Shifts(cot, cbuf, us, -1, CB)
    shift_v = Shifts(video, vbuf, xs, 1, CA)

    pl.semaphore_wait(barrier, len(peers))
    halo_c.rims()
    halo_v.rims()
    halo_c.ahead()
    halo_v.ahead()
    loads[0].wait()
    loads[1].wait()
    shift_c.make("own", (1, 2))
    shift_v.make("own", (1, 2))
    loads[2].wait()
    loads[3].wait()
    back_b = back(None, us, kb, CB, CENTRE)
    loads[4].wait()
    pre = conv(None, xs, ka, CA, CENTRE)

    halo_c.wait_rims()
    halo_c.corners()
    halo_v.wait_rims()
    halo_v.corners()
    shift_c.make("own", (0, 3))
    back_b = back(back_b, us, kb, CB, EDGE)
    shift_v.make("own", (0, 3))
    pre = conv(pre, xs, ka, CA, EDGE)
    halo_c.wait_ahead()
    shift_c.make("other", (1, 2))
    back_b = back(back_b, us, kb, CB, PAST)
    halo_v.wait_ahead()
    shift_v.make("other", (1, 2))
    pre = conv(pre, xs, ka, CA, PAST)
    halo_c.wait_corners()
    shift_c.make("other", (0, 3))
    back_b = back(back_b, us, kb, CB, CORNERS)
    grad_mid = cot[...].reshape(CELLS, CB).astype(F32) + back_b
    grad_h = dot(grad_mid.astype(BF16), project[...], 1, 1)

    halo_v.wait_corners()
    shift_v.make("other", (0, 3))
    pre = conv(pre, xs, ka, CA, CORNERS)
    sig = jax.nn.sigmoid(pre)
    hidden = (pre * sig).astype(BF16)
    grad_pre = grad_h * sig * (1.0 + pre * (1.0 - sig))
    grad_t = grad_pre.T
    for c in range(2):
        for j in range(8):
            gt[c, j] = grad_t[32 * j + 16 * c : 32 * j + 16 * c + 16].astype(BF16)

    def chunk_a(left, k):
        kt, kr = k // 3, k % 3
        return dot(left, xs[kt : kt + 2, kr : kr + 2].reshape(CELLS, 3 * CA))

    class Group:
        def __init__(self, s0x, q1x, r1x, s1x, r2y, s0y, q1y, r1y, s1y, r2x, sem1x, sem1y, sem2y, sem2x):
            self.s0x, self.q1x, self.r1x, self.s1x, self.r2y = s0x, q1x, r1x, s1x, r2y
            self.s0y, self.q1y, self.r1y, self.s1y, self.r2x = s0y, q1y, r1y, s1y, r2x
            self.sem1x, self.sem1y, self.sem2y, self.sem2x = sem1x, sem1y, sem2y, sem2x

        def x_far(self, yl, h):
            src = self.s0x.at[lax.rem(x + 2, 4), yl, h]
            return remote(src, self.q1x.at[yl, h], self.sem1x, 6 * yl + h, x_peer((1, 3)[h]))

        def x_near(self, yl, side, h):
            d = (1, 3)[side]
            src = self.s0x.at[lax.rem(x + d, 4), yl, h]
            return remote(src, self.r1x.at[side, yl, h], self.sem1x, 6 * yl + 2 + 2 * side + h, x_peer(d))

        def y_far(self, h):
            src = self.s0y.at[lax.rem(y + 2, 4), pl.ds(2 * h, 2)]
            return remote(src, self.q1y.at[h], self.sem1y, h, y_peer((1, 3)[h]))

        def y_near(self, side, h):
            d = (1, 3)[side]
            src = self.s0y.at[lax.rem(y + d, 4), pl.ds(2 * h, 2)]
            return remote(src, self.r1y.at[side, pl.ds(2 * h, 2)], self.sem1y, 2 + 2 * side + h, y_peer(d))

        def y2(self, d):
            return remote(self.s1x.at[lax.rem(y + d, 4)], self.r2y.at[d - 1], self.sem2y, d - 1, y_peer(d))

        def x2(self, d):
            return remote(self.s1y.at[lax.rem(x + d, 4)], self.r2x.at[d - 1], self.sem2x, d - 1, x_peer(d))

        def send_x(self, yl):
            self.x_far(yl, 0).start()
            self.x_far(yl, 1).start()
            self.x_near(yl, 0, 1).start()
            self.x_near(yl, 1, 0).start()

        def send_y(self, yl):
            @pl.when(y_lo == yl)
            def _():
                self.y_far(0).start()
                self.y_far(1).start()

            @pl.when(y_lo != yl)
            def _():
                self.y_near(0, 1).start()
                self.y_near(1, 0).start()

        def relay_x(self, yl):
            for h in range(2):
                to = lax.rem(x + (1, 3)[h], 4)
                self.x_far(yl, h).wait_recv()
                both = self.s0x[to, yl, h].astype(F32) + self.q1x[yl, h].astype(F32)
                self.s0x[to, yl, h] = both.astype(BF16)
                self.x_near(yl, h, h).start()

        def relay_y(self):
            for h in range(2):
                to, part = lax.rem(y + (1, 3)[h], 4), slice(2 * h, 2 * h + 2)
                self.y_far(h).wait_recv()
                both = self.s0y[to, part].astype(F32) + self.q1y[h].astype(F32)
                self.s0y[to, part] = both.astype(BF16)
                self.y_near(h, h).start()

        def add_x(self, yl):
            for h in range(2):
                self.x_far(yl, h).wait_send()
                for side in range(2):
                    self.x_near(yl, side, h).wait()
            for yh in range(2):
                to = 2 * yh + yl
                acc = self.s0x[x, yl, yh].astype(F32)
                for side in range(2):
                    acc = acc + self.r1x[side, yl, yh].astype(F32)
                self.s1x[to] = acc.astype(BF16)
                d = lax.rem(to - y + 4, 4)

                @pl.when(d > 0)
                def _():
                    self.y2(d).start()

        def add_y(self):
            for h in range(2):
                self.y_far(h).wait_send()
                for side in range(2):
                    self.y_near(side, h).wait()
            for d in ORDER:
                to = lax.rem(x + d, 4)
                acc = self.s0y[y, to].astype(F32)
                for side in range(2):
                    acc = acc + self.r1y[side, to].astype(F32)
                self.s1y[to] = acc.astype(BF16)
                if d:
                    self.x2(d).start()

        def finish_x(self, t_ref, lx):
            for d in (1, 2, 3):
                self.y2(d).wait()
            acc = self.s1x[y].astype(F32)
            for s in range(3):
                acc = acc + self.r2y[s].astype(F32)
            t_ref[:, :lx] = acc

        def finish_y(self, t_ref, lx):
            for d in (1, 2, 3):
                self.x2(d).wait()
            acc = self.s1y[x].astype(F32)
            for s in range(3):
                acc = acc + self.r2x[s].astype(F32)
            t_ref[:, lx:] = acc

    group_a = Group(s0xa, q1xa, r1xa, s1xa, r2ya, s0ya, q1ya, r1ya, s1ya, r2xa, sem1xa, sem1ya, sem2ya, sem2xa)
    group_b = Group(s0xb, q1xb, r1xb, s1xb, r2yb, s0yb, q1yb, r1yb, s1yb, r2xb, sem1xb, sem1yb, sem2yb, sem2xb)

    left = jnp.concatenate([gt[1 - core].reshape(128, CELLS), gt[core].reshape(128, CELLS)], 0)
    cuts = sorted({768 * k for k in range(10)} | {0, XA, HALF_A, HALF_A + XA, 2 * HALF_A})
    copies_a = []
    mid = dot(hidden, project[...])
    mown[...] = mid.astype(BF16).reshape(2, 2, W, CB)
    halo_m = Halo(mown, mbuf, 1, sem_m)
    halo_m.rims()
    halo_m.ahead()
    gown[...] = grad_pre.astype(BF16).reshape(2, 2, W, CA)
    halo_g = Halo(gown, gbuf, -1, sem_g)
    halo_g.rims()
    halo_g.ahead()
    out[...] = mid.reshape(2, 2, W, CB)
    for step in range(9 + LAG):
        if step < 9:
            value = chunk_a(left, step)
            send_a[step] = value[0:128].astype(BF16).reshape(8, 16, 768)
            cp = remote(send_a.at[step], recv_a.at[step], sem_a, step, partner)
            cp.start()
            copies_a.append(cp)
            own_a[step] = value[128:256]
        k = step - LAG
        if k < 0:
            continue
        copies_a[k].wait()
        value = (own_a[k] + recv_a[k].reshape(128, 768).astype(F32)).astype(BF16)
        inside = [c for c in cuts if 768 * k <= c <= 768 * k + 768]
        for lo, hi in zip(inside[:-1], inside[1:]):
            yl, at = lo // HALF_A, lo % HALF_A
            for j in range(8):
                cut = value[16 * j : 16 * j + 16, lo - 768 * k : hi - 768 * k]
                if at < XA:
                    s0xa[j % 4, yl, j // 4, :, at : at + hi - lo] = cut
                else:
                    s0ya[(j // 4) * 2 + yl, j % 4, :, at - XA : at - XA + hi - lo] = cut
            if hi % HALF_A == XA:
                group_a.send_x(yl)
            if hi % HALF_A == 0:
                group_a.send_y(yl)

    mid_t = grad_mid.T
    for c in range(2):
        pick = [mid_t[16 * j + 8 * c : 16 * j + 8 * c + 8] for j in range(8)]
        qt[c] = jnp.concatenate(pick, 0).astype(BF16)
    mid_own = mid.T.astype(BF16)
    for k in range(9):
        kt, kr = k // 3, k % 3
        value = dot(mid_own, us[2 - kt : 4 - kt, 2 - kr : 4 - kr].reshape(CELLS, 3 * CB))
        for kc in range(3):
            tap = value[:, (2 - kc) * CB : (3 - kc) * CB].T
            at = (3 * k + kc) * CB
            for c in range(2):
                for j in range(8):
                    part[c, j, :, at : at + CB] = tap[16 * j + 8 * c : 16 * j + 8 * c + 8]

    def packed(half):
        proj = dot(qt[half], hidden)
        for j in range(8):
            for yl in range(2):
                at = 13 * CB * yl
                upper_half = part[half, j, :, at : at + PB]
                lower_half = part[half, j, :, at + PB : at + 2 * PB]
                body = jnp.concatenate([upper_half, lower_half], 0)
                tail = proj[8 * j : 8 * j + 8, 128 * yl : 128 * yl + 128]
                tail = jnp.concatenate([tail, jnp.zeros((8, 128), F32)], 0)
                yield j, yl, jnp.concatenate([body, tail], 1)

    for j, yl, value in packed(1 - core):
        send_b[j, yl] = value.astype(BF16)
    copy_b = remote(send_b, recv_b, sem_b, 0, partner)
    copy_b.start()
    copy_b.wait()
    for j, yl, value in packed(core):
        value = (value + recv_b[j, yl].astype(F32)).astype(BF16)
        s0xb[j % 4, yl, j // 4] = value[:, :XB]
        s0yb[(j // 4) * 2 + yl, j % 4] = value[:, XB:]
    for yl in range(2):
        group_b.send_x(yl)
    for yl in range(2):
        group_b.send_y(yl)
    halo_m.wait_rims()
    halo_m.corners()
    halo_g.wait_rims()
    halo_g.corners()
    for yl in range(2):
        group_a.relay_x(yl)
    group_a.relay_y()
    for yl in range(2):
        group_b.relay_x(yl)
    group_b.relay_y()
    every = CENTRE + EDGE + PAST + CORNERS
    shift_m = Shifts(mown, mbuf, ms, 1, CB)
    shift_m.make("own", (0, 1, 2, 3))
    halo_m.wait_ahead()
    halo_m.wait_corners()
    shift_m.make("other", (0, 1, 2, 3))
    out[...] = out[...] + conv(None, ms, kb, CB, every).reshape(2, 2, W, CB)
    done = [
        pltpu.make_async_copy(out, out_hbm, sem_o.at[0]),
        pltpu.make_async_copy(grad_video, grad_video_hbm, sem_o.at[1]),
    ]
    done[0].start()
    group_a.add_x(0)
    group_a.add_x(1)
    group_a.add_y()
    group_b.add_x(0)
    group_b.add_x(1)
    group_b.add_y()
    def give(msg, r3, sem, k):
        d = lax.rem(k - b + 16, 16)

        @pl.when(d > 0)
        def _():
            remote(msg.at[k], r3.at[d - 1], sem, d - 1, z_peer(d)).start()

    for k in range(16):
        if k == 0:
            group_a.finish_x(t_a, XA)
        if k == 8:
            group_a.finish_y(t_a, XA)
        block = t_a[:, 216 * k : 216 * k + 216]
        msg_a[k] = jnp.concatenate([block, jnp.zeros((16, 40), F32)], 1).astype(BF16)
        give(msg_a, r3a, sem3a, k)
    group_b.finish_x(t_b, XB)
    group_b.finish_y(t_b, XB)
    part_b = jnp.concatenate([t_b[0:8, 0:PB], t_b[8:16, 0:PB]], 1)
    part_b = jnp.where(y_lo == 0, part_b[:, 0:1728], part_b[:, 64:1792])
    part_p = t_b[0:8, PB : PB + 128]
    for k in range(16):
        low = jnp.concatenate(
            [
                part_b[:, 108 * k : 108 * k + 108], jnp.zeros((8, 4), F32),
                part_p[:, 8 * k : 8 * k + 8], jnp.zeros((8, 8), F32),
            ], 1,
        )
        msg_b[k] = jnp.concatenate([low, jnp.zeros((8, 128), F32)], 0).astype(BF16)
        give(msg_b, r3b, sem3b, k)
    shift_g = Shifts(gown, gbuf, gs, -1, CA)
    shift_g.make("own", (0, 1, 2, 3))
    halo_g.wait_ahead()
    halo_g.wait_corners()
    shift_g.make("other", (0, 1, 2, 3))
    grad_video[...] = back(None, gs, ka, CA, every).reshape(2, 2, W, CA)
    done[1].start()
    scale = 1.0 / (64 * 16 * W) ** 0.5

    def gathered(msg, r3, sem, total):
        for d in range(1, 16):
            remote(msg.at[lax.rem(b + d, 16)], r3.at[d - 1], sem, d - 1, z_peer(d)).wait()
        same = msg[b].astype(F32)
        for d in range(2, 16, 2):
            same = same + r3[d - 1].astype(F32)
        other = r3[0].astype(F32)
        for d in range(3, 16, 2):
            other = other + r3[d - 1].astype(F32)
        total[core] = same * scale
        total[1 - core] = other * scale

    gathered(msg_a, r3a, sem3a, total_a)
    grad_a[...] = total_a[:, :, 0:216].reshape(32, 216)
    gathered(msg_b, r3b, sem3b, total_b)
    low = jnp.concatenate([total_b[0, 0:8], total_b[1, 0:8]], 0)
    grad_b[...] = low[:, 0:108]
    grad_p[...] = low.T[112:120]
    for halo in (halo_c, halo_v, halo_m, halo_g):
        halo.sent()
    for cp in done:
        cp.wait()


def written(*refs):
    took, gives, held, sem = refs[:5], refs[5:10], refs[10:15], refs[15]
    reads = [pltpu.make_async_copy(took[i], held[i], sem.at[0, i]) for i in range(5)]
    writes = [pltpu.make_async_copy(held[i], gives[i], sem.at[1, i]) for i in range(5)]
    for cp in reads:
        cp.start()
    for i in range(5):
        reads[i].wait()
        writes[i].start()
    for cp in writes:
        cp.wait()


def shards(video, kernel_a, project, kernel_b, cotangent):
    dma = pltpu.SemaphoreType.DMA
    vmem = pl.BlockSpec(memory_space=pltpu.VMEM)
    hbm = pl.BlockSpec(memory_space=pl.ANY)

    def group(lx, ly):
        return [
            pltpu.VMEM((4, 2, 2, 16, lx), BF16), pltpu.VMEM((4, 4, 16, ly), BF16),
            pltpu.VMEM((2, 2, 16, lx), BF16), pltpu.VMEM((2, 2, 16, ly), BF16),
            pltpu.VMEM((2, 2, 2, 16, lx), BF16), pltpu.VMEM((2, 4, 16, ly), BF16),
            pltpu.VMEM((4, 16, lx), BF16), pltpu.VMEM((4, 16, ly), BF16),
            pltpu.VMEM((3, 16, lx), BF16), pltpu.VMEM((3, 16, ly), BF16),
        ]

    results = pl.pallas_call(
        kernel,
        out_shape=[
            jax.ShapeDtypeStruct((2, 2, W, CB), F32),
            jax.ShapeDtypeStruct((2, 2, W, CA), F32),
            jax.ShapeDtypeStruct((32, 216), F32),
            jax.ShapeDtypeStruct((16, 108), F32),
            jax.ShapeDtypeStruct((8, 16), F32),
        ],
        in_specs=[hbm] * 5,
        out_specs=[hbm, hbm, vmem, vmem, vmem],
        scratch_shapes=[
            pltpu.VMEM((2, 2, W, CB), F32), pltpu.VMEM((2, 2, W, CA), F32),
            pltpu.VMEM((2, 2, W, CA), BF16), pltpu.VMEM((2, 2, W, CB), BF16), pltpu.VMEM((CA, CB), BF16),
            pltpu.VMEM((27 * CA, CA), BF16), pltpu.VMEM((27 * CB, CB), BF16),
            pltpu.VMEM((4, 4, W, CA), BF16), pltpu.VMEM((4, 4, W, CB), BF16),
            pltpu.VMEM((4, 4, W, CB), BF16), pltpu.VMEM((4, 4, W, CA), BF16),
            pltpu.VMEM((2, 2, W, CB), BF16), pltpu.VMEM((2, 2, W, CA), BF16),
            pltpu.VMEM((4, 4, W, 3 * CA), BF16), pltpu.VMEM((4, 4, W, 3 * CB), BF16),
            pltpu.VMEM((4, 4, W, 3 * CB), BF16), pltpu.VMEM((4, 4, W, 3 * CA), BF16),
            pltpu.VMEM((2, 8, 16, CELLS), BF16), pltpu.VMEM((2, 64, CELLS), BF16),
            pltpu.VMEM((9, 8, 16, 768), BF16), pltpu.VMEM((9, 8, 16, 768), BF16),
            pltpu.VMEM((9, 128, 768), F32),
            pltpu.VMEM((8, 2, 16, XB + YB), BF16), pltpu.VMEM((8, 2, 16, XB + YB), BF16),
            pltpu.VMEM((2, 8, 8, 27 * CB), F32),
            *group(XA, YA),
            *group(XB, YB),
            pltpu.VMEM((16, HALF_A), F32), pltpu.VMEM((16, XB + YB), F32),
            pltpu.VMEM((16, 16, 256), BF16), pltpu.VMEM((15, 16, 256), BF16), pltpu.VMEM((2, 16, 256), F32),
            pltpu.VMEM((16, 16, 128), BF16), pltpu.VMEM((15, 16, 128), BF16), pltpu.VMEM((2, 16, 128), F32),
            dma((5,)), dma((2, 5)), dma((2, 5)), dma((2, 5)), dma((2, 5)), dma((2, 9)), dma((2, 1)),
            *[dma((2, n)) for n in (12, 6, 3, 3, 12, 6, 3, 3, 15, 15)],
            dma((2,)),
        ],
        compiler_params=pltpu.CompilerParams(
            collective_id=0, has_side_effects=True, vmem_limit_bytes=56 * 1024 * 1024
        ),
    )(video, cotangent, kernel_a, project, kernel_b)
    results = pl.pallas_call(
        written,
        out_shape=[jax.ShapeDtypeStruct(r.shape, F32) for r in results],
        in_specs=[hbm] * 5,
        out_specs=[hbm] * 5,
        scratch_shapes=[*[pltpu.VMEM(r.shape, F32) for r in results], dma((2, 5))],
    )(*results)
    return results[0], results[1], results[2].T, results[3].T, results[4]


def solution(mesh):
    cells = P("tm", "rows", None, None)
    return jax.shard_map(
        shards,
        mesh=mesh,
        in_specs=(cells, P(), P(), P(), cells),
        out_specs=(cells, cells, P("tm", "rows"), P("tm", "rows"), P("tm", "rows")),
        check_vma=False,
    )
```
